32 devices in a mesh: dp: 8 (over y, x, core), tensor: 4 (over z).
Axes of the slice: x: 2, y: 2, z: 4, core: 2. Of those that a mesh axis runs over, the one named last changes fastest.
Arguments:
- hidden: bfloat16 [8, 1024, 4096], P('dp', None, 'tensor'), as said below
- gain: float32 [4096], replicated, may hold values from 0.5 to 1.5
- head: bfloat16 [4096, 16384], P(None, ('dp', 'tensor'))
- lengths: int32 [8], P('dp'), may hold values from 256 to 1024, as said below
- offsets: int32 [8, 32], P('dp'), may hold values from 0 to 255
- targets: int32 [8, 32], P('dp'), may hold values from 0 to 16383
- mask: int32 [8, 32], P('dp'), may hold values from 0 to 1, as said below
Outputs:
- logprob: float32 [8, 32], P('dp')
- entropy: float32 [8, 32], P('dp')
The draws below stay inside these ranges and needn't reach their ends.
Inputs may be any that keep to these rules, and one draw needn't show every extreme that they name: `lengths`: each length is at least 256; some sequence has length exactly 1024 in every draw. `mask`: among the 32 slots of the sequences of one index of dp, at most 16 are scored; some index of dp has exactly 16. `hidden`: entries are of order one or a few tens in magnitude.
All inputs are finite; a program needn't handle non-finite values.
Results may differ from the reference program's by a relative error of at most 0.0089.
Values may be sent and summed in bfloat16 or wider, within the bound.
No kernel may reach another device: no remote copies, remote signals or barrier semaphores. Data moves between devices by JAX's collectives and lax.ppermute only.
A program may use at most 64 MiB of HBM per device.

```python
import math
import jax
import jax.numpy as jnp
import numpy as np
from jax import lax

D = 4096
SEQ_DEV = 1
SLOTS = 32
MAXLEN = 1024
MINLEN = 256
VOCAB = 16384
SEQS = 8
LIVE_DEV = 16


def draw_hidden(key, part):
    first, second = jax.random.split(jax.random.fold_in(key, 11))
    scales = jnp.exp(jax.random.uniform(second, (SEQS, MAXLEN, 1), minval=math.log(0.3), maxval=math.log(3.0)))
    noise = jax.random.normal(first, (SEQS, MAXLEN, D))
    return (noise * scales).astype(jnp.bfloat16)


def draw_head(key, part):
    first, second = jax.random.split(jax.random.fold_in(key, 13), 2)
    colscale = jnp.exp(jax.random.uniform(second, (1, VOCAB), minval=0.0, maxval=math.log(10.0))) / math.sqrt(D)
    values = jax.random.normal(first, (D, VOCAB)) * colscale
    return values.astype(jnp.bfloat16)


def draw_lengths(key, part):
    first, second, third = jax.random.split(jax.random.fold_in(key, 21), 3)
    shifts = jax.random.randint(first, (SEQS,), 0, 6)
    spans = jnp.right_shift(jnp.full((SEQS,), MAXLEN - MINLEN, jnp.int32), shifts) + 1
    extra = jax.random.randint(second, (SEQS,), 0, spans)
    longest = jax.random.randint(third, (), 0, SEQS)
    return jnp.where(jnp.arange(SEQS) == longest, MAXLEN, MINLEN + extra).astype(jnp.int32)


def draw_mask(key, part):
    first, second, third = jax.random.split(jax.random.fold_in(key, 31), 3)
    blocks = SEQS // SEQ_DEV
    per_block = SEQ_DEV * SLOTS
    live = jnp.right_shift(jnp.full((blocks,), LIVE_DEV, jnp.int32), jax.random.randint(first, (blocks,), 0, 3))
    fullest = jax.random.randint(second, (), 0, blocks)
    live = jnp.where(jnp.arange(blocks) == fullest, LIVE_DEV, live)
    orders = jax.vmap(lambda k: jax.random.permutation(k, per_block))(jax.random.split(third, blocks))
    return (orders < live[:, None]).astype(jnp.int32).reshape(SEQS, SLOTS)


def touch_ends(entries, key, smallest, top_value):
    place = [jax.random.randint(jax.random.fold_in(key, axis), (), 0, length) for axis, length in enumerate(entries.shape)]
    widest = entries.shape.index(max(entries.shape))
    neighbour = place[:widest] + [(place[widest] + 1) % entries.shape[widest]] + place[widest + 1:]
    return entries.at[tuple(place)].set(smallest).at[tuple(neighbour)].set(top_value)


def rank_table(number_of, skew):
    weights = [(1 << 20) // math.isqrt(grade ** skew) + 1 for grade in range(1, number_of + 1)]
    deviation = 1 + sum(weights) // (1 << 30)
    return np.cumsum(np.array([max(1, weight // deviation) for weight in weights]))


def skewed_ids(own_key, shape, amount, skew):
    listing = rank_table(amount, skew)
    lot = jax.random.randint(jax.random.fold_in(own_key, 1), shape, 0, int(listing[amount - 1]))
    standing = jnp.searchsorted(jnp.asarray(listing, jnp.int32), lot, side="right")
    return jax.random.permutation(jax.random.fold_in(own_key, 2), amount)[standing].astype(jnp.int32)


def setup_inputs(seed: int = 0) -> dict:
    key_of = jax.random.split(jax.random.key(seed), 8)
    return {
        "hidden": draw_hidden(jax.random.fold_in(key_of[7], 71), 0),
        "gain": jnp.clip(1.0 + 0.1 * jax.random.normal(key_of[1], (D,), jnp.float32), 0.5, 1.5),
        "head": draw_head(jax.random.fold_in(key_of[7], 71), 0),
        "lengths": draw_lengths(jax.random.fold_in(key_of[7], 71), 0),
        "offsets": touch_ends(jax.random.randint(key_of[4], (SEQS, SLOTS), 0, MINLEN), jax.random.fold_in(key_of[4], 1), 0, MINLEN - 1).astype(jnp.int32),
        "targets": touch_ends(skewed_ids(key_of[5], (SEQS, SLOTS), VOCAB, 2), jax.random.fold_in(key_of[5], 3), 0, VOCAB - 1).astype(jnp.int32),
        "mask": draw_mask(jax.random.fold_in(key_of[7], 71), 0),
    }


def score_sequence(items, gain, head):
    states, length, offset, target, live = items
    position = (length - 1 - offset).astype(jnp.int32)
    rows = jnp.take(states, position, axis=0)
    values = rows.astype(jnp.float32)
    meansq = lax.optimization_barrier(jnp.mean(values * values, axis=-1, keepdims=True))
    normed = (values * lax.rsqrt(meansq + 1e-06) * gain).astype(jnp.bfloat16)
    logits = jnp.dot(normed, head, preferred_element_type=jnp.float32)
    top = lax.optimization_barrier(jnp.max(logits, axis=-1, keepdims=True))
    expo = jnp.exp(logits - top)
    total = lax.optimization_barrier(jnp.sum(expo, axis=-1))
    lse = top[:, 0] + jnp.log(total)
    picked = jnp.take_along_axis(logits, target[:, None].astype(jnp.int32), axis=1)[:, 0]
    weighted = lax.optimization_barrier(jnp.sum(expo * logits, axis=-1)) / total
    keep = live.astype(jnp.float32)
    return (keep * (picked - lse), keep * (lse - weighted))

def reference(hidden, gain, head, lengths, offsets, targets, mask):
    return lax.map(lambda items: score_sequence(items, gain, head), (hidden, lengths, offsets, targets, mask))
```

```python
import functools

import jax
import jax.numpy as jnp
from jax import lax
from jax.experimental import pallas as pl
from jax.experimental.pallas import tpu as pltpu
from jax.sharding import PartitionSpec as P

LIVE = 16
BLOCK = 16
CODE = 128
DIGIT = 64
STATS = 8


def pick_kernel(lengths, offsets, targets, mask, hidden, rows, place, slots, blocks, sems):
    slot_count = offsets.shape[1]
    features = hidden.shape[2]
    last = lengths[0] - 1

    def order(j, live):
        alive = mask[0, j] != 0
        slots[jnp.where(alive, live, slot_count - 1 - (j - live))] = j
        return live + alive.astype(jnp.int32)

    live = lax.fori_loop(0, slot_count, order, 0, unroll=True)

    def block_copy(k):
        position = last - offsets[0, slots[k]]
        start = pl.multiple_of((position // BLOCK) * BLOCK, BLOCK)
        return pltpu.make_async_copy(hidden.at[0, pl.ds(start, BLOCK)], blocks.at[k], sems.at[k])

    for k in range(LIVE):
        block_copy(k).start()

    row = lax.broadcasted_iota(jnp.int32, (LIVE, 1), 0)
    wanted = jnp.zeros((LIVE, 1), jnp.int32)
    target = jnp.zeros((LIVE, 1), jnp.int32)
    slot = jnp.full((LIVE, 1), -1, jnp.int32)
    for k in range(LIVE):
        j = slots[k]
        position = last - offsets[0, j]
        wanted = jnp.where(row == k, k * BLOCK + position % BLOCK, wanted)
        target = jnp.where(row == k, targets[0, j], target)
        slot = jnp.where(row == k, jnp.where(k < live, j, -1), slot)
    column = lax.broadcasted_iota(jnp.int32, (LIVE, LIVE * BLOCK), 1)
    select = jnp.where(column == wanted, 1.0, 0.0).astype(jnp.bfloat16)
    lane = lax.broadcasted_iota(jnp.int32, (LIVE, CODE), 1)
    digits = jnp.where(
        lane == 0,
        target % DIGIT,
        jnp.where(lane == 1, (target // DIGIT) % DIGIT, jnp.where(lane == 2, target // (DIGIT * DIGIT), 0)),
    )
    place[...] = jnp.where(lane == slot, 1.0, 0.0)
    rows[:, features:] = digits.astype(jnp.float32).astype(jnp.bfloat16)
    for k in range(LIVE):
        block_copy(k).wait()
    picked = jnp.dot(
        select, blocks[...].reshape(LIVE * BLOCK, features), preferred_element_type=jnp.float32
    )
    rows[:, :features] = picked.astype(jnp.bfloat16)


def pick(hidden, lengths, offsets, targets, mask):
    features = hidden.shape[2]
    smem = pl.BlockSpec(memory_space=pltpu.SMEM)
    vmem = pl.BlockSpec(memory_space=pltpu.VMEM)
    return pl.pallas_call(
        pick_kernel,
        out_shape=(
            jax.ShapeDtypeStruct((LIVE, features + CODE), jnp.bfloat16),
            jax.ShapeDtypeStruct((LIVE, CODE), jnp.float32),
        ),
        in_specs=[smem] * 4 + [pl.BlockSpec(memory_space=pltpu.HBM)],
        out_specs=(vmem, vmem),
        scratch_shapes=[
            pltpu.SMEM((offsets.shape[1],), jnp.int32),
            pltpu.VMEM((LIVE, BLOCK, features), jnp.bfloat16),
            pltpu.SemaphoreType.DMA((LIVE,)),
        ],
        name="pick",
    )(lengths, offsets, targets, mask, hidden)


def score_kernel(start, rows, gain, head, stats, held, sems):
    dp, tensor, live, width = rows.shape
    features = width - CODE
    vocab_width = head.shape[1]
    row_count = dp * live

    def head_copy(t):
        return pltpu.make_async_copy(head.at[pl.ds(t * features, features)], held.at[t], sems.at[t])

    for t in range(tensor):
        head_copy(t).start()

    def part(t):
        return rows[:, t, :, :features].reshape(row_count, features).astype(jnp.float32)

    square = jnp.zeros((row_count, 1), jnp.float32)
    for t in range(tensor):
        values = part(t)
        square += jnp.sum(values * values, axis=-1, keepdims=True)
    scale = lax.rsqrt(square / (tensor * features) + 1e-06)
    logits = jnp.zeros((row_count, vocab_width), jnp.float32)
    for t in range(tensor):
        normed = (part(t) * scale * gain[:, t * features : (t + 1) * features]).astype(jnp.bfloat16)
        head_copy(t).wait()
        logits += jnp.dot(normed, held[t], preferred_element_type=jnp.float32)

    digits = rows[:, 0, :, features:].reshape(row_count, CODE).astype(jnp.float32)
    lane = lax.broadcasted_iota(jnp.int32, (row_count, CODE), 1)
    weight = jnp.where(lane == 0, 1.0, jnp.where(lane == 1, float(DIGIT), jnp.where(lane == 2, float(DIGIT * DIGIT), 0.0)))
    target = jnp.sum(digits * weight, axis=-1, keepdims=True).astype(jnp.int32) - start[0]
    column = lax.broadcasted_iota(jnp.int32, (row_count, vocab_width), 1)
    top = jnp.max(logits, axis=-1, keepdims=True)
    expo = jnp.exp(logits - top)
    total = jnp.sum(expo, axis=-1, keepdims=True)
    weighted = jnp.sum(expo * logits, axis=-1, keepdims=True)
    chosen = jnp.sum(jnp.where(column == target, logits, 0.0), axis=-1, keepdims=True)
    table = jnp.where(
        lane == 0, top, jnp.where(lane == 1, total, jnp.where(lane == 2, weighted, jnp.where(lane == 3, chosen, 0.0)))
    )
    stats[...] = table.T[:STATS]


def score(rows, gain, head, start):
    dp, tensor, live, width = rows.shape
    features = width - CODE
    vmem = pl.BlockSpec(memory_space=pltpu.VMEM)
    return pl.pallas_call(
        score_kernel,
        out_shape=jax.ShapeDtypeStruct((STATS, dp * live), jnp.float32),
        in_specs=[pl.BlockSpec(memory_space=pltpu.SMEM), vmem, vmem, pl.BlockSpec(memory_space=pltpu.HBM)],
        out_specs=vmem,
        scratch_shapes=[
            pltpu.VMEM((tensor, features, head.shape[1]), head.dtype),
            pltpu.SemaphoreType.DMA((tensor,)),
        ],
        compiler_params=pltpu.CompilerParams(vmem_limit_bytes=32 * 1024 * 1024),
        name="score",
    )(start, rows, gain, head)


def finish_kernel(mine, stats, place, logprob, entropy):
    devices, _, row_count = stats.shape
    live = place.shape[0]
    slot_count = logprob.shape[1]
    top = jnp.max(stats[:, 0, :], axis=0, keepdims=True)
    factor = jnp.exp(stats[:, 0, :] - top)
    total = jnp.sum(stats[:, 1, :] * factor, axis=0, keepdims=True)
    weighted = jnp.sum(stats[:, 2, :] * factor, axis=0, keepdims=True)
    chosen = jnp.sum(stats[:, 3, :], axis=0, keepdims=True)
    lse = top + jnp.log(total)
    sublane = lax.broadcasted_iota(jnp.int32, (STATS, row_count), 0)
    values = jnp.where(sublane == 0, chosen - lse, jnp.where(sublane == 1, lse - weighted / total, 0.0))
    row = lax.broadcasted_iota(jnp.int32, (row_count, CODE), 0)
    spread = jnp.concatenate([place[...]] * (row_count // live), axis=0)
    spread = jnp.where(row // live == mine[0], spread, 0.0)
    out = jnp.dot(values, spread, precision=lax.Precision.HIGHEST, preferred_element_type=jnp.float32)
    logprob[...] = out[0:1, :slot_count]
    entropy[...] = out[1:2, :slot_count]


def finish(stats, place, mine, slot_count):
    vmem = pl.BlockSpec(memory_space=pltpu.VMEM)
    out = jax.ShapeDtypeStruct((1, slot_count), jnp.float32)
    return pl.pallas_call(
        finish_kernel,
        out_shape=(out, out),
        in_specs=[pl.BlockSpec(memory_space=pltpu.SMEM), vmem, vmem],
        out_specs=(vmem, vmem),
        name="finish",
    )(mine, stats, place)


def per_device(hidden, gain, head, lengths, offsets, targets, mask):
    dp, tensor = lax.axis_size("dp"), lax.axis_size("tensor")
    mine = lax.axis_index("dp")
    start = (mine * tensor + lax.axis_index("tensor")) * head.shape[1]
    rows, place = pick(hidden, lengths, offsets, targets, mask)
    rows = lax.all_gather(rows, ("dp", "tensor"))
    rows = rows.reshape(dp, tensor, *rows.shape[1:])
    stats = score(rows, gain.reshape(1, -1), head, start.reshape(1))
    stats = lax.all_gather(stats, ("dp", "tensor"))
    return finish(stats, place, mine.reshape(1), offsets.shape[1])


def solution(mesh):
    return jax.shard_map(
        per_device,
        mesh=mesh,
        in_specs=(
            P("dp", None, "tensor"),
            P(),
            P(None, ("dp", "tensor")),
            P("dp"),
            P("dp", None),
            P("dp", None),
            P("dp", None),
        ),
        out_specs=(P("dp", None), P("dp", None)),
        check_vma=False,
    )
```

```python
import functools

import jax
import jax.numpy as jnp
from jax import lax
from jax.experimental import pallas as pl
from jax.experimental.pallas import tpu as pltpu
from jax.sharding import PartitionSpec as P

LIVE = 16
BLOCK = 16
CODE = 128
DIGIT = 64
GROUP = 16


def pick_kernel(lengths, offsets, targets, mask, hidden, rows, place, slots, blocks, sems):
    slot_count = offsets.shape[1]
    features = hidden.shape[2]
    last = lengths[0] - 1

    def order(j, live):
        alive = mask[0, j] != 0
        slots[jnp.where(alive, live, slot_count - 1 - (j - live))] = j
        return live + alive.astype(jnp.int32)

    live = lax.fori_loop(0, slot_count, order, 0, unroll=True)

    def block_copy(k):
        position = last - offsets[0, slots[k]]
        start = pl.multiple_of((position // BLOCK) * BLOCK, BLOCK)
        return pltpu.make_async_copy(hidden.at[0, pl.ds(start, BLOCK)], blocks.at[k], sems.at[k])

    for k in range(LIVE):
        block_copy(k).start()

    row = lax.broadcasted_iota(jnp.int32, (LIVE, 1), 0)
    wanted = jnp.zeros((LIVE, 1), jnp.int32)
    target = jnp.zeros((LIVE, 1), jnp.int32)
    slot = jnp.full((LIVE, 1), -1, jnp.int32)
    for k in range(LIVE):
        j = slots[k]
        position = last - offsets[0, j]
        wanted = jnp.where(row == k, k * BLOCK + position % BLOCK, wanted)
        target = jnp.where(row == k, targets[0, j], target)
        slot = jnp.where(row == k, jnp.where(k < live, j, -1), slot)
    column = lax.broadcasted_iota(jnp.int32, (LIVE, LIVE * BLOCK), 1)
    select = jnp.where(column == wanted, 1.0, 0.0).astype(jnp.bfloat16)
    lane = lax.broadcasted_iota(jnp.int32, (LIVE, CODE), 1)
    digits = jnp.where(
        lane == 0,
        target % DIGIT,
        jnp.where(lane == 1, (target // DIGIT) % DIGIT, jnp.where(lane == 2, target // (DIGIT * DIGIT), 0)),
    )
    place[...] = jnp.where(lane == slot, 1.0, 0.0)
    rows[:, features:] = digits.astype(jnp.float32).astype(jnp.bfloat16)
    for k in range(LIVE):
        block_copy(k).wait()
    picked = jnp.dot(
        select, blocks[...].reshape(LIVE * BLOCK, features), preferred_element_type=jnp.float32
    )
    rows[:, :features] = picked.astype(jnp.bfloat16)


def pick(hidden, lengths, offsets, targets, mask):
    features = hidden.shape[2]
    smem = pl.BlockSpec(memory_space=pltpu.SMEM)
    vmem = pl.BlockSpec(memory_space=pltpu.VMEM)
    return pl.pallas_call(
        pick_kernel,
        out_shape=(
            jax.ShapeDtypeStruct((LIVE, features + CODE), jnp.bfloat16),
            jax.ShapeDtypeStruct((LIVE, CODE), jnp.float32),
        ),
        in_specs=[smem] * 4 + [pl.BlockSpec(memory_space=pltpu.HBM)],
        out_specs=(vmem, vmem),
        scratch_shapes=[
            pltpu.SMEM((offsets.shape[1],), jnp.int32),
            pltpu.VMEM((LIVE, BLOCK, features), jnp.bfloat16),
            pltpu.SemaphoreType.DMA((LIVE,)),
        ],
        name="pick",
    )(lengths, offsets, targets, mask, hidden)


def score_kernel(place, *refs):
    dp = len(refs) - 5
    pieces, (gain, head, stats, held, sems) = refs[:dp], refs[dp:]
    tensor, live, width = pieces[0].shape
    features = width - CODE
    vocab_width = head.shape[1]
    row_count = dp * live
    mine, shard = place[0], place[1]

    def head_copy(s):
        first = pl.multiple_of((shard ^ s) * features, features)
        return pltpu.make_async_copy(head.at[pl.ds(first, features)], held.at[s], sems.at[s])

    for s in range(tensor):
        head_copy(s).start()

    def part(s):
        return jnp.concatenate([piece[s, :, :features] for piece in pieces], axis=0).astype(jnp.float32)

    square = jnp.zeros((row_count, 1), jnp.float32)
    for s in range(tensor):
        values = part(s)
        square += jnp.sum(values * values, axis=-1, keepdims=True)
    scale = lax.rsqrt(square / (tensor * features) + 1e-06)
    logits = jnp.zeros((row_count, vocab_width), jnp.float32)
    for s in range(tensor):
        normed = (part(s) * scale * gain[shard ^ s]).astype(jnp.bfloat16)
        head_copy(s).wait()
        logits += jnp.dot(normed, held[s], preferred_element_type=jnp.float32)

    digits = jnp.concatenate([piece[0, :, features:] for piece in pieces], axis=0).astype(jnp.float32)
    lane = lax.broadcasted_iota(jnp.int32, (row_count, CODE), 1)
    weight = jnp.where(lane == 0, 1.0, jnp.where(lane == 1, float(DIGIT), jnp.where(lane == 2, float(DIGIT * DIGIT), 0.0)))
    start = (mine * tensor + shard) * vocab_width
    target = jnp.sum(digits * weight, axis=-1, keepdims=True).astype(jnp.int32) - start
    column = lax.broadcasted_iota(jnp.int32, (row_count, vocab_width), 1)
    top = jnp.max(logits, axis=-1, keepdims=True)
    expo = jnp.exp(logits - top)
    total = jnp.sum(expo, axis=-1, keepdims=True)
    weighted = jnp.sum(expo * logits, axis=-1, keepdims=True)
    chosen = jnp.sum(jnp.where(column == target, logits, 0.0), axis=-1, keepdims=True)
    spot = lane - lax.broadcasted_iota(jnp.int32, (row_count, CODE), 0) % live
    table = jnp.zeros((row_count, CODE), jnp.float32)
    for group, value in enumerate((top, total, weighted, chosen)):
        table = jnp.where(spot == GROUP * group, value, table)
    for d in range(dp):
        line = jnp.sum(table[d * live : (d + 1) * live], axis=0, keepdims=True)
        for t in range(tensor):
            stats[mine ^ d, t] = line


def score(pieces, gain, head, place):
    dp = len(pieces)
    tensor, live, width = pieces[0].shape
    features = width - CODE
    vmem = pl.BlockSpec(memory_space=pltpu.VMEM)
    return pl.pallas_call(
        score_kernel,
        out_shape=jax.ShapeDtypeStruct((dp, tensor, 1, CODE), jnp.float32),
        in_specs=[pl.BlockSpec(memory_space=pltpu.SMEM)] + [vmem] * (dp + 1) + [pl.BlockSpec(memory_space=pltpu.HBM)],
        out_specs=vmem,
        scratch_shapes=[
            pltpu.VMEM((tensor, features, head.shape[1]), head.dtype),
            pltpu.SemaphoreType.DMA((tensor,)),
        ],
        compiler_params=pltpu.CompilerParams(vmem_limit_bytes=32 * 1024 * 1024),
        name="score",
    )(place, *pieces, gain.reshape(tensor, 1, features), head)


def finish_kernel(stats, place, logprob, entropy):
    live = place.shape[0]
    slot_count = logprob.shape[1]
    values = stats[:, 0, :]
    lane = lax.broadcasted_iota(jnp.int32, values.shape, 1)
    top = jnp.where(lane < GROUP, values, 0.0)
    top = top + pltpu.roll(top, GROUP, 1)
    top = top + pltpu.roll(top, 2 * GROUP, 1)
    best = jnp.max(top, axis=0, keepdims=True)
    factor = jnp.where(lane < 3 * GROUP, jnp.exp(top - best), 1.0)
    sums = jnp.sum(values * factor, axis=0, keepdims=True)
    line = jnp.broadcast_to(sums, (8, CODE))
    total = pltpu.roll(line, CODE - GROUP, 1)
    weighted = pltpu.roll(line, CODE - 2 * GROUP, 1)
    chosen = pltpu.roll(line, CODE - 3 * GROUP, 1)
    lse = best + jnp.log(total)
    kind = lax.broadcasted_iota(jnp.int32, (8, CODE), 0)
    merged = jnp.where(kind == 0, chosen - lse, lse - weighted / total)
    merged = jnp.where(lax.broadcasted_iota(jnp.int32, (8, CODE), 1) < GROUP, merged, 0.0)
    spread = jnp.concatenate([place[...], jnp.zeros((CODE - live, CODE), jnp.float32)], axis=0)
    out = jnp.dot(merged, spread, precision=lax.Precision.HIGHEST, preferred_element_type=jnp.float32)
    logprob[...] = out[0:1, :slot_count]
    entropy[...] = out[1:2, :slot_count]


def finish(stats, place, slot_count):
    vmem = pl.BlockSpec(memory_space=pltpu.VMEM)
    out = jax.ShapeDtypeStruct((1, slot_count), jnp.float32)
    return pl.pallas_call(
        finish_kernel,
        out_shape=(out, out),
        in_specs=[vmem, vmem],
        out_specs=(vmem, vmem),
        name="finish",
    )(stats, place)


def swap(x, axis, distance):
    return lax.ppermute(x, axis, [(i, i ^ distance) for i in range(lax.axis_size(axis))])


def spread(x, axis):
    return [x] + [swap(x, axis, d) for d in range(1, lax.axis_size(axis))]


def per_device(hidden, gain, head, lengths, offsets, targets, mask):
    dp, tensor = lax.axis_size("dp"), lax.axis_size("tensor")
    place = jnp.stack([lax.axis_index("dp"), lax.axis_index("tensor")])
    rows, slots = pick(hidden, lengths, offsets, targets, mask)
    rows = jnp.stack(spread(rows, "tensor"))
    stats = score(spread(rows, "dp"), gain, head, place)
    stats = lax.all_to_all(stats.reshape(dp * tensor, 1, CODE), ("dp", "tensor"), 0, 0, tiled=True)
    return finish(stats, slots, offsets.shape[1])


def solution(mesh):
    return jax.shard_map(
        per_device,
        mesh=mesh,
        in_specs=(
            P("dp", None, "tensor"),
            P(),
            P(None, ("dp", "tensor")),
            P("dp"),
            P("dp", None),
            P("dp", None),
            P("dp", None),
        ),
        out_specs=(P("dp", None), P("dp", None)),
        check_vma=False,
    )
```

```python
import functools

import jax
import jax.numpy as jnp
from jax import lax
from jax.experimental import pallas as pl
from jax.experimental.pallas import tpu as pltpu
from jax.sharding import PartitionSpec as P

LIVE = 16
BLOCK = 16
CODE = 128
DIGIT = 64
GROUP = 16


def pick_kernel(lengths, offsets, targets, mask, hidden, rows, codes, place, slots, blocks, sems):
    slot_count = offsets.shape[1]
    features = hidden.shape[2]
    last = lengths[0] - 1

    def order(j, live):
        alive = mask[0, j] != 0
        slots[jnp.where(alive, live, slot_count - 1 - (j - live))] = j
        return live + alive.astype(jnp.int32)

    live = lax.fori_loop(0, slot_count, order, 0, unroll=True)

    def block_copy(k):
        position = last - offsets[0, slots[k]]
        start = pl.multiple_of((position // BLOCK) * BLOCK, BLOCK)
        return pltpu.make_async_copy(hidden.at[0, pl.ds(start, BLOCK)], blocks.at[k], sems.at[k])

    for k in range(LIVE):
        block_copy(k).start()

    row = lax.broadcasted_iota(jnp.int32, (LIVE, 1), 0)
    wanted = jnp.zeros((LIVE, 1), jnp.int32)
    target = jnp.zeros((LIVE, 1), jnp.int32)
    slot = jnp.full((LIVE, 1), -1, jnp.int32)
    for k in range(LIVE):
        j = slots[k]
        position = last - offsets[0, j]
        wanted = jnp.where(row == k, k * BLOCK + position % BLOCK, wanted)
        target = jnp.where(row == k, targets[0, j], target)
        slot = jnp.where(row == k, jnp.where(k < live, j, -1), slot)
    column = lax.broadcasted_iota(jnp.int32, (LIVE, LIVE * BLOCK), 1)
    select = jnp.where(column == wanted, 1.0, 0.0).astype(jnp.bfloat16)
    lane = lax.broadcasted_iota(jnp.int32, (LIVE, CODE), 1)
    digits = jnp.where(
        lane == 0,
        target % DIGIT,
        jnp.where(lane == 1, (target // DIGIT) % DIGIT, jnp.where(lane == 2, target // (DIGIT * DIGIT), 0)),
    )
    place[...] = jnp.where(lane == slot, 1.0, 0.0)
    codes[...] = digits.astype(jnp.float32).astype(jnp.bfloat16)
    for k in range(LIVE):
        block_copy(k).wait()
    picked = jnp.dot(
        select, blocks[...].reshape(LIVE * BLOCK, features), preferred_element_type=jnp.float32
    )
    for t in range(rows.shape[0]):
        rows[t] = picked.astype(jnp.bfloat16)


def pick(hidden, lengths, offsets, targets, mask, copies):
    features = hidden.shape[2]
    smem = pl.BlockSpec(memory_space=pltpu.SMEM)
    vmem = pl.BlockSpec(memory_space=pltpu.VMEM)
    return pl.pallas_call(
        pick_kernel,
        out_shape=(
            jax.ShapeDtypeStruct((copies, LIVE, features), jnp.bfloat16),
            jax.ShapeDtypeStruct((LIVE, CODE), jnp.bfloat16),
            jax.ShapeDtypeStruct((LIVE, CODE), jnp.float32),
        ),
        in_specs=[smem] * 4 + [pl.BlockSpec(memory_space=pltpu.HBM)],
        out_specs=(vmem, vmem, vmem),
        scratch_shapes=[
            pltpu.SMEM((offsets.shape[1],), jnp.int32),
            pltpu.VMEM((LIVE, BLOCK, features), jnp.bfloat16),
            pltpu.SemaphoreType.DMA((LIVE,)),
        ],
        name="pick",
    )(lengths, offsets, targets, mask, hidden)


def join_kernel(parts, codes, gain, rows):
    tensor, live, features = parts.shape
    square = jnp.zeros((live, 1), jnp.float32)
    for t in range(tensor):
        values = parts[t].astype(jnp.float32)
        square += jnp.sum(values * values, axis=-1, keepdims=True)
    scale = lax.rsqrt(square / (tensor * features) + 1e-06)
    for t in range(tensor):
        span = slice(t * features, (t + 1) * features)
        rows[:, span] = (parts[t].astype(jnp.float32) * scale * gain[:, span]).astype(jnp.bfloat16)
    rows[:, tensor * features :] = codes[...]


def join(parts, codes, gain):
    tensor, live, features = parts.shape
    vmem = pl.BlockSpec(memory_space=pltpu.VMEM)
    return pl.pallas_call(
        join_kernel,
        out_shape=jax.ShapeDtypeStruct((live, tensor * features + CODE), jnp.bfloat16),
        in_specs=[vmem] * 3,
        out_specs=vmem,
        name="join",
    )(parts, codes, gain.reshape(1, -1))


def fetch_kernel(head, after, held, sems):
    del after
    count = sems.shape[0]
    depth = head.shape[0] // count
    copies = [
        pltpu.make_async_copy(head.at[pl.ds(i * depth, depth)], held.at[pl.ds(i * depth, depth)], sems.at[i])
        for i in range(count)
    ]
    for copy in copies:
        copy.start()
    for copy in copies:
        copy.wait()


def fetch(head, after):
    return pl.pallas_call(
        fetch_kernel,
        out_shape=jax.ShapeDtypeStruct(head.shape, head.dtype),
        in_specs=[pl.BlockSpec(memory_space=pltpu.HBM), pl.BlockSpec(memory_space=pl.ANY)],
        out_specs=pl.BlockSpec(memory_space=pltpu.VMEM),
        scratch_shapes=[pltpu.SemaphoreType.DMA((4,))],
        compiler_params=pltpu.CompilerParams(vmem_limit_bytes=56 * 1024 * 1024),
        cost_estimate=pl.CostEstimate(flops=0, bytes_accessed=2 * head.size * 2, transcendentals=0),
        name="fetch",
    )(head, after)


def score_kernel(place, *refs):
    dp = len(refs) - 2
    pieces, (head, stats) = refs[:dp], refs[dp:]
    depth, vocab_width = head.shape
    live = pieces[0].shape[0]
    row_count = dp * live
    mine, start = place[0], place[1]

    normed = jnp.concatenate([piece[:, :depth] for piece in pieces], axis=0)
    logits = jnp.dot(normed, head[...], preferred_element_type=jnp.float32)
    digits = jnp.concatenate([piece[:, depth:] for piece in pieces], axis=0).astype(jnp.float32)
    lane = lax.broadcasted_iota(jnp.int32, (row_count, CODE), 1)
    weight = jnp.where(lane == 0, 1.0, jnp.where(lane == 1, float(DIGIT), jnp.where(lane == 2, float(DIGIT * DIGIT), 0.0)))
    target = jnp.sum(digits * weight, axis=-1, keepdims=True).astype(jnp.int32) - start
    column = lax.broadcasted_iota(jnp.int32, (row_count, vocab_width), 1)
    top = jnp.max(logits, axis=-1, keepdims=True)
    expo = jnp.exp(logits - top)
    total = jnp.sum(expo, axis=-1, keepdims=True)
    weighted = jnp.sum(expo * logits, axis=-1, keepdims=True)
    chosen = jnp.sum(jnp.where(column == target, logits, 0.0), axis=-1, keepdims=True)
    spot = lane - lax.broadcasted_iota(jnp.int32, (row_count, CODE), 0) % live
    table = jnp.zeros((row_count, CODE), jnp.float32)
    for group, value in enumerate((top, total, weighted, chosen)):
        table = jnp.where(spot == GROUP * group, value, table)
    for d in range(dp):
        stats[mine ^ d] = jnp.sum(table[d * live : (d + 1) * live], axis=0, keepdims=True)


def score(pieces, head, place):
    dp = len(pieces)
    live, width = pieces[0].shape
    vmem = pl.BlockSpec(memory_space=pltpu.VMEM)
    return pl.pallas_call(
        score_kernel,
        out_shape=jax.ShapeDtypeStruct((dp, 1, CODE), jnp.float32),
        in_specs=[pl.BlockSpec(memory_space=pltpu.SMEM)] + [vmem] * (dp + 1),
        out_specs=vmem,
        compiler_params=pltpu.CompilerParams(vmem_limit_bytes=32 * 1024 * 1024),
        name="score",
    )(place, *pieces, head)


def combine(values):
    lane = lax.broadcasted_iota(jnp.int32, values.shape, 1)
    top = jnp.where(lane < GROUP, values, 0.0)
    top = top + pltpu.roll(top, GROUP, 1)
    top = top + pltpu.roll(top, 2 * GROUP, 1)
    best = jnp.max(top, axis=0, keepdims=True)
    factor = jnp.where(lane < 3 * GROUP, jnp.exp(top - best), 1.0)
    return jnp.sum(values * factor, axis=0, keepdims=True), best


def merge_kernel(stats, line):
    sums, best = combine(stats[:, 0, :])
    lane = lax.broadcasted_iota(jnp.int32, sums.shape, 1)
    merged = jnp.where(lane < GROUP, best, sums)
    for t in range(line.shape[0]):
        line[t] = merged


def merge(stats, copies):
    vmem = pl.BlockSpec(memory_space=pltpu.VMEM)
    return pl.pallas_call(
        merge_kernel,
        out_shape=jax.ShapeDtypeStruct((copies, 1, CODE), jnp.float32),
        in_specs=[vmem],
        out_specs=vmem,
        name="merge",
    )(stats)


def finish_kernel(stats, place, logprob, entropy):
    live = place.shape[0]
    slot_count = logprob.shape[1]
    sums, best = combine(stats[:, 0, :])
    line = jnp.broadcast_to(sums, (8, CODE))
    total = pltpu.roll(line, CODE - GROUP, 1)
    weighted = pltpu.roll(line, CODE - 2 * GROUP, 1)
    chosen = pltpu.roll(line, CODE - 3 * GROUP, 1)
    lse = best + jnp.log(total)
    kind = lax.broadcasted_iota(jnp.int32, (8, CODE), 0)
    merged = jnp.where(kind == 0, chosen - lse, lse - weighted / total)
    merged = jnp.where(lax.broadcasted_iota(jnp.int32, (8, CODE), 1) < GROUP, merged, 0.0)
    spread = jnp.concatenate([place[...], jnp.zeros((CODE - live, CODE), jnp.float32)], axis=0)
    out = jnp.dot(merged, spread, precision=lax.Precision.HIGHEST, preferred_element_type=jnp.float32)
    logprob[...] = out[0:1, :slot_count]
    entropy[...] = out[1:2, :slot_count]


def finish(stats, place, slot_count):
    vmem = pl.BlockSpec(memory_space=pltpu.VMEM)
    out = jax.ShapeDtypeStruct((1, slot_count), jnp.float32)
    return pl.pallas_call(
        finish_kernel,
        out_shape=(out, out),
        in_specs=[vmem, vmem],
        out_specs=(vmem, vmem),
        name="finish",
    )(stats, place)


def swap(x, axis, distance):
    return lax.ppermute(x, axis, [(i, i ^ distance) for i in range(lax.axis_size(axis))])


def gather_dp(rows):
    pieces = []
    arrived = [rows] + [swap(rows, "dp", d) for d in range(2, lax.axis_size("dp"), 2)]
    for piece in arrived:
        pieces += [piece, swap(piece, "dp", 1)]
    return pieces


def per_device(hidden, gain, head, lengths, offsets, targets, mask):
    dp, tensor = lax.axis_size("dp"), lax.axis_size("tensor")
    mine, shard = lax.axis_index("dp"), lax.axis_index("tensor")
    place = jnp.stack([mine, (mine * tensor + shard) * head.shape[1]])
    parts, codes, slots = pick(hidden, lengths, offsets, targets, mask, tensor)
    parts = lax.all_to_all(parts, "tensor", 0, 0, tiled=True)
    rows = join(parts, codes, gain)
    held = fetch(head, rows)
    stats = score(gather_dp(rows), held, place)
    stats = lax.all_to_all(stats, "dp", 0, 0, tiled=True)
    stats = lax.all_to_all(merge(stats, tensor), "tensor", 0, 0, tiled=True)
    return finish(stats, slots, offsets.shape[1])


def solution(mesh):
    return jax.shard_map(
        per_device,
        mesh=mesh,
        in_specs=(
            P("dp", None, "tensor"),
            P(),
            P(None, ("dp", "tensor")),
            P("dp"),
            P("dp", None),
            P("dp", None),
            P("dp", None),
        ),
        out_specs=(P("dp", None), P("dp", None)),
        check_vma=False,
    )
```

```python
import functools

import jax
import jax.numpy as jnp
from jax import lax
from jax.experimental import pallas as pl
from jax.experimental.pallas import tpu as pltpu
from jax.sharding import PartitionSpec as P

LIVE = 16
BLOCK = 16
CODE = 128
DIGIT = 64
GROUP = 16


def vmem_limit(mebibytes):
    return pltpu.CompilerParams(vmem_limit_bytes=mebibytes * 1024 * 1024)


def pick_kernel(lengths, offsets, targets, mask, hidden, rows, codes, place, slots, blocks, sems):
    slot_count = offsets.shape[1]
    features = hidden.shape[2]
    last = lengths[0, 0] - 1

    def order(j, live):
        alive = mask[0, j] != 0
        slots[jnp.where(alive, live, slot_count - 1 - (j - live))] = j
        return live + alive.astype(jnp.int32)

    live = lax.fori_loop(0, slot_count, order, 0, unroll=True)

    def block_copy(k):
        position = last - offsets[0, slots[k]]
        start = pl.multiple_of((position // BLOCK) * BLOCK, BLOCK)
        return pltpu.make_async_copy(hidden.at[0, pl.ds(start, BLOCK)], blocks.at[k], sems.at[k])

    for k in range(LIVE):
        block_copy(k).start()

    row = lax.broadcasted_iota(jnp.int32, (LIVE, 1), 0)
    wanted = jnp.zeros((LIVE, 1), jnp.int32)
    target = jnp.zeros((LIVE, 1), jnp.int32)
    slot = jnp.full((LIVE, 1), -1, jnp.int32)
    for k in range(LIVE):
        j = slots[k]
        position = last - offsets[0, j]
        wanted = jnp.where(row == k, k * BLOCK + position % BLOCK, wanted)
        target = jnp.where(row == k, targets[0, j], target)
        slot = jnp.where(row == k, jnp.where(k < live, j, -1), slot)
    column = lax.broadcasted_iota(jnp.int32, (LIVE, LIVE * BLOCK), 1)
    select = jnp.where(column == wanted, 1.0, 0.0).astype(jnp.bfloat16)
    lane = lax.broadcasted_iota(jnp.int32, (LIVE, CODE), 1)
    digits = jnp.where(
        lane == 0,
        target % DIGIT,
        jnp.where(lane == 1, (target // DIGIT) % DIGIT, jnp.where(lane == 2, target // (DIGIT * DIGIT), 0)),
    )
    place[...] = jnp.where(lane == slot, 1.0, 0.0)
    codes[...] = digits.astype(jnp.float32).astype(jnp.bfloat16)
    for k in range(LIVE):
        block_copy(k).wait()
    picked = jnp.dot(
        select, blocks[...].reshape(LIVE * BLOCK, features), preferred_element_type=jnp.float32
    )
    rows[...] = picked.astype(jnp.bfloat16)


def pick(hidden, lengths, offsets, targets, mask):
    features = hidden.shape[2]
    smem = pl.BlockSpec(memory_space=pltpu.SMEM)
    vmem = pl.BlockSpec(memory_space=pltpu.VMEM)
    return pl.pallas_call(
        pick_kernel,
        out_shape=(
            jax.ShapeDtypeStruct((LIVE, features), jnp.bfloat16),
            jax.ShapeDtypeStruct((LIVE, CODE), jnp.bfloat16),
            jax.ShapeDtypeStruct((LIVE, CODE), jnp.float32),
        ),
        in_specs=[smem] * 4 + [pl.BlockSpec(memory_space=pltpu.HBM)],
        out_specs=(vmem, vmem, vmem),
        scratch_shapes=[
            pltpu.SMEM((offsets.shape[1],), jnp.int32),
            pltpu.VMEM((LIVE, BLOCK, features), jnp.bfloat16),
            pltpu.SemaphoreType.DMA((LIVE,)),
        ],
        compiler_params=vmem_limit(52),
        name="pick",
    )(lengths.reshape(1, 1), offsets, targets, mask, hidden)


def join_kernel(shard, *refs):
    tensor = len(refs) - 3
    parts, (codes, gain, rows) = refs[:tensor], refs[tensor:]
    live, features = parts[0].shape
    square = jnp.zeros((live, 1), jnp.float32)
    for part in parts:
        values = part[...].astype(jnp.float32)
        square += jnp.sum(values * values, axis=-1, keepdims=True)
    scale = lax.rsqrt(square / (tensor * features) + 1e-06)
    for s, part in enumerate(parts):
        span = pl.ds(pl.multiple_of((shard[0] ^ s) * features, features), features)
        rows[:, span] = (part[...].astype(jnp.float32) * scale * gain[:, span]).astype(jnp.bfloat16)
    rows[:, tensor * features :] = codes[...]


def join(parts, codes, gain, shard):
    tensor = len(parts)
    live, features = parts[0].shape
    vmem = pl.BlockSpec(memory_space=pltpu.VMEM)
    return pl.pallas_call(
        join_kernel,
        out_shape=jax.ShapeDtypeStruct((live, tensor * features + CODE), jnp.bfloat16),
        in_specs=[pl.BlockSpec(memory_space=pltpu.SMEM)] + [vmem] * (tensor + 2),
        out_specs=vmem,
        compiler_params=vmem_limit(32),
        name="join",
    )(shard, *parts, codes, gain.reshape(1, -1))


def fetch_kernel(head, after, held, sems):
    del after
    count = sems.shape[0]
    depth = head.shape[0] // count
    copies = [
        pltpu.make_async_copy(head.at[pl.ds(i * depth, depth)], held.at[pl.ds(i * depth, depth)], sems.at[i])
        for i in range(count)
    ]
    for copy in copies:
        copy.start()
    for copy in copies:
        copy.wait()


def fetch(head, after):
    return pl.pallas_call(
        fetch_kernel,
        out_shape=jax.ShapeDtypeStruct(head.shape, head.dtype),
        in_specs=[pl.BlockSpec(memory_space=pltpu.HBM), pl.BlockSpec(memory_space=pl.ANY)],
        out_specs=pl.BlockSpec(memory_space=pltpu.VMEM),
        scratch_shapes=[pltpu.SemaphoreType.DMA((4,))],
        compiler_params=vmem_limit(47),
        cost_estimate=pl.CostEstimate(flops=0, bytes_accessed=2 * head.size * 2, transcendentals=0),
        name="fetch",
    )(head, after)


def score_kernel(index, start, *refs):
    dp = len(refs) - 2
    pieces, (head, stats) = refs[:dp], refs[dp:]
    depth, vocab_width = head.shape
    live = pieces[0].shape[0]
    row_count = dp * live
    mine = index[0]

    normed = jnp.concatenate([piece[:, :depth] for piece in pieces], axis=0)
    logits = jnp.dot(normed, head[...], preferred_element_type=jnp.float32)
    digits = jnp.concatenate([piece[:, depth:] for piece in pieces], axis=0).astype(jnp.float32)
    lane = lax.broadcasted_iota(jnp.int32, (row_count, CODE), 1)
    weight = jnp.where(lane == 0, 1.0, jnp.where(lane == 1, float(DIGIT), jnp.where(lane == 2, float(DIGIT * DIGIT), 0.0)))
    target = jnp.sum(digits * weight, axis=-1, keepdims=True).astype(jnp.int32) - start[0]
    column = lax.broadcasted_iota(jnp.int32, (row_count, vocab_width), 1)
    top = jnp.max(logits, axis=-1, keepdims=True)
    expo = jnp.exp(logits - top)
    total = jnp.sum(expo, axis=-1, keepdims=True)
    weighted = jnp.sum(expo * logits, axis=-1, keepdims=True)
    chosen = jnp.sum(jnp.where(column == target, logits, 0.0), axis=-1, keepdims=True)
    spot = lane - lax.broadcasted_iota(jnp.int32, (row_count, CODE), 0) % live
    table = jnp.zeros((row_count, CODE), jnp.float32)
    for group, value in enumerate((top, total, weighted, chosen)):
        table = jnp.where(spot == GROUP * group, value, table)
    for d in range(dp):
        line = jnp.sum(table[d * live : (d + 1) * live], axis=0, keepdims=True)
        for t in range(stats.shape[1]):
            stats[mine ^ d, t] = line


def score(pieces, head, index, start, copies):
    dp = len(pieces)
    live, width = pieces[0].shape
    vmem = pl.BlockSpec(memory_space=pltpu.VMEM)
    return pl.pallas_call(
        score_kernel,
        out_shape=jax.ShapeDtypeStruct((dp, copies, 1, CODE), jnp.float32),
        in_specs=[pl.BlockSpec(memory_space=pltpu.SMEM)] * 2 + [vmem] * (dp + 1),
        out_specs=vmem,
        compiler_params=vmem_limit(32),
        name="score",
    )(index, start, *pieces, head)


def combine(values):
    lane = lax.broadcasted_iota(jnp.int32, values.shape, 1)
    top = jnp.where(lane < GROUP, values, 0.0)
    top = top + pltpu.roll(top, GROUP, 1)
    top = top + pltpu.roll(top, 2 * GROUP, 1)
    best = jnp.max(top, axis=0, keepdims=True)
    factor = jnp.where(lane < 3 * GROUP, jnp.exp(top - best), 1.0)
    return jnp.sum(values * factor, axis=0, keepdims=True), best


def finish_kernel(stats, place, logprob, entropy):
    live = place.shape[0]
    slot_count = logprob.shape[1]
    sums, best = combine(stats[:, 0, :])
    line = jnp.broadcast_to(sums, (8, CODE))
    total = pltpu.roll(line, CODE - GROUP, 1)
    weighted = pltpu.roll(line, CODE - 2 * GROUP, 1)
    chosen = pltpu.roll(line, CODE - 3 * GROUP, 1)
    lse = best + jnp.log(total)
    kind = lax.broadcasted_iota(jnp.int32, (8, CODE), 0)
    merged = jnp.where(kind == 0, chosen - lse, lse - weighted / total)
    merged = jnp.where(lax.broadcasted_iota(jnp.int32, (8, CODE), 1) < GROUP, merged, 0.0)
    spread = jnp.concatenate([place[...], jnp.zeros((CODE - live, CODE), jnp.float32)], axis=0)
    out = jnp.dot(merged, spread, precision=lax.Precision.HIGHEST, preferred_element_type=jnp.float32)
    logprob[...] = out[0:1, :slot_count]
    entropy[...] = out[1:2, :slot_count]


def finish(stats, place, slot_count):
    vmem = pl.BlockSpec(memory_space=pltpu.VMEM)
    out = jax.ShapeDtypeStruct((1, slot_count), jnp.float32)
    return pl.pallas_call(
        finish_kernel,
        out_shape=(out, out),
        in_specs=[vmem, vmem],
        out_specs=(vmem, vmem),
        compiler_params=vmem_limit(32),
        name="finish",
    )(stats, place)


def swap(x, axis, distance):
    return lax.ppermute(x, axis, [(i, i ^ distance) for i in range(lax.axis_size(axis))])


def gather_dp(rows):
    pieces = []
    arrived = [rows] + [swap(rows, "dp", d) for d in range(2, lax.axis_size("dp"), 2)]
    for piece in arrived:
        pieces += [piece, swap(piece, "dp", 1)]
    return pieces


def per_device(hidden, gain, head, lengths, offsets, targets, mask):
    dp, tensor = lax.axis_size("dp"), lax.axis_size("tensor")
    mine, shard = lax.axis_index("dp"), lax.axis_index("tensor")
    start = (mine * tensor + shard) * head.shape[1]
    rows, codes, slots = pick(hidden, lengths, offsets, targets, mask)
    parts = [rows] + [swap(rows, "tensor", s) for s in range(1, tensor)]
    rows = join(parts, codes, gain, shard.reshape(1))
    held = fetch(head, rows)
    stats = score(gather_dp(rows), held, mine.reshape(1), start.reshape(1), tensor)
    stats = lax.all_to_all(stats.reshape(dp * tensor, 1, CODE), ("dp", "tensor"), 0, 0, tiled=True)
    return finish(stats, slots, offsets.shape[1])


def solution(mesh):
    return jax.shard_map(
        per_device,
        mesh=mesh,
        in_specs=(
            P("dp", None, "tensor"),
            P(),
            P(None, ("dp", "tensor")),
            P("dp"),
            P("dp", None),
            P("dp", None),
            P("dp", None),
        ),
        out_specs=(P("dp", None), P("dp", None)),
        check_vma=False,
    )
```

```python
import functools

import jax
import jax.numpy as jnp
from jax import lax
from jax.experimental import pallas as pl
from jax.experimental.pallas import tpu as pltpu
from jax.sharding import PartitionSpec as P

LIVE = 16
BLOCK = 16
CODE = 128
DIGIT = 64
GROUP = 16


def vmem_limit(mebibytes):
    return pltpu.CompilerParams(vmem_limit_bytes=mebibytes * 1024 * 1024)


def in_hbm(x):
    return pltpu.with_memory_space_constraint(x, pltpu.HBM)


def pick_kernel(lengths, offsets, targets, mask, gain, hidden, rows, codes, place, gain_out, slots, blocks, sems):
    slot_count = offsets.shape[1]
    features = hidden.shape[2]
    last = lengths[0] - 1

    def order(j, live):
        alive = mask[0, j] != 0
        slots[jnp.where(alive, live, slot_count - 1 - (j - live))] = j
        return live + alive.astype(jnp.int32)

    live = lax.fori_loop(0, slot_count, order, 0, unroll=True)

    def block_copy(k):
        position = last - offsets[0, slots[k]]
        start = pl.multiple_of((position // BLOCK) * BLOCK, BLOCK)
        return pltpu.make_async_copy(hidden.at[0, pl.ds(start, BLOCK)], blocks.at[k], sems.at[k])

    for k in range(LIVE):
        block_copy(k).start()
    gain_out[...] = gain[...]

    row = lax.broadcasted_iota(jnp.int32, (LIVE, 1), 0)
    wanted = jnp.zeros((LIVE, 1), jnp.int32)
    target = jnp.zeros((LIVE, 1), jnp.int32)
    slot = jnp.full((LIVE, 1), -1, jnp.int32)
    for k in range(LIVE):
        j = slots[k]
        position = last - offsets[0, j]
        wanted = jnp.where(row == k, k * BLOCK + position % BLOCK, wanted)
        target = jnp.where(row == k, targets[0, j], target)
        slot = jnp.where(row == k, jnp.where(k < live, j, -1), slot)
    column = lax.broadcasted_iota(jnp.int32, (LIVE, LIVE * BLOCK), 1)
    select = jnp.where(column == wanted, 1.0, 0.0).astype(jnp.bfloat16)
    lane = lax.broadcasted_iota(jnp.int32, (LIVE, CODE), 1)
    digits = jnp.where(
        lane == 0,
        target % DIGIT,
        jnp.where(lane == 1, (target // DIGIT) % DIGIT, jnp.where(lane == 2, target // (DIGIT * DIGIT), 0)),
    )
    place[...] = jnp.where(lane == slot, 1.0, 0.0)
    codes[...] = digits.astype(jnp.float32).astype(jnp.bfloat16)
    for k in range(LIVE):
        block_copy(k).wait()
    picked = jnp.dot(
        select, blocks[...].reshape(LIVE * BLOCK, features), preferred_element_type=jnp.float32
    )
    rows[...] = picked.astype(jnp.bfloat16)


def pick(hidden, gain, lengths, offsets, targets, mask):
    features = hidden.shape[2]
    smem = pl.BlockSpec(memory_space=pltpu.SMEM)
    vmem = pl.BlockSpec(memory_space=pltpu.VMEM)
    return pl.pallas_call(
        pick_kernel,
        out_shape=(
            jax.ShapeDtypeStruct((LIVE, features), jnp.bfloat16),
            jax.ShapeDtypeStruct((LIVE, CODE), jnp.bfloat16),
            jax.ShapeDtypeStruct((LIVE, CODE), jnp.float32),
            jax.ShapeDtypeStruct((1, gain.shape[0]), jnp.float32),
        ),
        in_specs=[smem] * 4 + [vmem, pl.BlockSpec(memory_space=pltpu.HBM)],
        out_specs=(vmem, vmem, vmem, vmem),
        scratch_shapes=[
            pltpu.SMEM((offsets.shape[1],), jnp.int32),
            pltpu.VMEM((LIVE, BLOCK, features), jnp.bfloat16),
            pltpu.SemaphoreType.DMA((LIVE,)),
        ],
        compiler_params=vmem_limit(32),
        name="pick",
    )(lengths, *map(in_hbm, (offsets, targets, mask, gain.reshape(1, -1), hidden)))


def join_kernel(shard, *refs):
    tensor = len(refs) - 3
    parts, (codes, gain, rows) = refs[:tensor], refs[tensor:]
    live, features = parts[0].shape
    square = jnp.zeros((live, 1), jnp.float32)
    for part in parts:
        values = part[...].astype(jnp.float32)
        square += jnp.sum(values * values, axis=-1, keepdims=True)
    scale = lax.rsqrt(square / (tensor * features) + 1e-06)
    for s, part in enumerate(parts):
        span = pl.ds(pl.multiple_of((shard[0] ^ s) * features, features), features)
        rows[:, span] = (part[...].astype(jnp.float32) * scale * gain[:, span]).astype(jnp.bfloat16)
    rows[:, tensor * features :] = codes[...]


def join(parts, codes, gain, shard):
    tensor = len(parts)
    live, features = parts[0].shape
    vmem = pl.BlockSpec(memory_space=pltpu.VMEM)
    return pl.pallas_call(
        join_kernel,
        out_shape=jax.ShapeDtypeStruct((live, tensor * features + CODE), jnp.bfloat16),
        in_specs=[pl.BlockSpec(memory_space=pltpu.SMEM)] + [vmem] * (tensor + 2),
        out_specs=vmem,
        compiler_params=vmem_limit(32),
        name="join",
    )(shard, *parts, codes, gain)


def fetch_kernel(head, rows, held, rows_out, sems):
    count = sems.shape[0]
    depth = head.shape[0] // count
    copies = [
        pltpu.make_async_copy(head.at[pl.ds(i * depth, depth)], held.at[pl.ds(i * depth, depth)], sems.at[i])
        for i in range(count)
    ]
    for copy in copies:
        copy.start()
    rows_out[...] = rows[...]
    for copy in copies:
        copy.wait()


def fetch(head, rows):
    vmem = pl.BlockSpec(memory_space=pltpu.VMEM)
    return pl.pallas_call(
        fetch_kernel,
        out_shape=(jax.ShapeDtypeStruct(head.shape, head.dtype), jax.ShapeDtypeStruct(rows.shape, rows.dtype)),
        in_specs=[pl.BlockSpec(memory_space=pltpu.HBM), vmem],
        out_specs=(vmem, vmem),
        scratch_shapes=[pltpu.SemaphoreType.DMA((4,))],
        compiler_params=vmem_limit(32),
        cost_estimate=pl.CostEstimate(flops=0, bytes_accessed=2 * head.size * 2, transcendentals=0),
        name="fetch",
    )(in_hbm(head), rows)


def score_kernel(index, start, *refs):
    dp = len(refs) - 2
    pieces, (head, stats) = refs[:dp], refs[dp:]
    depth, vocab_width = head.shape
    live = pieces[0].shape[0]
    row_count = dp * live
    mine = index[0]

    normed = jnp.concatenate([piece[:, :depth] for piece in pieces], axis=0)
    logits = jnp.dot(normed, head[...], preferred_element_type=jnp.float32)
    digits = jnp.concatenate([piece[:, depth:] for piece in pieces], axis=0).astype(jnp.float32)
    lane = lax.broadcasted_iota(jnp.int32, (row_count, CODE), 1)
    weight = jnp.where(lane == 0, 1.0, jnp.where(lane == 1, float(DIGIT), jnp.where(lane == 2, float(DIGIT * DIGIT), 0.0)))
    target = jnp.sum(digits * weight, axis=-1, keepdims=True).astype(jnp.int32) - start[0]
    column = lax.broadcasted_iota(jnp.int32, (row_count, vocab_width), 1)
    top = jnp.max(logits, axis=-1, keepdims=True)
    expo = jnp.exp(logits - top)
    total = jnp.sum(expo, axis=-1, keepdims=True)
    weighted = jnp.sum(expo * logits, axis=-1, keepdims=True)
    chosen = jnp.sum(jnp.where(column == target, logits, 0.0), axis=-1, keepdims=True)
    spot = lane - lax.broadcasted_iota(jnp.int32, (row_count, CODE), 0) % live
    table = jnp.zeros((row_count, CODE), jnp.float32)
    for group, value in enumerate((top, total, weighted, chosen)):
        table = jnp.where(spot == GROUP * group, value, table)
    for d in range(dp):
        line = jnp.sum(table[d * live : (d + 1) * live], axis=0, keepdims=True)
        for t in range(stats.shape[1]):
            stats[mine ^ d, t] = line


def score(pieces, head, index, start, copies):
    dp = len(pieces)
    live, width = pieces[0].shape
    vmem = pl.BlockSpec(memory_space=pltpu.VMEM)
    return pl.pallas_call(
        score_kernel,
        out_shape=jax.ShapeDtypeStruct((dp, copies, 1, CODE), jnp.float32),
        in_specs=[pl.BlockSpec(memory_space=pltpu.SMEM)] * 2 + [vmem] * (dp + 1),
        out_specs=vmem,
        compiler_params=vmem_limit(32),
        name="score",
    )(index, start, *pieces, head)


def combine(values):
    lane = lax.broadcasted_iota(jnp.int32, values.shape, 1)
    top = jnp.where(lane < GROUP, values, 0.0)
    top = top + pltpu.roll(top, GROUP, 1)
    top = top + pltpu.roll(top, 2 * GROUP, 1)
    best = jnp.max(top, axis=0, keepdims=True)
    factor = jnp.where(lane < 3 * GROUP, jnp.exp(top - best), 1.0)
    return jnp.sum(values * factor, axis=0, keepdims=True), best


def finish_kernel(stats, place, logprob, entropy):
    live = place.shape[0]
    slot_count = logprob.shape[1]
    sums, best = combine(stats[:, 0, :])
    line = jnp.broadcast_to(sums, (8, CODE))
    total = pltpu.roll(line, CODE - GROUP, 1)
    weighted = pltpu.roll(line, CODE - 2 * GROUP, 1)
    chosen = pltpu.roll(line, CODE - 3 * GROUP, 1)
    lse = best + jnp.log(total)
    kind = lax.broadcasted_iota(jnp.int32, (8, CODE), 0)
    merged = jnp.where(kind == 0, chosen - lse, lse - weighted / total)
    merged = jnp.where(lax.broadcasted_iota(jnp.int32, (8, CODE), 1) < GROUP, merged, 0.0)
    spread = jnp.concatenate([place[...], jnp.zeros((CODE - live, CODE), jnp.float32)], axis=0)
    out = jnp.dot(merged, spread, precision=lax.Precision.HIGHEST, preferred_element_type=jnp.float32)
    logprob[...] = out[0:1, :slot_count]
    entropy[...] = out[1:2, :slot_count]


def finish(stats, place, slot_count):
    vmem = pl.BlockSpec(memory_space=pltpu.VMEM)
    out = jax.ShapeDtypeStruct((1, slot_count), jnp.float32)
    return pl.pallas_call(
        finish_kernel,
        out_shape=(out, out),
        in_specs=[vmem, vmem],
        out_specs=(vmem, vmem),
        compiler_params=vmem_limit(32),
        name="finish",
    )(stats, place)


def swap(x, axis, distance):
    return lax.ppermute(x, axis, [(i, i ^ distance) for i in range(lax.axis_size(axis))])


def per_device(hidden, gain, head, lengths, offsets, targets, mask):
    dp, tensor = lax.axis_size("dp"), lax.axis_size("tensor")
    mine, shard = lax.axis_index("dp"), lax.axis_index("tensor")
    start = (mine * tensor + shard) * head.shape[1]
    rows, codes, slots, gain = pick(hidden, gain, lengths, offsets, targets, mask)
    parts = {0: rows} | {s: swap(rows, "tensor", s) for s in reversed(range(1, tensor))}
    rows = join([parts[s] for s in range(tensor)], codes, gain, shard.reshape(1))

    pieces = {d: swap(rows, "dp", d) for d in reversed(range(2, dp, 2))}
    held, pieces[0] = fetch(head, rows)
    for d in range(0, dp, 2):
        pieces[d + 1] = swap(pieces[d], "dp", 1)
    stats = score([pieces[d] for d in range(dp)], held, mine.reshape(1), start.reshape(1), tensor)
    stats = lax.all_to_all(stats.reshape(dp * tensor, 1, CODE), ("dp", "tensor"), 0, 0, tiled=True)
    return finish(stats, slots, offsets.shape[1])


def solution(mesh):
    return jax.shard_map(
        per_device,
        mesh=mesh,
        in_specs=(
            P("dp", None, "tensor"),
            P(),
            P(None, ("dp", "tensor")),
            P("dp"),
            P("dp", None),
            P("dp", None),
            P("dp", None),
        ),
        out_specs=(P("dp", None), P("dp", None)),
        check_vma=False,
    )
```

```python
import functools

import jax
import jax.numpy as jnp
from jax import lax
from jax.experimental import pallas as pl
from jax.experimental.pallas import tpu as pltpu
from jax.sharding import PartitionSpec as P

LIVE = 16
BLOCK = 16
CODE = 128
DIGIT = 64
GROUP = 16


def vmem_limit(mebibytes):
    return pltpu.CompilerParams(vmem_limit_bytes=mebibytes * 1024 * 1024)


def in_hbm(x):
    return pltpu.with_memory_space_constraint(x, pltpu.HBM)


def pick_kernel(lengths, offsets, targets, mask, gain, hidden, rows, codes, place, gain_out, slots, blocks, sems):
    slot_count = offsets.shape[1]
    features = hidden.shape[2]
    last = lengths[0] - 1

    def order(j, live):
        alive = mask[0, j] != 0
        slots[jnp.where(alive, live, slot_count - 1 - (j - live))] = j
        return live + alive.astype(jnp.int32)

    live = lax.fori_loop(0, slot_count, order, 0, unroll=True)

    def block_copy(k):
        position = last - offsets[0, slots[k]]
        start = pl.multiple_of((position // BLOCK) * BLOCK, BLOCK)
        return pltpu.make_async_copy(hidden.at[0, pl.ds(start, BLOCK)], blocks.at[k], sems.at[k])

    for k in range(LIVE):
        block_copy(k).start()
    gain_out[...] = gain[...]

    row = lax.broadcasted_iota(jnp.int32, (LIVE, 1), 0)
    wanted = jnp.zeros((LIVE, 1), jnp.int32)
    target = jnp.zeros((LIVE, 1), jnp.int32)
    slot = jnp.full((LIVE, 1), -1, jnp.int32)
    for k in range(LIVE):
        j = slots[k]
        position = last - offsets[0, j]
        wanted = jnp.where(row == k, k * BLOCK + position % BLOCK, wanted)
        target = jnp.where(row == k, targets[0, j], target)
        slot = jnp.where(row == k, jnp.where(k < live, j, -1), slot)
    column = lax.broadcasted_iota(jnp.int32, (LIVE, LIVE * BLOCK), 1)
    select = jnp.where(column == wanted, 1.0, 0.0).astype(jnp.bfloat16)
    lane = lax.broadcasted_iota(jnp.int32, (LIVE, CODE), 1)
    digits = jnp.where(
        lane == 0,
        target % DIGIT,
        jnp.where(lane == 1, (target // DIGIT) % DIGIT, jnp.where(lane == 2, target // (DIGIT * DIGIT), 0)),
    )
    place[...] = jnp.where(lane == slot, 1.0, 0.0)
    codes[...] = digits.astype(jnp.float32).astype(jnp.bfloat16)
    for k in range(LIVE):
        block_copy(k).wait()
    picked = jnp.dot(
        select, blocks[...].reshape(LIVE * BLOCK, features), preferred_element_type=jnp.float32
    )
    rows[...] = picked.astype(jnp.bfloat16)


def pick(hidden, gain, lengths, offsets, targets, mask):
    features = hidden.shape[2]
    smem = pl.BlockSpec(memory_space=pltpu.SMEM)
    vmem = pl.BlockSpec(memory_space=pltpu.VMEM)
    return pl.pallas_call(
        pick_kernel,
        out_shape=(
            jax.ShapeDtypeStruct((LIVE, features), jnp.bfloat16),
            jax.ShapeDtypeStruct((LIVE, CODE), jnp.bfloat16),
            jax.ShapeDtypeStruct((LIVE, CODE), jnp.float32),
            jax.ShapeDtypeStruct((1, gain.shape[0]), jnp.float32),
        ),
        in_specs=[smem] * 4 + [vmem, pl.BlockSpec(memory_space=pltpu.HBM)],
        out_specs=(vmem, vmem, vmem, vmem),
        scratch_shapes=[
            pltpu.SMEM((offsets.shape[1],), jnp.int32),
            pltpu.VMEM((LIVE, BLOCK, features), jnp.bfloat16),
            pltpu.SemaphoreType.DMA((LIVE,)),
        ],
        compiler_params=vmem_limit(32),
        name="pick",
    )(lengths, *map(in_hbm, (offsets, targets, mask, gain.reshape(1, -1), hidden)))


def join_kernel(shard, *refs):
    tensor = len(refs) - 3
    parts, (codes, gain, rows) = refs[:tensor], refs[tensor:]
    live, features = parts[0].shape
    square = jnp.zeros((live, 1), jnp.float32)
    for part in parts:
        values = part[...].astype(jnp.float32)
        square += jnp.sum(values * values, axis=-1, keepdims=True)
    scale = lax.rsqrt(square / (tensor * features) + 1e-06)
    for s, part in enumerate(parts):
        span = pl.ds(pl.multiple_of((shard[0] ^ s) * features, features), features)
        rows[:, span] = (part[...].astype(jnp.float32) * scale * gain[:, span]).astype(jnp.bfloat16)
    rows[:, tensor * features :] = codes[...]


def join(parts, codes, gain, shard):
    tensor = len(parts)
    live, features = parts[0].shape
    vmem = pl.BlockSpec(memory_space=pltpu.VMEM)
    return pl.pallas_call(
        join_kernel,
        out_shape=jax.ShapeDtypeStruct((live, tensor * features + CODE), jnp.bfloat16),
        in_specs=[pl.BlockSpec(memory_space=pltpu.SMEM)] + [vmem] * (tensor + 2),
        out_specs=vmem,
        compiler_params=vmem_limit(32),
        name="join",
    )(shard, *parts, codes, gain)


def fetch_kernel(head, rows, held, rows_out, sems):
    count = sems.shape[0]
    depth = head.shape[0] // count
    copies = [
        pltpu.make_async_copy(head.at[pl.ds(i * depth, depth)], held.at[pl.ds(i * depth, depth)], sems.at[i])
        for i in range(count)
    ]
    for copy in copies:
        copy.start()
    rows_out[...] = rows[...]
    for copy in copies:
        copy.wait()


def fetch(head, rows):
    vmem = pl.BlockSpec(memory_space=pltpu.VMEM)
    return pl.pallas_call(
        fetch_kernel,
        out_shape=(pltpu.VMEM(head.shape, head.dtype), jax.ShapeDtypeStruct(rows.shape, rows.dtype)),
        in_specs=[pl.BlockSpec(memory_space=pltpu.HBM), vmem],
        out_specs=(vmem, vmem),
        scratch_shapes=[pltpu.SemaphoreType.DMA((4,))],
        compiler_params=vmem_limit(32),
        cost_estimate=pl.CostEstimate(flops=0, bytes_accessed=2 * head.size * 2, transcendentals=0),
        name="fetch",
    )(in_hbm(head), rows)


def score_kernel(index, start, *refs):
    dp = len(refs) - 2
    pieces, (head, stats) = refs[:dp], refs[dp:]
    depth, vocab_width = head.shape
    live = pieces[0].shape[0]
    row_count = dp * live
    mine = index[0]

    normed = jnp.concatenate([piece[:, :depth] for piece in pieces], axis=0)
    logits = jnp.dot(normed, head[...], preferred_element_type=jnp.float32)
    digits = jnp.concatenate([piece[:, depth:] for piece in pieces], axis=0).astype(jnp.float32)
    lane = lax.broadcasted_iota(jnp.int32, (row_count, CODE), 1)
    weight = jnp.where(lane == 0, 1.0, jnp.where(lane == 1, float(DIGIT), jnp.where(lane == 2, float(DIGIT * DIGIT), 0.0)))
    target = jnp.sum(digits * weight, axis=-1, keepdims=True).astype(jnp.int32) - start[0]
    column = lax.broadcasted_iota(jnp.int32, (row_count, vocab_width), 1)
    top = jnp.max(logits, axis=-1, keepdims=True)
    expo = jnp.exp(logits - top)
    total = jnp.sum(expo, axis=-1, keepdims=True)
    weighted = jnp.sum(expo * logits, axis=-1, keepdims=True)
    chosen = jnp.sum(jnp.where(column == target, logits, 0.0), axis=-1, keepdims=True)
    spot = lane - lax.broadcasted_iota(jnp.int32, (row_count, CODE), 0) % live
    table = jnp.zeros((row_count, CODE), jnp.float32)
    for group, value in enumerate((top, total, weighted, chosen)):
        table = jnp.where(spot == GROUP * group, value, table)
    for d in range(dp):
        line = jnp.sum(table[d * live : (d + 1) * live], axis=0, keepdims=True)
        for t in range(stats.shape[1]):
            stats[mine ^ d, t] = line


def score(pieces, head, index, start, copies):
    dp = len(pieces)
    live, width = pieces[0].shape
    vmem = pl.BlockSpec(memory_space=pltpu.VMEM)
    return pl.pallas_call(
        score_kernel,
        out_shape=jax.ShapeDtypeStruct((dp, copies, 1, CODE), jnp.float32),
        in_specs=[pl.BlockSpec(memory_space=pltpu.SMEM)] * 2 + [vmem] * (dp + 1),
        out_specs=vmem,
        compiler_params=vmem_limit(32),
        name="score",
    )(index, start, *pieces, pltpu.with_memory_space_constraint(head, pltpu.VMEM))


def combine(values):
    lane = lax.broadcasted_iota(jnp.int32, values.shape, 1)
    top = jnp.where(lane < GROUP, values, 0.0)
    top = top + pltpu.roll(top, GROUP, 1)
    top = top + pltpu.roll(top, 2 * GROUP, 1)
    best = jnp.max(top, axis=0, keepdims=True)
    factor = jnp.where(lane < 3 * GROUP, jnp.exp(top - best), 1.0)
    return jnp.sum(values * factor, axis=0, keepdims=True), best


def finish_kernel(stats, place, logprob, entropy):
    live = place.shape[0]
    slot_count = logprob.shape[1]
    sums, best = combine(stats[:, 0, :])
    line = jnp.broadcast_to(sums, (8, CODE))
    total = pltpu.roll(line, CODE - GROUP, 1)
    weighted = pltpu.roll(line, CODE - 2 * GROUP, 1)
    chosen = pltpu.roll(line, CODE - 3 * GROUP, 1)
    lse = best + jnp.log(total)
    kind = lax.broadcasted_iota(jnp.int32, (8, CODE), 0)
    merged = jnp.where(kind == 0, chosen - lse, lse - weighted / total)
    merged = jnp.where(lax.broadcasted_iota(jnp.int32, (8, CODE), 1) < GROUP, merged, 0.0)
    spread = jnp.concatenate([place[...], jnp.zeros((CODE - live, CODE), jnp.float32)], axis=0)
    out = jnp.dot(merged, spread, precision=lax.Precision.HIGHEST, preferred_element_type=jnp.float32)
    logprob[...] = out[0:1, :slot_count]
    entropy[...] = out[1:2, :slot_count]


def finish(stats, place, slot_count):
    vmem = pl.BlockSpec(memory_space=pltpu.VMEM)
    out = jax.ShapeDtypeStruct((1, slot_count), jnp.float32)
    return pl.pallas_call(
        finish_kernel,
        out_shape=(out, out),
        in_specs=[vmem, vmem],
        out_specs=(vmem, vmem),
        compiler_params=vmem_limit(32),
        name="finish",
    )(stats, place)


def swap(x, axis, distance):
    return lax.ppermute(x, axis, [(i, i ^ distance) for i in range(lax.axis_size(axis))])


def per_device(hidden, gain, head, lengths, offsets, targets, mask):
    dp, tensor = lax.axis_size("dp"), lax.axis_size("tensor")
    mine, shard = lax.axis_index("dp"), lax.axis_index("tensor")
    start = (mine * tensor + shard) * head.shape[1]
    rows, codes, slots, gain = pick(hidden, gain, lengths, offsets, targets, mask)
    parts = {0: rows} | {s: swap(rows, "tensor", s) for s in reversed(range(1, tensor))}
    rows = join([parts[s] for s in range(tensor)], codes, gain, shard.reshape(1))

    pieces = {d: swap(rows, "dp", d) for d in reversed(range(2, dp, 2))}
    held, pieces[0] = fetch(head, rows)
    for d in range(0, dp, 2):
        pieces[d + 1] = swap(pieces[d], "dp", 1)
    stats = score([pieces[d] for d in range(dp)], held, mine.reshape(1), start.reshape(1), tensor)
    stats = lax.all_to_all(stats.reshape(dp * tensor, 1, CODE), ("dp", "tensor"), 0, 0, tiled=True)
    return finish(stats, slots, offsets.shape[1])


def solution(mesh):
    return jax.shard_map(
        per_device,
        mesh=mesh,
        in_specs=(
            P("dp", None, "tensor"),
            P(),
            P(None, ("dp", "tensor")),
            P("dp"),
            P("dp", None),
            P("dp", None),
            P("dp", None),
        ),
        out_specs=(P("dp", None), P("dp", None)),
        check_vma=False,
    )
```

```python
import functools

import jax
import jax.numpy as jnp
from jax import lax
from jax.experimental import pallas as pl
from jax.experimental.pallas import tpu as pltpu
from jax.sharding import PartitionSpec as P

LIVE = 16
BLOCK = 16
CODE = 128
DIGIT = 64
GROUP = 16


def vmem_limit(mebibytes):
    return pltpu.CompilerParams(vmem_limit_bytes=mebibytes * 1024 * 1024)


def in_hbm(x):
    return pltpu.with_memory_space_constraint(x, pltpu.HBM)


def pick_kernel(lengths, offsets, targets, mask, gain, hidden, rows, codes, place, gain_out, slots, blocks, sems):
    slot_count = offsets.shape[1]
    features = hidden.shape[2]
    last = lengths[0] - 1

    def order(j, live):
        alive = mask[0, j] != 0
        slots[jnp.where(alive, live, slot_count - 1 - (j - live))] = j
        return live + alive.astype(jnp.int32)

    live = lax.fori_loop(0, slot_count, order, 0, unroll=True)

    def block_copy(k):
        position = last - offsets[0, slots[k]]
        start = pl.multiple_of((position // BLOCK) * BLOCK, BLOCK)
        return pltpu.make_async_copy(hidden.at[0, pl.ds(start, BLOCK)], blocks.at[k], sems.at[k])

    for k in range(LIVE):
        block_copy(k).start()
    gain_out[...] = gain[...]

    row = lax.broadcasted_iota(jnp.int32, (LIVE, 1), 0)
    wanted = jnp.zeros((LIVE, 1), jnp.int32)
    target = jnp.zeros((LIVE, 1), jnp.int32)
    slot = jnp.full((LIVE, 1), -1, jnp.int32)
    for k in range(LIVE):
        j = slots[k]
        position = last - offsets[0, j]
        wanted = jnp.where(row == k, k * BLOCK + position % BLOCK, wanted)
        target = jnp.where(row == k, targets[0, j], target)
        slot = jnp.where(row == k, jnp.where(k < live, j, -1), slot)
    column = lax.broadcasted_iota(jnp.int32, (LIVE, LIVE * BLOCK), 1)
    select = jnp.where(column == wanted, 1.0, 0.0).astype(jnp.bfloat16)
    lane = lax.broadcasted_iota(jnp.int32, (LIVE, CODE), 1)
    digits = jnp.where(
        lane == 0,
        target % DIGIT,
        jnp.where(lane == 1, (target // DIGIT) % DIGIT, jnp.where(lane == 2, target // (DIGIT * DIGIT), 0)),
    )
    place[...] = jnp.where(lane == slot, 1.0, 0.0)
    codes[...] = digits.astype(jnp.float32).astype(jnp.bfloat16)
    for k in range(LIVE):
        block_copy(k).wait()
    picked = jnp.dot(
        select, blocks[...].reshape(LIVE * BLOCK, features), preferred_element_type=jnp.float32
    )
    rows[...] = picked.astype(jnp.bfloat16)


def pick(hidden, gain, lengths, offsets, targets, mask):
    features = hidden.shape[2]
    smem = pl.BlockSpec(memory_space=pltpu.SMEM)
    vmem = pl.BlockSpec(memory_space=pltpu.VMEM)
    return pl.pallas_call(
        pick_kernel,
        out_shape=(
            jax.ShapeDtypeStruct((LIVE, features), jnp.bfloat16),
            jax.ShapeDtypeStruct((LIVE, CODE), jnp.bfloat16),
            jax.ShapeDtypeStruct((LIVE, CODE), jnp.float32),
            jax.ShapeDtypeStruct((1, gain.shape[0]), jnp.float32),
        ),
        in_specs=[smem] * 4 + [vmem, pl.BlockSpec(memory_space=pltpu.HBM)],
        out_specs=(vmem, vmem, vmem, vmem),
        scratch_shapes=[
            pltpu.SMEM((offsets.shape[1],), jnp.int32),
            pltpu.VMEM((LIVE, BLOCK, features), jnp.bfloat16),
            pltpu.SemaphoreType.DMA((LIVE,)),
        ],
        compiler_params=vmem_limit(32),
        name="pick",
    )(lengths, *map(in_hbm, (offsets, targets, mask, gain.reshape(1, -1), hidden)))


def join_kernel(*refs):
    tensor = len(refs) - 3
    parts, (codes, gain, rows) = refs[:tensor], refs[tensor:]
    live, features = parts[0].shape
    square = jnp.zeros((live, 1), jnp.float32)
    for part in parts:
        values = part[...].astype(jnp.float32)
        square += jnp.sum(values * values, axis=-1, keepdims=True)
    scale = lax.rsqrt(square / (tensor * features) + 1e-06)
    shard = lax.axis_index("tensor")
    for s, part in enumerate(parts):
        span = pl.ds(pl.multiple_of((shard ^ s) * features, features), features)
        rows[:, span] = (part[...].astype(jnp.float32) * scale * gain[:, span]).astype(jnp.bfloat16)
    rows[:, tensor * features :] = codes[...]


def join(parts, codes, gain):
    tensor = len(parts)
    live, features = parts[0].shape
    vmem = pl.BlockSpec(memory_space=pltpu.VMEM)
    return pl.pallas_call(
        join_kernel,
        out_shape=jax.ShapeDtypeStruct((live, tensor * features + CODE), jnp.bfloat16),
        in_specs=[vmem] * (tensor + 2),
        out_specs=vmem,
        compiler_params=vmem_limit(32),
        name="join",
    )(*parts, codes, gain)


def fetch_kernel(head, rows, held, rows_out, sems):
    count = sems.shape[0]
    depth = head.shape[0] // count
    copies = [
        pltpu.make_async_copy(head.at[pl.ds(i * depth, depth)], held.at[pl.ds(i * depth, depth)], sems.at[i])
        for i in range(count)
    ]
    for copy in copies:
        copy.start()
    rows_out[...] = rows[...]
    for copy in copies:
        copy.wait()


def fetch(head, rows):
    vmem = pl.BlockSpec(memory_space=pltpu.VMEM)
    return pl.pallas_call(
        fetch_kernel,
        out_shape=(pltpu.VMEM(head.shape, head.dtype), jax.ShapeDtypeStruct(rows.shape, rows.dtype)),
        in_specs=[pl.BlockSpec(memory_space=pltpu.HBM), vmem],
        out_specs=(vmem, vmem),
        scratch_shapes=[pltpu.SemaphoreType.DMA((4,))],
        compiler_params=vmem_limit(32),
        cost_estimate=pl.CostEstimate(flops=0, bytes_accessed=2 * head.size * 2, transcendentals=0),
        name="fetch",
    )(in_hbm(head), rows)


def score_kernel(*refs):
    dp = len(refs) - 2
    pieces, (head, stats) = refs[:dp], refs[dp:]
    depth, vocab_width = head.shape
    live = pieces[0].shape[0]
    row_count = dp * live
    mine = lax.axis_index("dp")
    start = (mine * stats.shape[1] + lax.axis_index("tensor")) * vocab_width

    normed = jnp.concatenate([piece[:, :depth] for piece in pieces], axis=0)
    logits = jnp.dot(normed, head[...], preferred_element_type=jnp.float32)
    digits = jnp.concatenate([piece[:, depth:] for piece in pieces], axis=0).astype(jnp.float32)
    lane = lax.broadcasted_iota(jnp.int32, (row_count, CODE), 1)
    weight = jnp.where(lane == 0, 1.0, jnp.where(lane == 1, float(DIGIT), jnp.where(lane == 2, float(DIGIT * DIGIT), 0.0)))
    target = jnp.sum(digits * weight, axis=-1, keepdims=True).astype(jnp.int32) - start
    column = lax.broadcasted_iota(jnp.int32, (row_count, vocab_width), 1)
    top = jnp.max(logits, axis=-1, keepdims=True)
    expo = jnp.exp(logits - top)
    total = jnp.sum(expo, axis=-1, keepdims=True)
    weighted = jnp.sum(expo * logits, axis=-1, keepdims=True)
    chosen = jnp.sum(jnp.where(column == target, logits, 0.0), axis=-1, keepdims=True)
    spot = lane - lax.broadcasted_iota(jnp.int32, (row_count, CODE), 0) % live
    table = jnp.zeros((row_count, CODE), jnp.float32)
    for group, value in enumerate((top, total, weighted, chosen)):
        table = jnp.where(spot == GROUP * group, value, table)
    for d in range(dp):
        line = jnp.sum(table[d * live : (d + 1) * live], axis=0, keepdims=True)
        for t in range(stats.shape[1]):
            stats[mine ^ d, t] = line


def score(pieces, head, copies):
    dp = len(pieces)
    live, width = pieces[0].shape
    vmem = pl.BlockSpec(memory_space=pltpu.VMEM)
    return pl.pallas_call(
        score_kernel,
        out_shape=jax.ShapeDtypeStruct((dp, copies, 1, CODE), jnp.float32),
        in_specs=[vmem] * (dp + 1),
        out_specs=vmem,
        compiler_params=vmem_limit(32),
        name="score",
    )(*pieces, pltpu.with_memory_space_constraint(head, pltpu.VMEM))


def combine(values):
    lane = lax.broadcasted_iota(jnp.int32, values.shape, 1)
    top = jnp.where(lane < GROUP, values, 0.0)
    top = top + pltpu.roll(top, GROUP, 1)
    top = top + pltpu.roll(top, 2 * GROUP, 1)
    best = jnp.max(top, axis=0, keepdims=True)
    factor = jnp.where(lane < 3 * GROUP, jnp.exp(top - best), 1.0)
    return jnp.sum(values * factor, axis=0, keepdims=True), best


def finish_kernel(stats, place, logprob, entropy):
    live = place.shape[0]
    slot_count = logprob.shape[1]
    sums, best = combine(stats[:, 0, :])
    line = jnp.broadcast_to(sums, (8, CODE))
    total = pltpu.roll(line, CODE - GROUP, 1)
    weighted = pltpu.roll(line, CODE - 2 * GROUP, 1)
    chosen = pltpu.roll(line, CODE - 3 * GROUP, 1)
    lse = best + jnp.log(total)
    kind = lax.broadcasted_iota(jnp.int32, (8, CODE), 0)
    merged = jnp.where(kind == 0, chosen - lse, lse - weighted / total)
    merged = jnp.where(lax.broadcasted_iota(jnp.int32, (8, CODE), 1) < GROUP, merged, 0.0)
    spread = jnp.concatenate([place[...], jnp.zeros((CODE - live, CODE), jnp.float32)], axis=0)
    out = jnp.dot(merged, spread, precision=lax.Precision.HIGHEST, preferred_element_type=jnp.float32)
    logprob[...] = out[0:1, :slot_count]
    entropy[...] = out[1:2, :slot_count]


def finish(stats, place, slot_count):
    vmem = pl.BlockSpec(memory_space=pltpu.VMEM)
    out = jax.ShapeDtypeStruct((1, slot_count), jnp.float32)
    return pl.pallas_call(
        finish_kernel,
        out_shape=(out, out),
        in_specs=[vmem, vmem],
        out_specs=(vmem, vmem),
        compiler_params=vmem_limit(32),
        name="finish",
    )(stats, place)


def swap(x, axis, distance):
    return lax.ppermute(x, axis, [(i, i ^ distance) for i in range(lax.axis_size(axis))])


def per_device(hidden, gain, head, lengths, offsets, targets, mask):
    dp, tensor = lax.axis_size("dp"), lax.axis_size("tensor")
    rows, codes, slots, gain = pick(hidden, gain, lengths, offsets, targets, mask)
    parts = {0: rows} | {s: swap(rows, "tensor", s) for s in reversed(range(1, tensor))}
    rows = join([parts[s] for s in range(tensor)], codes, gain)

    pieces = {d: swap(rows, "dp", d) for d in reversed(range(2, dp, 2))}
    held, pieces[0] = fetch(head, rows)
    for d in range(0, dp, 2):
        pieces[d + 1] = swap(pieces[d], "dp", 1)
    stats = score([pieces[d] for d in range(dp)], held, tensor)
    stats = lax.all_to_all(stats.reshape(dp * tensor, 1, CODE), ("dp", "tensor"), 0, 0, tiled=True)
    return finish(stats, slots, offsets.shape[1])


def solution(mesh):
    return jax.shard_map(
        per_device,
        mesh=mesh,
        in_specs=(
            P("dp", None, "tensor"),
            P(),
            P(None, ("dp", "tensor")),
            P("dp"),
            P("dp", None),
            P("dp", None),
            P("dp", None),
        ),
        out_specs=(P("dp", None), P("dp", None)),
        check_vma=False,
    )
```

```python
import functools

import jax
import jax.numpy as jnp
from jax import lax
from jax.experimental import pallas as pl
from jax.experimental.pallas import tpu as pltpu
from jax.sharding import PartitionSpec as P

LIVE = 16
BLOCK = 16
CODE = 128
DIGIT = 64
GROUP = 16


def vmem_limit(mebibytes):
    return pltpu.CompilerParams(vmem_limit_bytes=mebibytes * 1024 * 1024)


def in_hbm(x):
    return pltpu.with_memory_space_constraint(x, pltpu.HBM)


def pick_kernel(lengths, offsets, targets, mask, gain, hidden, rows, codes, place, gain_out, slots, blocks, sems):
    slot_count = offsets.shape[1]
    features = hidden.shape[2]
    last = lengths[0] - 1

    def order(j, live):
        alive = mask[0, j] != 0
        slots[jnp.where(alive, live, slot_count - 1 - (j - live))] = j
        return live + alive.astype(jnp.int32)

    live = lax.fori_loop(0, slot_count, order, 0, unroll=True)

    def block_copy(k):
        position = last - offsets[0, slots[k]]
        start = pl.multiple_of((position // BLOCK) * BLOCK, BLOCK)
        return pltpu.make_async_copy(hidden.at[0, pl.ds(start, BLOCK)], blocks.at[k], sems.at[k])

    for k in range(LIVE):
        block_copy(k).start()
    gain_out[...] = gain[...]

    row = lax.broadcasted_iota(jnp.int32, (LIVE, 1), 0)
    wanted = jnp.zeros((LIVE, 1), jnp.int32)
    target = jnp.zeros((LIVE, 1), jnp.int32)
    slot = jnp.full((LIVE, 1), -1, jnp.int32)
    for k in range(LIVE):
        j = slots[k]
        position = last - offsets[0, j]
        wanted = jnp.where(row == k, k * BLOCK + position % BLOCK, wanted)
        target = jnp.where(row == k, targets[0, j], target)
        slot = jnp.where(row == k, jnp.where(k < live, j, -1), slot)
    column = lax.broadcasted_iota(jnp.int32, (LIVE, LIVE * BLOCK), 1)
    select = jnp.where(column == wanted, 1.0, 0.0).astype(jnp.bfloat16)
    lane = lax.broadcasted_iota(jnp.int32, (LIVE, CODE), 1)
    digits = jnp.where(
        lane == 0,
        target % DIGIT,
        jnp.where(lane == 1, (target // DIGIT) % DIGIT, jnp.where(lane == 2, target // (DIGIT * DIGIT), 0)),
    )
    place[...] = jnp.where(lane == slot, 1.0, 0.0)
    codes[...] = digits.astype(jnp.float32).astype(jnp.bfloat16)
    for k in range(LIVE):
        block_copy(k).wait()
    picked = jnp.dot(
        select, blocks[...].reshape(LIVE * BLOCK, features), preferred_element_type=jnp.float32
    )
    rows[...] = picked.astype(jnp.bfloat16)


def pick(hidden, gain, lengths, offsets, targets, mask):
    features = hidden.shape[2]
    smem = pl.BlockSpec(memory_space=pltpu.SMEM)
    vmem = pl.BlockSpec(memory_space=pltpu.VMEM)
    return pl.pallas_call(
        pick_kernel,
        out_shape=(
            jax.ShapeDtypeStruct((LIVE, features), jnp.bfloat16),
            jax.ShapeDtypeStruct((LIVE, CODE), jnp.bfloat16),
            jax.ShapeDtypeStruct((LIVE, CODE), jnp.float32),
            jax.ShapeDtypeStruct((1, gain.shape[0]), jnp.float32),
        ),
        in_specs=[smem] * 4 + [vmem, pl.BlockSpec(memory_space=pltpu.HBM)],
        out_specs=(vmem, vmem, vmem, vmem),
        scratch_shapes=[
            pltpu.SMEM((offsets.shape[1],), jnp.int32),
            pltpu.VMEM((LIVE, BLOCK, features), jnp.bfloat16),
            pltpu.SemaphoreType.DMA((LIVE,)),
        ],
        compiler_params=vmem_limit(32),
        name="pick",
    )(lengths, *map(in_hbm, (offsets, targets, mask, gain.reshape(1, -1), hidden)))


def join_kernel(*refs):
    tensor = len(refs) - 3
    parts, (codes, gain, rows) = refs[:tensor], refs[tensor:]
    live, features = parts[0].shape
    square = jnp.zeros((live, 1), jnp.float32)
    for part in parts:
        values = part[...].astype(jnp.float32)
        square += jnp.sum(values * values, axis=-1, keepdims=True)
    scale = lax.rsqrt(square / (tensor * features) + 1e-06)
    shard = lax.axis_index("tensor")
    for s, part in enumerate(parts):
        span = pl.ds(pl.multiple_of((shard ^ s) * features, features), features)
        rows[:, span] = (part[...].astype(jnp.float32) * scale * gain[:, span]).astype(jnp.bfloat16)
    rows[:, tensor * features :] = codes[...]


def join(parts, codes, gain):
    tensor = len(parts)
    live, features = parts[0].shape
    vmem = pl.BlockSpec(memory_space=pltpu.VMEM)
    return pl.pallas_call(
        join_kernel,
        out_shape=jax.ShapeDtypeStruct((live, tensor * features + CODE), jnp.bfloat16),
        in_specs=[vmem] * (tensor + 2),
        out_specs=vmem,
        compiler_params=vmem_limit(32),
        name="join",
    )(*parts, codes, gain)


def fetch_kernel(half, head, after, held, after_out, sems):
    count = sems.shape[0]
    depth = held.shape[0] // count
    copies = [
        pltpu.make_async_copy(
            head.at[pl.ds(half * held.shape[0] + i * depth, depth)], held.at[pl.ds(i * depth, depth)], sems.at[i]
        )
        for i in range(count)
    ]
    for copy in copies:
        copy.start()
    after_out[...] = after[...]
    for copy in copies:
        copy.wait()


def fetch(head, half, after):
    vmem = pl.BlockSpec(memory_space=pltpu.VMEM)
    shape = (head.shape[0] // 2, head.shape[1])
    return pl.pallas_call(
        functools.partial(fetch_kernel, half),
        out_shape=(pltpu.VMEM(shape, head.dtype), jax.ShapeDtypeStruct(after.shape, after.dtype)),
        in_specs=[pl.BlockSpec(memory_space=pltpu.HBM), vmem],
        out_specs=(vmem, vmem),
        scratch_shapes=[pltpu.SemaphoreType.DMA((4,))],
        compiler_params=vmem_limit(32),
        cost_estimate=pl.CostEstimate(flops=0, bytes_accessed=2 * head.size, transcendentals=0),
        name="fetch",
    )(in_hbm(head), after)


def score_kernel(order, *refs):
    dp = len(order)
    pieces, (first, second, stats) = refs[:dp], refs[dp:]
    depth, vocab_width = 2 * first.shape[0], first.shape[1]
    live = pieces[0].shape[0]
    row_count = dp * live
    mine = lax.axis_index("dp")
    start = (mine * stats.shape[1] + lax.axis_index("tensor")) * vocab_width

    normed = jnp.concatenate([piece[:, :depth] for piece in pieces], axis=0)
    logits = jnp.dot(normed[:, : depth // 2], first[...], preferred_element_type=jnp.float32)
    logits += jnp.dot(normed[:, depth // 2 :], second[...], preferred_element_type=jnp.float32)
    digits = jnp.concatenate([piece[:, depth:] for piece in pieces], axis=0).astype(jnp.float32)
    lane = lax.broadcasted_iota(jnp.int32, (row_count, CODE), 1)
    weight = jnp.where(lane == 0, 1.0, jnp.where(lane == 1, float(DIGIT), jnp.where(lane == 2, float(DIGIT * DIGIT), 0.0)))
    target = jnp.sum(digits * weight, axis=-1, keepdims=True).astype(jnp.int32) - start
    column = lax.broadcasted_iota(jnp.int32, (row_count, vocab_width), 1)
    top = jnp.max(logits, axis=-1, keepdims=True)
    expo = jnp.exp(logits - top)
    total = jnp.sum(expo, axis=-1, keepdims=True)
    weighted = jnp.sum(expo * logits, axis=-1, keepdims=True)
    chosen = jnp.sum(jnp.where(column == target, logits, 0.0), axis=-1, keepdims=True)
    spot = lane - lax.broadcasted_iota(jnp.int32, (row_count, CODE), 0) % live
    table = jnp.zeros((row_count, CODE), jnp.float32)
    for group, value in enumerate((top, total, weighted, chosen)):
        table = jnp.where(spot == GROUP * group, value, table)
    for i, d in enumerate(order):
        line = jnp.sum(table[i * live : (i + 1) * live], axis=0, keepdims=True)
        for t in range(stats.shape[1]):
            stats[mine ^ d, t] = line


def score(pieces, order, halves, copies):
    dp = len(order)
    vmem = pl.BlockSpec(memory_space=pltpu.VMEM)
    return pl.pallas_call(
        functools.partial(score_kernel, order),
        out_shape=jax.ShapeDtypeStruct((dp, copies, 1, CODE), jnp.float32),
        in_specs=[vmem] * (dp + 2),
        out_specs=vmem,
        compiler_params=vmem_limit(32),
        name="score",
    )(*[pieces[d] for d in order], *[pltpu.with_memory_space_constraint(half, pltpu.VMEM) for half in halves])


def combine(values):
    lane = lax.broadcasted_iota(jnp.int32, values.shape, 1)
    top = jnp.where(lane < GROUP, values, 0.0)
    top = top + pltpu.roll(top, GROUP, 1)
    top = top + pltpu.roll(top, 2 * GROUP, 1)
    best = jnp.max(top, axis=0, keepdims=True)
    factor = jnp.where(lane < 3 * GROUP, jnp.exp(top - best), 1.0)
    return jnp.sum(values * factor, axis=0, keepdims=True), best


def finish_kernel(stats, place, logprob, entropy):
    live = place.shape[0]
    slot_count = logprob.shape[1]
    sums, best = combine(stats[:, 0, :])
    line = jnp.broadcast_to(sums, (8, CODE))
    total = pltpu.roll(line, CODE - GROUP, 1)
    weighted = pltpu.roll(line, CODE - 2 * GROUP, 1)
    chosen = pltpu.roll(line, CODE - 3 * GROUP, 1)
    lse = best + jnp.log(total)
    kind = lax.broadcasted_iota(jnp.int32, (8, CODE), 0)
    merged = jnp.where(kind == 0, chosen - lse, lse - weighted / total)
    merged = jnp.where(lax.broadcasted_iota(jnp.int32, (8, CODE), 1) < GROUP, merged, 0.0)
    spread = jnp.concatenate([place[...], jnp.zeros((CODE - live, CODE), jnp.float32)], axis=0)
    out = jnp.dot(merged, spread, precision=lax.Precision.HIGHEST, preferred_element_type=jnp.float32)
    logprob[...] = out[0:1, :slot_count]
    entropy[...] = out[1:2, :slot_count]


def finish(stats, place, slot_count):
    vmem = pl.BlockSpec(memory_space=pltpu.VMEM)
    out = jax.ShapeDtypeStruct((1, slot_count), jnp.float32)
    return pl.pallas_call(
        finish_kernel,
        out_shape=(out, out),
        in_specs=[vmem, vmem],
        out_specs=(vmem, vmem),
        compiler_params=vmem_limit(32),
        name="finish",
    )(stats, place)


def swap(x, axis, distance):
    return lax.ppermute(x, axis, [(i, i ^ distance) for i in range(lax.axis_size(axis))])


def per_device(hidden, gain, head, lengths, offsets, targets, mask):
    dp, tensor = lax.axis_size("dp"), lax.axis_size("tensor")
    rows, codes, slots, gain = pick(hidden, gain, lengths, offsets, targets, mask)
    parts = [rows] + [swap(rows, "tensor", s) for s in range(1, tensor)]
    first, codes = fetch(head, 0, codes)
    rows = join(parts, codes, gain)

    pieces = {0: rows} | {d: swap(rows, "dp", d) for d in range(2, dp, 2)}
    pieces |= {d + 1: swap(pieces[d], "dp", 1) for d in range(0, dp, 2)}
    second, _ = fetch(head, 1, rows)
    order = list(range(dp))
    stats = score(pieces, order, (first, second), tensor)
    stats = lax.all_to_all(stats.reshape(dp * tensor, 1, CODE), ("dp", "tensor"), 0, 0, tiled=True)
    return finish(stats, slots, offsets.shape[1])


def solution(mesh):
    return jax.shard_map(
        per_device,
        mesh=mesh,
        in_specs=(
            P("dp", None, "tensor"),
            P(),
            P(None, ("dp", "tensor")),
            P("dp"),
            P("dp", None),
            P("dp", None),
            P("dp", None),
        ),
        out_specs=(P("dp", None), P("dp", None)),
        check_vma=False,
    )
```

```python
import functools

import jax
import jax.numpy as jnp
from jax import lax
from jax.experimental import pallas as pl
from jax.experimental.pallas import tpu as pltpu
from jax.sharding import PartitionSpec as P

LIVE = 16
SPAN = 256
BLOCK = 16
CODE = 128
DIGIT = 64
GROUP = 16


def vmem_limit(mebibytes):
    return pltpu.CompilerParams(vmem_limit_bytes=mebibytes * 1024 * 1024)


def in_hbm(x):
    return pltpu.with_memory_space_constraint(x, pltpu.HBM)


def pick_kernel(
    lengths, offsets, targets, mask, gain, hidden, rows, codes, place, gain_out, window, offset, target, alive, sems
):
    slot_count = offsets.shape[1]
    depth = window.shape[0]
    first = jnp.minimum((lengths[0] - SPAN) // BLOCK * BLOCK, hidden.shape[1] - depth)
    first = pl.multiple_of(first, BLOCK)
    copies = [
        pltpu.make_async_copy(offsets, offset, sems.at[0]),
        pltpu.make_async_copy(mask, alive, sems.at[1]),
        pltpu.make_async_copy(targets, target, sems.at[2]),
        pltpu.make_async_copy(gain, gain_out, sems.at[3]),
        pltpu.make_async_copy(hidden.at[0, pl.ds(first, depth)], window, sems.at[4]),
    ]
    for copy in copies:
        copy.start()
    for copy in copies[:2]:
        copy.wait()

    def iota(shape, axis):
        return lax.broadcasted_iota(jnp.int32, shape, axis)

    square = (slot_count, slot_count)
    live = jnp.where(alive[...] != 0, 1.0, 0.0)
    column = jnp.sum(jnp.where(iota(square, 0) == iota(square, 1), live, 0.0), axis=1, keepdims=True)
    rank = jnp.sum(jnp.where(iota(square, 0) < iota(square, 1), column, 0.0), axis=0, keepdims=True)
    wide = (LIVE, slot_count)
    chosen = jnp.where(iota(wide, 0).astype(jnp.float32) == rank, jnp.broadcast_to(live, wide), 0.0)
    place[...] = chosen
    offset_in = (lengths[0] - 1 - first) - offset[...]
    wanted = jnp.sum(chosen * (offset_in + 1).astype(jnp.float32), axis=1, keepdims=True) - 1.0
    select = jnp.where(iota((LIVE, depth), 1).astype(jnp.float32) == wanted, 1.0, 0.0).astype(jnp.bfloat16)
    copies[2].wait()
    ids = jnp.sum(chosen * target[...].astype(jnp.float32), axis=1, keepdims=True).astype(jnp.int32)
    lane = iota((LIVE, CODE), 1)
    digits = jnp.where(
        lane == 0, ids % DIGIT, jnp.where(lane == 1, (ids // DIGIT) % DIGIT, jnp.where(lane == 2, ids // (DIGIT * DIGIT), 0))
    )
    codes[...] = digits.astype(jnp.float32).astype(jnp.bfloat16)
    for copy in copies[3:]:
        copy.wait()
    rows[...] = jnp.dot(select, window[...], preferred_element_type=jnp.float32).astype(jnp.bfloat16)


def pick(hidden, gain, lengths, offsets, targets, mask):
    features = hidden.shape[2]
    slot_count = offsets.shape[1]
    vmem = pl.BlockSpec(memory_space=pltpu.VMEM)
    return pl.pallas_call(
        pick_kernel,
        out_shape=(
            jax.ShapeDtypeStruct((LIVE, features), jnp.bfloat16),
            jax.ShapeDtypeStruct((LIVE, CODE), jnp.bfloat16),
            jax.ShapeDtypeStruct((LIVE, slot_count), jnp.float32),
            jax.ShapeDtypeStruct((1, gain.shape[0]), jnp.float32),
        ),
        in_specs=[pl.BlockSpec(memory_space=pltpu.SMEM)] + [pl.BlockSpec(memory_space=pltpu.HBM)] * 5,
        out_specs=(vmem, vmem, vmem, vmem),
        scratch_shapes=[
            pltpu.VMEM((SPAN + BLOCK, features), jnp.bfloat16),
            pltpu.VMEM(offsets.shape, jnp.int32),
            pltpu.VMEM(offsets.shape, jnp.int32),
            pltpu.VMEM(offsets.shape, jnp.int32),
            pltpu.SemaphoreType.DMA((5,)),
        ],
        compiler_params=vmem_limit(32),
        name="pick",
    )(lengths, *map(in_hbm, (offsets, targets, mask, gain.reshape(1, -1), hidden)))


def join_kernel(tensor, *refs):
    pieces, (codes, gain, rows) = refs[:-3][::-1], refs[-3:]
    own, turned, paired = pieces[0], pieces[1 : tensor - 1], pieces[tensor - 1 :]
    live, features = own.shape
    shard = lax.axis_index("tensor")
    final = tensor - 1

    parts = [(shard, own[...].astype(jnp.float32))]
    for r, (around, pair) in enumerate(zip(turned, paired), 1):
        source = jnp.where(shard == final, r - 1, lax.rem(shard + final - r, final))
        parts.append((source, jnp.where(shard == final, pair[...], around[...]).astype(jnp.float32)))
    left = paired[final - 1][...]
    for i, pair in enumerate(paired[:-1]):
        left = jnp.where(shard == i, pair[...], left)
    parts.append((jnp.where(shard == final, final - 1, final), left.astype(jnp.float32)))

    square = sum(jnp.sum(values * values, axis=-1, keepdims=True) for _, values in parts)
    scale = lax.rsqrt(square / (tensor * features) + 1e-06)
    for source, values in parts:
        span = pl.ds(pl.multiple_of(source * features, features), features)
        rows[:, span] = (values * scale * gain[:, span]).astype(jnp.bfloat16)
    rows[:, tensor * features :] = codes[...]


def join(pieces, tensor, codes, gain):
    live, features = pieces[0].shape
    vmem = pl.BlockSpec(memory_space=pltpu.VMEM)
    return pl.pallas_call(
        functools.partial(join_kernel, tensor),
        out_shape=jax.ShapeDtypeStruct((live, tensor * features + CODE), jnp.bfloat16),
        in_specs=[vmem] * (len(pieces) + 2),
        out_specs=vmem,
        compiler_params=vmem_limit(32),
        name="join",
    )(*reversed(pieces), codes, gain)


def fetch_kernel(head, after, held, after_out, sems):
    count = sems.shape[0]
    depth = held.shape[0] // count
    copies = [
        pltpu.make_async_copy(head.at[pl.ds(i * depth, depth)], held.at[pl.ds(i * depth, depth)], sems.at[i])
        for i in range(count)
    ]
    for copy in copies:
        copy.start()
    after_out[...] = after[...]
    for copy in copies:
        copy.wait()


def fetch(head, after):
    vmem = pl.BlockSpec(memory_space=pltpu.VMEM)
    return pl.pallas_call(
        fetch_kernel,
        out_shape=(pltpu.VMEM(head.shape, head.dtype), jax.ShapeDtypeStruct(after.shape, after.dtype)),
        in_specs=[pl.BlockSpec(memory_space=pltpu.HBM), vmem],
        out_specs=(vmem, vmem),
        scratch_shapes=[pltpu.SemaphoreType.DMA((4,))],
        compiler_params=vmem_limit(32),
        cost_estimate=pl.CostEstimate(flops=0, bytes_accessed=4 * head.size, transcendentals=0),
        name="fetch",
    )(in_hbm(head), after)


def score_kernel(order, *refs):
    dp = len(order)
    pieces, (head, stats) = refs[:dp], refs[dp:]
    depth, vocab_width = head.shape
    live = pieces[0].shape[0]
    row_count = dp * live
    mine = lax.axis_index("dp")
    start = (mine * stats.shape[1] + lax.axis_index("tensor")) * vocab_width

    normed = jnp.concatenate([piece[:, :depth] for piece in pieces], axis=0)
    logits = jnp.dot(normed, head[...], preferred_element_type=jnp.float32)
    digits = jnp.concatenate([piece[:, depth:] for piece in pieces], axis=0).astype(jnp.float32)
    lane = lax.broadcasted_iota(jnp.int32, (row_count, CODE), 1)
    weight = jnp.where(lane == 0, 1.0, jnp.where(lane == 1, float(DIGIT), jnp.where(lane == 2, float(DIGIT * DIGIT), 0.0)))
    target = jnp.sum(digits * weight, axis=-1, keepdims=True).astype(jnp.int32) - start
    column = lax.broadcasted_iota(jnp.int32, (row_count, vocab_width), 1)
    top = jnp.max(logits, axis=-1, keepdims=True)
    expo = jnp.exp(logits - top)
    total = jnp.sum(expo, axis=-1, keepdims=True)
    weighted = jnp.sum(expo * logits, axis=-1, keepdims=True)
    chosen = jnp.sum(jnp.where(column == target, logits, 0.0), axis=-1, keepdims=True)
    spot = lane - lax.broadcasted_iota(jnp.int32, (row_count, CODE), 0) % live
    table = jnp.zeros((row_count, CODE), jnp.float32)
    for group, value in enumerate((top, total, weighted, chosen)):
        table = jnp.where(spot == GROUP * group, value, table)
    for i, d in enumerate(order):
        line = jnp.sum(table[i * live : (i + 1) * live], axis=0, keepdims=True)
        for t in range(stats.shape[1]):
            stats[mine ^ d, t] = line


def score(pieces, order, head, copies):
    dp = len(order)
    vmem = pl.BlockSpec(memory_space=pltpu.VMEM)
    return pl.pallas_call(
        functools.partial(score_kernel, order),
        out_shape=jax.ShapeDtypeStruct((dp, copies, 1, CODE), jnp.float32),
        in_specs=[vmem] * (dp + 1),
        out_specs=vmem,
        compiler_params=vmem_limit(32),
        name="score",
    )(*[pieces[d] for d in order], pltpu.with_memory_space_constraint(head, pltpu.VMEM))


def combine(values):
    lane = lax.broadcasted_iota(jnp.int32, values.shape, 1)
    top = jnp.where(lane < GROUP, values, 0.0)
    top = top + pltpu.roll(top, GROUP, 1)
    top = top + pltpu.roll(top, 2 * GROUP, 1)
    best = jnp.max(top, axis=0, keepdims=True)
    factor = jnp.where(lane < 3 * GROUP, jnp.exp(top - best), 1.0)
    return jnp.sum(values * factor, axis=0, keepdims=True), best


def finish_kernel(stats, place, logprob, entropy):
    live = place.shape[0]
    slot_count = logprob.shape[1]
    sums, best = combine(stats[:, 0, :])
    line = jnp.broadcast_to(sums, (8, CODE))
    total = pltpu.roll(line, CODE - GROUP, 1)
    weighted = pltpu.roll(line, CODE - 2 * GROUP, 1)
    chosen = pltpu.roll(line, CODE - 3 * GROUP, 1)
    lse = best + jnp.log(total)
    kind = lax.broadcasted_iota(jnp.int32, (8, CODE), 0)
    merged = jnp.where(kind == 0, chosen - lse, lse - weighted / total)
    merged = jnp.where(lax.broadcasted_iota(jnp.int32, (8, CODE), 1) < GROUP, merged, 0.0)
    spread = jnp.concatenate([place[...], jnp.zeros((CODE - live, slot_count), jnp.float32)], axis=0)
    out = jnp.dot(merged, spread, precision=lax.Precision.HIGHEST, preferred_element_type=jnp.float32)
    logprob[...] = out[0:1]
    entropy[...] = out[1:2]


def finish(stats, place, slot_count):
    vmem = pl.BlockSpec(memory_space=pltpu.VMEM)
    out = jax.ShapeDtypeStruct((1, slot_count), jnp.float32)
    return pl.pallas_call(
        finish_kernel,
        out_shape=(out, out),
        in_specs=[vmem, vmem],
        out_specs=(vmem, vmem),
        compiler_params=vmem_limit(32),
        name="finish",
    )(stats, place)


def swap(x, axis, distance):
    return lax.ppermute(x, axis, [(i, i ^ distance) for i in range(lax.axis_size(axis))])


def per_device(hidden, gain, head, lengths, offsets, targets, mask):
    dp, tensor = lax.axis_size("dp"), lax.axis_size("tensor")
    rows, codes, slots, gain = pick(hidden, gain, lengths, offsets, targets, mask)
    final = tensor - 1
    pieces = [rows]
    for r in range(1, final):
        pieces.append(lax.ppermute(rows, "tensor", [(i, (i + r) % final) for i in range(final)]))
    for i in range(final):
        pieces.append(lax.ppermute(rows, "tensor", [(i, final), (final, i)]))
    held, codes = fetch(head, codes)
    rows = join(pieces, tensor, codes, gain)

    pieces = {0: rows} | {d: swap(rows, "dp", d) for d in range(2, dp, 2)}
    pieces |= {d + 1: swap(pieces[d], "dp", 1) for d in range(0, dp, 2)}
    order = [0, 1] + [d + core for d in reversed(range(2, dp, 2)) for core in (0, 1)]
    stats = score(pieces, order, held, tensor)
    stats = lax.all_to_all(stats.reshape(dp * tensor, 1, CODE), ("dp", "tensor"), 0, 0, tiled=True)
    return finish(stats, slots, offsets.shape[1])


def solution(mesh):
    return jax.shard_map(
        per_device,
        mesh=mesh,
        in_specs=(
            P("dp", None, "tensor"),
            P(),
            P(None, ("dp", "tensor")),
            P("dp"),
            P("dp", None),
            P("dp", None),
            P("dp", None),
        ),
        out_specs=(P("dp", None), P("dp", None)),
        check_vma=False,
    )
```

```python
import functools

import jax
import jax.numpy as jnp
from jax import lax
from jax.experimental import pallas as pl
from jax.experimental.pallas import tpu as pltpu
from jax.sharding import PartitionSpec as P

LIVE = 16
SPAN = 256
BLOCK = 16
CODE = 128
DIGIT = 64
GROUP = 16


def vmem_limit(mebibytes):
    return pltpu.CompilerParams(vmem_limit_bytes=mebibytes * 1024 * 1024)


def in_hbm(x):
    return pltpu.with_memory_space_constraint(x, pltpu.HBM)


def pick_kernel(
    lengths, offsets, targets, mask, gain, hidden, rows, codes, place, gain_out, window, offset, target, alive, sems
):
    slot_count = offsets.shape[1]
    depth = window.shape[0]
    first = jnp.minimum((lengths[0] - SPAN) // BLOCK * BLOCK, hidden.shape[1] - depth)
    first = pl.multiple_of(first, BLOCK)
    copies = [
        pltpu.make_async_copy(offsets, offset, sems.at[0]),
        pltpu.make_async_copy(mask, alive, sems.at[1]),
        pltpu.make_async_copy(targets, target, sems.at[2]),
        pltpu.make_async_copy(gain, gain_out, sems.at[3]),
        pltpu.make_async_copy(hidden.at[0, pl.ds(first, depth)], window, sems.at[4]),
    ]
    for copy in copies:
        copy.start()
    for copy in copies[:2]:
        copy.wait()

    def iota(shape, axis):
        return lax.broadcasted_iota(jnp.int32, shape, axis)

    square = (slot_count, slot_count)
    live = jnp.where(alive[...] != 0, 1.0, 0.0)
    column = jnp.sum(jnp.where(iota(square, 0) == iota(square, 1), live, 0.0), axis=1, keepdims=True)
    rank = jnp.sum(jnp.where(iota(square, 0) < iota(square, 1), column, 0.0), axis=0, keepdims=True)
    wide = (LIVE, slot_count)
    chosen = jnp.where(iota(wide, 0).astype(jnp.float32) == rank, jnp.broadcast_to(live, wide), 0.0)
    place[...] = chosen
    offset_in = (lengths[0] - 1 - first) - offset[...]
    wanted = jnp.sum(chosen * (offset_in + 1).astype(jnp.float32), axis=1, keepdims=True) - 1.0
    select = jnp.where(iota((LIVE, depth), 1).astype(jnp.float32) == wanted, 1.0, 0.0).astype(jnp.bfloat16)
    copies[2].wait()
    ids = jnp.sum(chosen * target[...].astype(jnp.float32), axis=1, keepdims=True).astype(jnp.int32)
    lane = iota((LIVE, CODE), 1)
    digits = jnp.where(
        lane == 0, ids % DIGIT, jnp.where(lane == 1, (ids // DIGIT) % DIGIT, jnp.where(lane == 2, ids // (DIGIT * DIGIT), 0))
    )
    codes[...] = digits.astype(jnp.float32).astype(jnp.bfloat16)
    for copy in copies[3:]:
        copy.wait()
    rows[...] = jnp.dot(select, window[...], preferred_element_type=jnp.float32).astype(jnp.bfloat16)


def pick(hidden, gain, lengths, offsets, targets, mask):
    features = hidden.shape[2]
    slot_count = offsets.shape[1]
    vmem = pl.BlockSpec(memory_space=pltpu.VMEM)
    return pl.pallas_call(
        pick_kernel,
        out_shape=(
            jax.ShapeDtypeStruct((LIVE, features), jnp.bfloat16),
            jax.ShapeDtypeStruct((LIVE, CODE), jnp.bfloat16),
            jax.ShapeDtypeStruct((LIVE, slot_count), jnp.float32),
            jax.ShapeDtypeStruct((1, gain.shape[0]), jnp.float32),
        ),
        in_specs=[pl.BlockSpec(memory_space=pltpu.SMEM)] + [pl.BlockSpec(memory_space=pltpu.HBM)] * 5,
        out_specs=(vmem, vmem, vmem, vmem),
        scratch_shapes=[
            pltpu.VMEM((SPAN + BLOCK, features), jnp.bfloat16),
            pltpu.VMEM(offsets.shape, jnp.int32),
            pltpu.VMEM(offsets.shape, jnp.int32),
            pltpu.VMEM(offsets.shape, jnp.int32),
            pltpu.SemaphoreType.DMA((5,)),
        ],
        compiler_params=vmem_limit(32),
        name="pick",
    )(lengths, *map(in_hbm, (offsets, targets, mask, gain.reshape(1, -1), hidden)))


def join_kernel(*refs):
    tensor = len(refs) - 3
    parts, (codes, gain, rows) = refs[:tensor], refs[tensor:]
    live, features = parts[0].shape
    square = jnp.zeros((live, 1), jnp.float32)
    for part in parts:
        values = part[...].astype(jnp.float32)
        square += jnp.sum(values * values, axis=-1, keepdims=True)
    scale = lax.rsqrt(square / (tensor * features) + 1e-06)
    shard = lax.axis_index("tensor")
    for s, part in enumerate(parts):
        span = pl.ds(pl.multiple_of((shard ^ s) * features, features), features)
        rows[:, span] = (part[...].astype(jnp.float32) * scale * gain[:, span]).astype(jnp.bfloat16)
    rows[:, tensor * features :] = codes[...]


def join(parts, codes, gain):
    tensor = len(parts)
    live, features = parts[0].shape
    vmem = pl.BlockSpec(memory_space=pltpu.VMEM)
    return pl.pallas_call(
        join_kernel,
        out_shape=jax.ShapeDtypeStruct((live, tensor * features + CODE), jnp.bfloat16),
        in_specs=[vmem] * (tensor + 2),
        out_specs=vmem,
        compiler_params=vmem_limit(32),
        name="join",
    )(*parts, codes, gain)


def fetch_kernel(head, rows, held, rows_out, sems):
    count = sems.shape[0]
    depth = head.shape[0] // count
    copies = [
        pltpu.make_async_copy(head.at[pl.ds(i * depth, depth)], held.at[pl.ds(i * depth, depth)], sems.at[i])
        for i in range(count)
    ]
    for copy in copies:
        copy.start()
    rows_out[...] = rows[...]
    for copy in copies:
        copy.wait()


def fetch(head, rows):
    vmem = pl.BlockSpec(memory_space=pltpu.VMEM)
    return pl.pallas_call(
        fetch_kernel,
        out_shape=(pltpu.VMEM(head.shape, head.dtype), jax.ShapeDtypeStruct(rows.shape, rows.dtype)),
        in_specs=[pl.BlockSpec(memory_space=pltpu.HBM), vmem],
        out_specs=(vmem, vmem),
        scratch_shapes=[pltpu.SemaphoreType.DMA((4,))],
        compiler_params=vmem_limit(32),
        cost_estimate=pl.CostEstimate(flops=0, bytes_accessed=2 * head.size * 2, transcendentals=0),
        name="fetch",
    )(in_hbm(head), rows)


def score_kernel(*refs):
    dp = len(refs) - 2
    pieces, (head, stats) = refs[:dp], refs[dp:]
    depth, vocab_width = head.shape
    live = pieces[0].shape[0]
    row_count = dp * live
    mine = lax.axis_index("dp")
    start = (mine * stats.shape[1] + lax.axis_index("tensor")) * vocab_width

    normed = jnp.concatenate([piece[:, :depth] for piece in pieces], axis=0)
    logits = jnp.dot(normed, head[...], preferred_element_type=jnp.float32)
    digits = jnp.concatenate([piece[:, depth:] for piece in pieces], axis=0).astype(jnp.float32)
    lane = lax.broadcasted_iota(jnp.int32, (row_count, CODE), 1)
    weight = jnp.where(lane == 0, 1.0, jnp.where(lane == 1, float(DIGIT), jnp.where(lane == 2, float(DIGIT * DIGIT), 0.0)))
    target = jnp.sum(digits * weight, axis=-1, keepdims=True).astype(jnp.int32) - start
    column = lax.broadcasted_iota(jnp.int32, (row_count, vocab_width), 1)
    top = jnp.max(logits, axis=-1, keepdims=True)
    expo = jnp.exp(logits - top)
    total = jnp.sum(expo, axis=-1, keepdims=True)
    weighted = jnp.sum(expo * logits, axis=-1, keepdims=True)
    chosen = jnp.sum(jnp.where(column == target, logits, 0.0), axis=-1, keepdims=True)
    spot = lane - lax.broadcasted_iota(jnp.int32, (row_count, CODE), 0) % live
    table = jnp.zeros((row_count, CODE), jnp.float32)
    for group, value in enumerate((top, total, weighted, chosen)):
        table = jnp.where(spot == GROUP * group, value, table)
    for d in range(dp):
        line = jnp.sum(table[d * live : (d + 1) * live], axis=0, keepdims=True)
        for t in range(stats.shape[1]):
            stats[mine ^ d, t] = line


def score(pieces, head, copies):
    dp = len(pieces)
    live, width = pieces[0].shape
    vmem = pl.BlockSpec(memory_space=pltpu.VMEM)
    return pl.pallas_call(
        score_kernel,
        out_shape=jax.ShapeDtypeStruct((dp, copies, 1, CODE), jnp.float32),
        in_specs=[vmem] * (dp + 1),
        out_specs=vmem,
        compiler_params=vmem_limit(32),
        name="score",
    )(*pieces, pltpu.with_memory_space_constraint(head, pltpu.VMEM))


def combine(values):
    lane = lax.broadcasted_iota(jnp.int32, values.shape, 1)
    top = jnp.where(lane < GROUP, values, 0.0)
    top = top + pltpu.roll(top, GROUP, 1)
    top = top + pltpu.roll(top, 2 * GROUP, 1)
    best = jnp.max(top, axis=0, keepdims=True)
    factor = jnp.where(lane < 3 * GROUP, jnp.exp(top - best), 1.0)
    return jnp.sum(values * factor, axis=0, keepdims=True), best


def finish_kernel(stats, place, logprob, entropy, scored, spread, sems):
    sums, best = combine(stats[:, 0, :])
    total = pltpu.roll(sums, CODE - GROUP, 1)
    weighted = pltpu.roll(sums, CODE - 2 * GROUP, 1)
    chosen = pltpu.roll(sums, CODE - 3 * GROUP, 1)
    lse = best + jnp.log(total)
    lane = lax.broadcasted_iota(jnp.int32, (LIVE, CODE), 1)
    row = lax.broadcasted_iota(jnp.int32, (LIVE, CODE), 0)

    def to_slots(values):
        column = jnp.sum(jnp.where(lane == row, values, 0.0), axis=1, keepdims=True)
        return jnp.sum(place[...] * column, axis=0, keepdims=True)

    scored[...] = to_slots(chosen - lse)
    first = pltpu.make_async_copy(scored, logprob, sems.at[0])
    first.start()
    spread[...] = to_slots(lse - weighted / total)
    second = pltpu.make_async_copy(spread, entropy, sems.at[1])
    second.start()
    first.wait()
    second.wait()


def finish(stats, place, slot_count):
    vmem = pl.BlockSpec(memory_space=pltpu.VMEM)
    out = jax.ShapeDtypeStruct((1, slot_count), jnp.float32)
    return pl.pallas_call(
        finish_kernel,
        out_shape=(out, out),
        in_specs=[vmem, vmem],
        out_specs=[pl.BlockSpec(memory_space=pltpu.HBM)] * 2,
        scratch_shapes=[
            pltpu.VMEM((1, slot_count), jnp.float32),
            pltpu.VMEM((1, slot_count), jnp.float32),
            pltpu.SemaphoreType.DMA((2,)),
        ],
        compiler_params=vmem_limit(32),
        name="finish",
    )(stats, place)


def swap(x, axis, distance):
    return lax.ppermute(x, axis, [(i, i ^ distance) for i in range(lax.axis_size(axis))])


def per_device(hidden, gain, head, lengths, offsets, targets, mask):
    dp, tensor = lax.axis_size("dp"), lax.axis_size("tensor")
    rows, codes, slots, gain = pick(hidden, gain, lengths, offsets, targets, mask)
    parts = {0: rows} | {s: swap(rows, "tensor", s) for s in reversed(range(1, tensor))}
    rows = join([parts[s] for s in range(tensor)], codes, gain)

    pieces = {d: swap(rows, "dp", d) for d in reversed(range(2, dp, 2))}
    held, pieces[0] = fetch(head, rows)
    for d in range(0, dp, 2):
        pieces[d + 1] = swap(pieces[d], "dp", 1)
    stats = score([pieces[d] for d in range(dp)], held, tensor)
    stats = lax.all_to_all(stats.reshape(dp * tensor, 1, CODE), ("dp", "tensor"), 0, 0, tiled=True)
    return finish(stats, slots, offsets.shape[1])


def solution(mesh):
    return jax.shard_map(
        per_device,
        mesh=mesh,
        in_specs=(
            P("dp", None, "tensor"),
            P(),
            P(None, ("dp", "tensor")),
            P("dp"),
            P("dp", None),
            P("dp", None),
            P("dp", None),
        ),
        out_specs=(P("dp", None), P("dp", None)),
        check_vma=False,
    )
```

```python
import functools

import jax
import jax.numpy as jnp
from jax import lax
from jax.experimental import pallas as pl
from jax.experimental.pallas import tpu as pltpu
from jax.sharding import PartitionSpec as P

LIVE = 16
SPAN = 256
BLOCK = 16
CODE = 128
DIGIT = 64
GROUP = 16


def vmem_limit(mebibytes):
    return pltpu.CompilerParams(vmem_limit_bytes=mebibytes * 1024 * 1024)


def in_hbm(x):
    return pltpu.with_memory_space_constraint(x, pltpu.HBM)


def pick_kernel(
    lengths, offsets, targets, mask, gain, hidden, rows, codes, place, gain_out, window, offset, target, alive, sems
):
    slot_count = offsets.shape[1]
    depth = window.shape[0]
    first = jnp.minimum((lengths[0] - SPAN) // BLOCK * BLOCK, hidden.shape[1] - depth)
    first = pl.multiple_of(first, BLOCK)
    copies = [
        pltpu.make_async_copy(offsets, offset, sems.at[0]),
        pltpu.make_async_copy(mask, alive, sems.at[1]),
        pltpu.make_async_copy(targets, target, sems.at[2]),
        pltpu.make_async_copy(gain, gain_out, sems.at[3]),
        pltpu.make_async_copy(hidden.at[0, pl.ds(first, depth)], window, sems.at[4]),
    ]
    for copy in copies:
        copy.start()
    for copy in copies[:2]:
        copy.wait()

    def iota(shape, axis):
        return lax.broadcasted_iota(jnp.int32, shape, axis)

    square = (slot_count, slot_count)
    live = jnp.where(alive[...] != 0, 1.0, 0.0)
    column = jnp.sum(jnp.where(iota(square, 0) == iota(square, 1), live, 0.0), axis=1, keepdims=True)
    rank = jnp.sum(jnp.where(iota(square, 0) < iota(square, 1), column, 0.0), axis=0, keepdims=True)
    wide = (LIVE, slot_count)
    chosen = jnp.where(iota(wide, 0).astype(jnp.float32) == rank, jnp.broadcast_to(live, wide), 0.0)
    place[...] = chosen
    offset_in = (lengths[0] - 1 - first) - offset[...]
    wanted = jnp.sum(chosen * (offset_in + 1).astype(jnp.float32), axis=1, keepdims=True) - 1.0
    select = jnp.where(iota((LIVE, depth), 1).astype(jnp.float32) == wanted, 1.0, 0.0).astype(jnp.bfloat16)
    copies[2].wait()
    ids = jnp.sum(chosen * target[...].astype(jnp.float32), axis=1, keepdims=True).astype(jnp.int32)
    lane = iota((LIVE, CODE), 1)
    digits = jnp.where(
        lane == 0, ids % DIGIT, jnp.where(lane == 1, (ids // DIGIT) % DIGIT, jnp.where(lane == 2, ids // (DIGIT * DIGIT), 0))
    )
    codes[...] = digits.astype(jnp.float32).astype(jnp.bfloat16)
    for copy in copies[3:]:
        copy.wait()
    rows[...] = jnp.dot(select, window[...], preferred_element_type=jnp.float32).astype(jnp.bfloat16)


def pick(hidden, gain, lengths, offsets, targets, mask):
    features = hidden.shape[2]
    slot_count = offsets.shape[1]
    vmem = pl.BlockSpec(memory_space=pltpu.VMEM)
    return pl.pallas_call(
        pick_kernel,
        out_shape=(
            jax.ShapeDtypeStruct((LIVE, features), jnp.bfloat16),
            jax.ShapeDtypeStruct((LIVE, CODE), jnp.bfloat16),
            jax.ShapeDtypeStruct((LIVE, slot_count), jnp.float32),
            jax.ShapeDtypeStruct((1, gain.shape[0]), jnp.float32),
        ),
        in_specs=[pl.BlockSpec(memory_space=pltpu.SMEM)] + [pl.BlockSpec(memory_space=pltpu.HBM)] * 5,
        out_specs=(vmem, vmem, vmem, vmem),
        scratch_shapes=[
            pltpu.VMEM((SPAN + BLOCK, features), jnp.bfloat16),
            pltpu.VMEM(offsets.shape, jnp.int32),
            pltpu.VMEM(offsets.shape, jnp.int32),
            pltpu.VMEM(offsets.shape, jnp.int32),
            pltpu.SemaphoreType.DMA((5,)),
        ],
        compiler_params=vmem_limit(32),
        name="pick",
    )(lengths, *map(in_hbm, (offsets, targets, mask, gain.reshape(1, -1), hidden)))


def join_kernel(tensor, *refs):
    pieces, (codes, gain, rows) = refs[:-3][::-1], refs[-3:]
    own, turned, paired = pieces[0], pieces[1 : tensor - 1], pieces[tensor - 1 :]
    live, features = own.shape
    shard = lax.axis_index("tensor")
    final = tensor - 1

    parts = [(shard, own[...].astype(jnp.float32))]
    for r, (around, pair) in enumerate(zip(turned, paired), 1):
        source = jnp.where(shard == final, r - 1, lax.rem(shard + final - r, final))
        parts.append((source, jnp.where(shard == final, pair[...], around[...]).astype(jnp.float32)))
    left = paired[final - 1][...]
    for i, pair in enumerate(paired[:-1]):
        left = jnp.where(shard == i, pair[...], left)
    parts.append((jnp.where(shard == final, final - 1, final), left.astype(jnp.float32)))

    square = sum(jnp.sum(values * values, axis=-1, keepdims=True) for _, values in parts)
    scale = lax.rsqrt(square / (tensor * features) + 1e-06)
    for source, values in parts:
        span = pl.ds(pl.multiple_of(source * features, features), features)
        rows[:, span] = (values * scale * gain[:, span]).astype(jnp.bfloat16)
    rows[:, tensor * features :] = codes[...]


def join(pieces, tensor, codes, gain):
    live, features = pieces[0].shape
    vmem = pl.BlockSpec(memory_space=pltpu.VMEM)
    return pl.pallas_call(
        functools.partial(join_kernel, tensor),
        out_shape=jax.ShapeDtypeStruct((live, tensor * features + CODE), jnp.bfloat16),
        in_specs=[vmem] * (len(pieces) + 2),
        out_specs=vmem,
        compiler_params=vmem_limit(32),
        name="join",
    )(*reversed(pieces), codes, gain)


def fetch_kernel(head, rows, held, rows_out, sems):
    count = sems.shape[0]
    depth = head.shape[0] // count
    copies = [
        pltpu.make_async_copy(head.at[pl.ds(i * depth, depth)], held.at[pl.ds(i * depth, depth)], sems.at[i])
        for i in range(count)
    ]
    for copy in copies:
        copy.start()
    rows_out[...] = rows[...]
    for copy in copies:
        copy.wait()


def fetch(head, rows):
    vmem = pl.BlockSpec(memory_space=pltpu.VMEM)
    return pl.pallas_call(
        fetch_kernel,
        out_shape=(pltpu.VMEM(head.shape, head.dtype), jax.ShapeDtypeStruct(rows.shape, rows.dtype)),
        in_specs=[pl.BlockSpec(memory_space=pltpu.HBM), vmem],
        out_specs=(vmem, vmem),
        scratch_shapes=[pltpu.SemaphoreType.DMA((4,))],
        compiler_params=vmem_limit(32),
        cost_estimate=pl.CostEstimate(flops=0, bytes_accessed=2 * head.size * 2, transcendentals=0),
        name="fetch",
    )(in_hbm(head), rows)


def score_kernel(*refs):
    dp = len(refs) - 2
    pieces, (head, stats) = refs[:dp], refs[dp:]
    depth, vocab_width = head.shape
    live = pieces[0].shape[0]
    row_count = dp * live
    mine = lax.axis_index("dp")
    start = (mine * stats.shape[1] + lax.axis_index("tensor")) * vocab_width

    normed = jnp.concatenate([piece[:, :depth] for piece in pieces], axis=0)
    logits = jnp.dot(normed, head[...], preferred_element_type=jnp.float32)
    digits = jnp.concatenate([piece[:, depth:] for piece in pieces], axis=0).astype(jnp.float32)
    lane = lax.broadcasted_iota(jnp.int32, (row_count, CODE), 1)
    weight = jnp.where(lane == 0, 1.0, jnp.where(lane == 1, float(DIGIT), jnp.where(lane == 2, float(DIGIT * DIGIT), 0.0)))
    target = jnp.sum(digits * weight, axis=-1, keepdims=True).astype(jnp.int32) - start
    column = lax.broadcasted_iota(jnp.int32, (row_count, vocab_width), 1)
    top = jnp.max(logits, axis=-1, keepdims=True)
    expo = jnp.exp(logits - top)
    total = jnp.sum(expo, axis=-1, keepdims=True)
    weighted = jnp.sum(expo * logits, axis=-1, keepdims=True)
    chosen = jnp.sum(jnp.where(column == target, logits, 0.0), axis=-1, keepdims=True)
    spot = lane - lax.broadcasted_iota(jnp.int32, (row_count, CODE), 0) % live
    table = jnp.zeros((row_count, CODE), jnp.float32)
    for group, value in enumerate((top, total, weighted, chosen)):
        table = jnp.where(spot == GROUP * group, value, table)
    for d in range(dp):
        line = jnp.sum(table[d * live : (d + 1) * live], axis=0, keepdims=True)
        for t in range(stats.shape[1]):
            stats[mine ^ d, t] = line


def score(pieces, head, copies):
    dp = len(pieces)
    live, width = pieces[0].shape
    vmem = pl.BlockSpec(memory_space=pltpu.VMEM)
    return pl.pallas_call(
        score_kernel,
        out_shape=jax.ShapeDtypeStruct((dp, copies, 1, CODE), jnp.float32),
        in_specs=[vmem] * (dp + 1),
        out_specs=vmem,
        compiler_params=vmem_limit(32),
        name="score",
    )(*pieces, pltpu.with_memory_space_constraint(head, pltpu.VMEM))


def combine(values):
    lane = lax.broadcasted_iota(jnp.int32, values.shape, 1)
    top = jnp.where(lane < GROUP, values, 0.0)
    top = top + pltpu.roll(top, GROUP, 1)
    top = top + pltpu.roll(top, 2 * GROUP, 1)
    best = jnp.max(top, axis=0, keepdims=True)
    factor = jnp.where(lane < 3 * GROUP, jnp.exp(top - best), 1.0)
    return jnp.sum(values * factor, axis=0, keepdims=True), best


def finish_kernel(stats, place, logprob, entropy, scored, spread, sems):
    sums, best = combine(stats[:, 0, :])
    total = pltpu.roll(sums, CODE - GROUP, 1)
    weighted = pltpu.roll(sums, CODE - 2 * GROUP, 1)
    chosen = pltpu.roll(sums, CODE - 3 * GROUP, 1)
    lse = best + jnp.log(total)
    lane = lax.broadcasted_iota(jnp.int32, (LIVE, CODE), 1)
    row = lax.broadcasted_iota(jnp.int32, (LIVE, CODE), 0)

    def to_slots(values):
        column = jnp.sum(jnp.where(lane == row, values, 0.0), axis=1, keepdims=True)
        return jnp.sum(place[...] * column, axis=0, keepdims=True)

    scored[...] = to_slots(chosen - lse)
    first = pltpu.make_async_copy(scored, logprob, sems.at[0])
    first.start()
    spread[...] = to_slots(lse - weighted / total)
    second = pltpu.make_async_copy(spread, entropy, sems.at[1])
    second.start()
    first.wait()
    second.wait()


def finish(stats, place, slot_count):
    vmem = pl.BlockSpec(memory_space=pltpu.VMEM)
    out = jax.ShapeDtypeStruct((1, slot_count), jnp.float32)
    return pl.pallas_call(
        finish_kernel,
        out_shape=(out, out),
        in_specs=[vmem, vmem],
        out_specs=[pl.BlockSpec(memory_space=pltpu.HBM)] * 2,
        scratch_shapes=[
            pltpu.VMEM((1, slot_count), jnp.float32),
            pltpu.VMEM((1, slot_count), jnp.float32),
            pltpu.SemaphoreType.DMA((2,)),
        ],
        compiler_params=vmem_limit(32),
        name="finish",
    )(stats, place)


def swap(x, axis, distance):
    return lax.ppermute(x, axis, [(i, i ^ distance) for i in range(lax.axis_size(axis))])


def per_device(hidden, gain, head, lengths, offsets, targets, mask):
    dp, tensor = lax.axis_size("dp"), lax.axis_size("tensor")
    rows, codes, slots, gain = pick(hidden, gain, lengths, offsets, targets, mask)
    final = tensor - 1
    pairs = [[(i, (i + r) % final) for i in range(final)] + [(final, final)] for r in range(1, final)]
    pairs += [[(i, final), (final, i)] + [(j, j) for j in range(final) if j != i] for i in range(final)]
    rows = join([rows] + [lax.ppermute(rows, "tensor", pair) for pair in pairs], tensor, codes, gain)

    pieces = {d: swap(rows, "dp", d) for d in reversed(range(2, dp, 2))}
    held, pieces[0] = fetch(head, rows)
    for d in range(0, dp, 2):
        pieces[d + 1] = swap(pieces[d], "dp", 1)
    stats = score([pieces[d] for d in range(dp)], held, tensor)
    stats = lax.all_to_all(stats.reshape(dp * tensor, 1, CODE), ("dp", "tensor"), 0, 0, tiled=True)
    return finish(stats, slots, offsets.shape[1])


def solution(mesh):
    return jax.shard_map(
        per_device,
        mesh=mesh,
        in_specs=(
            P("dp", None, "tensor"),
            P(),
            P(None, ("dp", "tensor")),
            P("dp"),
            P("dp", None),
            P("dp", None),
            P("dp", None),
        ),
        out_specs=(P("dp", None), P("dp", None)),
        check_vma=False,
    )
```

```python
import functools

import jax
import jax.numpy as jnp
from jax import lax
from jax.experimental import pallas as pl
from jax.experimental.pallas import tpu as pltpu
from jax.sharding import PartitionSpec as P

LIVE = 16
SPAN = 256
BLOCK = 16
CODE = 128
DIGIT = 64
GROUP = 16
CHUNK = 1024


def vmem_limit(mebibytes):
    return pltpu.CompilerParams(vmem_limit_bytes=mebibytes * 1024 * 1024)


def in_hbm(x):
    return pltpu.with_memory_space_constraint(x, pltpu.HBM)


def pick_kernel(
    lengths, offsets, targets, mask, gain, hidden, rows, codes, place, gain_out, window, offset, target, alive, sems
):
    slot_count = offsets.shape[1]
    depth = window.shape[0]
    first = jnp.minimum((lengths[0] - SPAN) // BLOCK * BLOCK, hidden.shape[1] - depth)
    first = pl.multiple_of(first, BLOCK)
    copies = [
        pltpu.make_async_copy(offsets, offset, sems.at[0]),
        pltpu.make_async_copy(mask, alive, sems.at[1]),
        pltpu.make_async_copy(hidden.at[0, pl.ds(first, depth)], window, sems.at[2]),
        pltpu.make_async_copy(targets, target, sems.at[3]),
        pltpu.make_async_copy(gain, gain_out, sems.at[4]),
    ]
    for copy in copies:
        copy.start()
    for copy in copies[:2]:
        copy.wait()

    def iota(shape, axis):
        return lax.broadcasted_iota(jnp.int32, shape, axis)

    square = (slot_count, slot_count)
    live = jnp.where(alive[...] != 0, 1.0, 0.0)
    column = jnp.sum(jnp.where(iota(square, 0) == iota(square, 1), live, 0.0), axis=1, keepdims=True)
    rank = jnp.sum(jnp.where(iota(square, 0) < iota(square, 1), column, 0.0), axis=0, keepdims=True)
    wide = (LIVE, slot_count)
    chosen = jnp.where(iota(wide, 0).astype(jnp.float32) == rank, jnp.broadcast_to(live, wide), 0.0)
    place[...] = chosen
    offset_in = (lengths[0] - 1 - first) - offset[...]
    wanted = jnp.sum(chosen * (offset_in + 1).astype(jnp.float32), axis=1, keepdims=True) - 1.0
    select = jnp.where(iota((LIVE, depth), 1).astype(jnp.float32) == wanted, 1.0, 0.0).astype(jnp.bfloat16)
    copies[3].wait()
    ids = jnp.sum(chosen * target[...].astype(jnp.float32), axis=1, keepdims=True).astype(jnp.int32)
    lane = iota((LIVE, CODE), 1)
    digits = jnp.where(
        lane == 0, ids % DIGIT, jnp.where(lane == 1, (ids // DIGIT) % DIGIT, jnp.where(lane == 2, ids // (DIGIT * DIGIT), 0))
    )
    codes[...] = digits.astype(jnp.float32).astype(jnp.bfloat16)
    copies[4].wait()
    copies[2].wait()
    rows[...] = jnp.dot(select, window[...], preferred_element_type=jnp.float32).astype(jnp.bfloat16)


def pick(hidden, gain, lengths, offsets, targets, mask):
    features = hidden.shape[2]
    slot_count = offsets.shape[1]
    vmem = pl.BlockSpec(memory_space=pltpu.VMEM)
    return pl.pallas_call(
        pick_kernel,
        out_shape=(
            jax.ShapeDtypeStruct((LIVE, features), jnp.bfloat16),
            jax.ShapeDtypeStruct((LIVE, CODE), jnp.bfloat16),
            jax.ShapeDtypeStruct((LIVE, slot_count), jnp.float32),
            jax.ShapeDtypeStruct((1, gain.shape[0]), jnp.float32),
        ),
        in_specs=[pl.BlockSpec(memory_space=pltpu.SMEM)] + [pl.BlockSpec(memory_space=pltpu.HBM)] * 5,
        out_specs=(vmem, vmem, vmem, vmem),
        scratch_shapes=[
            pltpu.VMEM((SPAN + BLOCK, features), jnp.bfloat16),
            pltpu.VMEM(offsets.shape, jnp.int32),
            pltpu.VMEM(offsets.shape, jnp.int32),
            pltpu.VMEM(offsets.shape, jnp.int32),
            pltpu.SemaphoreType.DMA((5,)),
        ],
        compiler_params=vmem_limit(32),
        name="pick",
    )(lengths, *map(in_hbm, (offsets, targets, mask, gain.reshape(1, -1), hidden)))


def join_kernel(*refs):
    tensor = len(refs) - 3
    parts, (codes, gain, rows) = refs[:tensor], refs[tensor:]
    live, features = parts[0].shape
    square = jnp.zeros((live, 1), jnp.float32)
    for part in parts:
        values = part[...].astype(jnp.float32)
        square += jnp.sum(values * values, axis=-1, keepdims=True)
    scale = lax.rsqrt(square / (tensor * features) + 1e-06)
    shard = lax.axis_index("tensor")
    for s, part in enumerate(parts):
        span = pl.ds(pl.multiple_of((shard ^ s) * features, features), features)
        rows[:, span] = (part[...].astype(jnp.float32) * scale * gain[:, span]).astype(jnp.bfloat16)
    rows[:, tensor * features :] = codes[...]


def join(parts, codes, gain):
    tensor = len(parts)
    live, features = parts[0].shape
    vmem = pl.BlockSpec(memory_space=pltpu.VMEM)
    return pl.pallas_call(
        join_kernel,
        out_shape=jax.ShapeDtypeStruct((live, tensor * features + CODE), jnp.bfloat16),
        in_specs=[vmem] * (tensor + 2),
        out_specs=vmem,
        compiler_params=vmem_limit(32),
        name="join",
    )(*parts, codes, gain)


def fetch_kernel(head, rows, held, rows_out, sems):
    count = sems.shape[0]
    depth = head.shape[0] // count
    copies = [
        pltpu.make_async_copy(head.at[pl.ds(i * depth, depth)], held.at[pl.ds(i * depth, depth)], sems.at[i])
        for i in range(count)
    ]
    for copy in copies:
        copy.start()
    rows_out[...] = rows[...]
    for copy in copies:
        copy.wait()


def fetch(head, rows):
    vmem = pl.BlockSpec(memory_space=pltpu.VMEM)
    return pl.pallas_call(
        fetch_kernel,
        out_shape=(pltpu.VMEM(head.shape, head.dtype), jax.ShapeDtypeStruct(rows.shape, rows.dtype)),
        in_specs=[pl.BlockSpec(memory_space=pltpu.HBM), vmem],
        out_specs=(vmem, vmem),
        scratch_shapes=[pltpu.SemaphoreType.DMA((4,))],
        compiler_params=vmem_limit(32),
        cost_estimate=pl.CostEstimate(flops=0, bytes_accessed=2 * head.size * 2, transcendentals=0),
        name="fetch",
    )(in_hbm(head), rows)


def score_kernel(order, *refs):
    dp = len(order)
    pieces, (head, stats) = refs[:dp], refs[dp:]
    depth, vocab_width = head.shape
    live = pieces[0].shape[0]
    row_count = dp * live
    mine = lax.axis_index("dp")
    start = (mine * stats.shape[1] + lax.axis_index("tensor")) * vocab_width

    logits = jnp.zeros((row_count, vocab_width), jnp.float32)
    for k in range(0, depth, CHUNK):
        normed = jnp.concatenate([piece[:, k : k + CHUNK] for piece in pieces], axis=0)
        logits += jnp.dot(normed, head[k : k + CHUNK], preferred_element_type=jnp.float32)
    digits = jnp.concatenate([piece[:, depth:] for piece in pieces], axis=0).astype(jnp.float32)
    lane = lax.broadcasted_iota(jnp.int32, (row_count, CODE), 1)
    weight = jnp.where(lane == 0, 1.0, jnp.where(lane == 1, float(DIGIT), jnp.where(lane == 2, float(DIGIT * DIGIT), 0.0)))
    target = jnp.sum(digits * weight, axis=-1, keepdims=True).astype(jnp.int32) - start
    column = lax.broadcasted_iota(jnp.int32, (row_count, vocab_width), 1)
    top = jnp.max(logits, axis=-1, keepdims=True)
    expo = jnp.exp(logits - top)
    total = jnp.sum(expo, axis=-1, keepdims=True)
    weighted = jnp.sum(expo * logits, axis=-1, keepdims=True)
    chosen = jnp.sum(jnp.where(column == target, logits, 0.0), axis=-1, keepdims=True)
    spot = lane - lax.broadcasted_iota(jnp.int32, (row_count, CODE), 0) % live
    tops = jnp.where((spot == 0) | (spot == GROUP), top, 0.0)
    sums = jnp.zeros((row_count, CODE), jnp.float32)
    for group, value in enumerate((total, weighted, chosen)):
        sums = jnp.where(spot == GROUP * group, value, sums)
    for i, d in enumerate(order):
        for line, table in enumerate((tops, sums)):
            packed = jnp.sum(table[i * live : (i + 1) * live], axis=0, keepdims=True)
            for t in range(stats.shape[1]):
                stats[mine ^ d, t, line : line + 1] = packed


def score(pieces, order, head, copies):
    dp = len(order)
    vmem = pl.BlockSpec(memory_space=pltpu.VMEM)
    return pl.pallas_call(
        functools.partial(score_kernel, order),
        out_shape=jax.ShapeDtypeStruct((dp, copies, 2, CODE), jnp.float32),
        in_specs=[vmem] * (dp + 1),
        out_specs=vmem,
        compiler_params=vmem_limit(32),
        name="score",
    )(*pieces, pltpu.with_memory_space_constraint(head, pltpu.VMEM))


def finish_kernel(stats, place, logprob, entropy, scored, spread, sems):
    tops = stats[:, 0:1, :]
    best = jnp.max(tops, axis=0)
    total = jnp.sum(stats[:, 1:2, :] * jnp.exp(tops - best), axis=0)
    weighted = pltpu.roll(total, CODE - GROUP, 1)
    chosen = pltpu.roll(total, CODE - 2 * GROUP, 1)
    lse = best + jnp.log(total)
    lane = lax.broadcasted_iota(jnp.int32, (LIVE, CODE), 1)
    row = lax.broadcasted_iota(jnp.int32, (LIVE, CODE), 0)

    def to_slots(values):
        column = jnp.sum(jnp.where(lane == row, values, 0.0), axis=1, keepdims=True)
        return jnp.sum(place[...] * column, axis=0, keepdims=True)

    scored[...] = to_slots(chosen - lse)
    first = pltpu.make_async_copy(scored, logprob, sems.at[0])
    first.start()
    spread[...] = to_slots(lse - weighted / total)
    second = pltpu.make_async_copy(spread, entropy, sems.at[1])
    second.start()
    first.wait()
    second.wait()


def finish(stats, place, slot_count):
    vmem = pl.BlockSpec(memory_space=pltpu.VMEM)
    out = jax.ShapeDtypeStruct((1, slot_count), jnp.float32)
    return pl.pallas_call(
        finish_kernel,
        out_shape=(out, out),
        in_specs=[vmem, vmem],
        out_specs=[pl.BlockSpec(memory_space=pltpu.HBM)] * 2,
        scratch_shapes=[
            pltpu.VMEM((1, slot_count), jnp.float32),
            pltpu.VMEM((1, slot_count), jnp.float32),
            pltpu.SemaphoreType.DMA((2,)),
        ],
        compiler_params=vmem_limit(32),
        name="finish",
    )(stats, place)


def swap(x, axis, distance):
    return lax.ppermute(x, axis, [(i, i ^ distance) for i in range(lax.axis_size(axis))])


def per_device(hidden, gain, head, lengths, offsets, targets, mask):
    dp, tensor = lax.axis_size("dp"), lax.axis_size("tensor")
    rows, codes, slots, gain = pick(hidden, gain, lengths, offsets, targets, mask)
    parts = {0: rows} | {s: swap(rows, "tensor", s) for s in reversed(range(1, tensor))}
    rows = join([parts[s] for s in range(tensor)], codes, gain)

    pieces = {d: swap(rows, "dp", d) for d in reversed(range(2, dp, 2))}
    held, pieces[0] = fetch(head, rows)
    for d in range(0, dp, 2):
        pieces[d + 1] = swap(pieces[d], "dp", 1)
    order = [0, 1] + [d + core for d in reversed(range(2, dp, 2)) for core in (0, 1)]
    stats = score([pieces[d] for d in order], order, held, tensor)
    stats = lax.all_to_all(stats.reshape(dp * tensor, 2, CODE), ("dp", "tensor"), 0, 0, tiled=True)
    return finish(stats, slots, offsets.shape[1])


def solution(mesh):
    return jax.shard_map(
        per_device,
        mesh=mesh,
        in_specs=(
            P("dp", None, "tensor"),
            P(),
            P(None, ("dp", "tensor")),
            P("dp"),
            P("dp", None),
            P("dp", None),
            P("dp", None),
        ),
        out_specs=(P("dp", None), P("dp", None)),
        check_vma=False,
    )
```

```python
import functools

import jax
import jax.numpy as jnp
from jax import lax
from jax.experimental import pallas as pl
from jax.experimental.pallas import tpu as pltpu
from jax.sharding import PartitionSpec as P

LIVE = 16
SPAN = 256
BLOCK = 16
CODE = 128
DIGIT = 64
GROUP = 16


def vmem_limit(mebibytes):
    return pltpu.CompilerParams(vmem_limit_bytes=mebibytes * 1024 * 1024)


def in_hbm(x):
    return pltpu.with_memory_space_constraint(x, pltpu.HBM)


def pick_kernel(
    lengths, offsets, targets, mask, gain, hidden, rows, codes, place, gain_out, window, offset, target, alive, sems
):
    slot_count = offsets.shape[1]
    depth = window.shape[0]
    first = jnp.minimum((lengths[0] - SPAN) // BLOCK * BLOCK, hidden.shape[1] - depth)
    first = pl.multiple_of(first, BLOCK)
    copies = [
        pltpu.make_async_copy(offsets, offset, sems.at[0]),
        pltpu.make_async_copy(mask, alive, sems.at[1]),
        pltpu.make_async_copy(hidden.at[0, pl.ds(first, depth)], window, sems.at[2]),
        pltpu.make_async_copy(targets, target, sems.at[3]),
        pltpu.make_async_copy(gain, gain_out, sems.at[4]),
    ]
    for copy in copies:
        copy.start()
    for copy in copies[:2]:
        copy.wait()

    def iota(shape, axis):
        return lax.broadcasted_iota(jnp.int32, shape, axis)

    square = (slot_count, slot_count)
    live = jnp.where(alive[...] != 0, 1.0, 0.0)
    column = jnp.sum(jnp.where(iota(square, 0) == iota(square, 1), live, 0.0), axis=1, keepdims=True)
    rank = jnp.sum(jnp.where(iota(square, 0) < iota(square, 1), column, 0.0), axis=0, keepdims=True)
    wide = (LIVE, slot_count)
    chosen = jnp.where(iota(wide, 0).astype(jnp.float32) == rank, jnp.broadcast_to(live, wide), 0.0)
    place[...] = chosen
    offset_in = (lengths[0] - 1 - first) - offset[...]
    wanted = jnp.sum(chosen * (offset_in + 1).astype(jnp.float32), axis=1, keepdims=True) - 1.0
    select = jnp.where(iota((LIVE, depth), 1).astype(jnp.float32) == wanted, 1.0, 0.0).astype(jnp.bfloat16)
    copies[3].wait()
    ids = jnp.sum(chosen * target[...].astype(jnp.float32), axis=1, keepdims=True).astype(jnp.int32)
    lane = iota((LIVE, CODE), 1)
    digits = jnp.where(
        lane == 0, ids % DIGIT, jnp.where(lane == 1, (ids // DIGIT) % DIGIT, jnp.where(lane == 2, ids // (DIGIT * DIGIT), 0))
    )
    codes[...] = digits.astype(jnp.float32).astype(jnp.bfloat16)
    copies[4].wait()
    copies[2].wait()
    rows[...] = jnp.dot(select, window[...], preferred_element_type=jnp.float32).astype(jnp.bfloat16)


def pick(hidden, gain, lengths, offsets, targets, mask):
    features = hidden.shape[2]
    slot_count = offsets.shape[1]
    vmem = pl.BlockSpec(memory_space=pltpu.VMEM)
    return pl.pallas_call(
        pick_kernel,
        out_shape=(
            jax.ShapeDtypeStruct((LIVE, features), jnp.bfloat16),
            jax.ShapeDtypeStruct((LIVE, CODE), jnp.bfloat16),
            jax.ShapeDtypeStruct((LIVE, slot_count), jnp.float32),
            jax.ShapeDtypeStruct((1, gain.shape[0]), jnp.float32),
        ),
        in_specs=[pl.BlockSpec(memory_space=pltpu.SMEM)] + [pl.BlockSpec(memory_space=pltpu.HBM)] * 5,
        out_specs=(vmem, vmem, vmem, vmem),
        scratch_shapes=[
            pltpu.VMEM((SPAN + BLOCK, features), jnp.bfloat16),
            pltpu.VMEM(offsets.shape, jnp.int32),
            pltpu.VMEM(offsets.shape, jnp.int32),
            pltpu.VMEM(offsets.shape, jnp.int32),
            pltpu.SemaphoreType.DMA((5,)),
        ],
        compiler_params=vmem_limit(32),
        name="pick",
    )(lengths, *map(in_hbm, (offsets, targets, mask, gain.reshape(1, -1), hidden)))


def join_kernel(*refs):
    tensor = len(refs) - 3
    parts, (codes, gain, rows) = refs[:tensor], refs[tensor:]
    live, features = parts[0].shape
    square = jnp.zeros((live, 1), jnp.float32)
    for part in parts:
        values = part[...].astype(jnp.float32)
        square += jnp.sum(values * values, axis=-1, keepdims=True)
    scale = lax.rsqrt(square / (tensor * features) + 1e-06)
    shard = lax.axis_index("tensor")
    for s, part in enumerate(reversed(parts)):
        span = pl.ds(pl.multiple_of((shard ^ s) * features, features), features)
        rows[:, span] = (part[...].astype(jnp.float32) * scale * gain[:, span]).astype(jnp.bfloat16)
    rows[:, tensor * features :] = codes[...]


def join(parts, codes, gain):
    tensor = len(parts)
    live, features = parts[0].shape
    vmem = pl.BlockSpec(memory_space=pltpu.VMEM)
    return pl.pallas_call(
        join_kernel,
        out_shape=jax.ShapeDtypeStruct((live, tensor * features + CODE), jnp.bfloat16),
        in_specs=[vmem] * (tensor + 2),
        out_specs=vmem,
        compiler_params=vmem_limit(32),
        name="join",
    )(*parts, codes, gain)


def fetch_kernel(head, rows, held, rows_out, sems):
    count = sems.shape[0]
    depth = head.shape[0] // count
    copies = [
        pltpu.make_async_copy(head.at[pl.ds(i * depth, depth)], held.at[pl.ds(i * depth, depth)], sems.at[i])
        for i in range(count)
    ]
    for copy in copies:
        copy.start()
    rows_out[...] = rows[...]
    for copy in copies:
        copy.wait()


def fetch(head, rows):
    vmem = pl.BlockSpec(memory_space=pltpu.VMEM)
    return pl.pallas_call(
        fetch_kernel,
        out_shape=(pltpu.VMEM(head.shape, head.dtype), jax.ShapeDtypeStruct(rows.shape, rows.dtype)),
        in_specs=[pl.BlockSpec(memory_space=pltpu.HBM), vmem],
        out_specs=(vmem, vmem),
        scratch_shapes=[pltpu.SemaphoreType.DMA((4,))],
        compiler_params=vmem_limit(32),
        cost_estimate=pl.CostEstimate(flops=0, bytes_accessed=2 * head.size * 2, transcendentals=0),
        name="fetch",
    )(in_hbm(head), rows)


def score_kernel(order, head, *refs):
    pieces, (*earlier, stats) = refs[: len(order)], refs[len(order) :]
    depth, vocab_width = head.shape
    live = pieces[0].shape[0]
    row_count = len(order) * live
    mine = lax.axis_index("dp")
    start = (mine * lax.axis_size("tensor") + lax.axis_index("tensor")) * vocab_width

    normed = jnp.concatenate([piece[:, :depth] for piece in pieces], axis=0)
    logits = jnp.dot(normed, head[...], preferred_element_type=jnp.float32)
    digits = jnp.concatenate([piece[:, depth:] for piece in pieces], axis=0).astype(jnp.float32)
    lane = lax.broadcasted_iota(jnp.int32, (row_count, CODE), 1)
    weight = jnp.where(lane == 0, 1.0, jnp.where(lane == 1, float(DIGIT), jnp.where(lane == 2, float(DIGIT * DIGIT), 0.0)))
    target = jnp.sum(digits * weight, axis=-1, keepdims=True).astype(jnp.int32) - start
    column = lax.broadcasted_iota(jnp.int32, (row_count, vocab_width), 1)
    top = jnp.max(logits, axis=-1, keepdims=True)
    expo = jnp.exp(logits - top)
    total = jnp.sum(expo, axis=-1, keepdims=True)
    weighted = jnp.sum(expo * logits, axis=-1, keepdims=True)
    chosen = jnp.sum(jnp.where(column == target, logits, 0.0), axis=-1, keepdims=True)
    spot = lane - lax.broadcasted_iota(jnp.int32, (row_count, CODE), 0) % live
    tops = jnp.where((spot == 0) | (spot == GROUP), top, 0.0)
    sums = jnp.zeros((row_count, CODE), jnp.float32)
    for group, value in enumerate((total, weighted, chosen)):
        sums = jnp.where(spot == GROUP * group, value, sums)
    for i, d in enumerate(order):
        for line, table in enumerate((tops, sums)):
            packed = jnp.sum(table[i * live : (i + 1) * live], axis=0, keepdims=True)
            if earlier:
                for t in range(stats.shape[1]):
                    stats[mine ^ d, t, line : line + 1] = packed
            else:
                stats[i, line : line + 1] = packed
    for i, d in enumerate(order if earlier else ()):
        for t in range(stats.shape[1]):
            stats[mine ^ (d - 1), t] = earlier[0][i]


def score(order, head, pieces, *rest, shape):
    vmem = pl.BlockSpec(memory_space=pltpu.VMEM)
    return pl.pallas_call(
        functools.partial(score_kernel, order),
        out_shape=jax.ShapeDtypeStruct(shape, jnp.float32),
        in_specs=[vmem] * (1 + len(order) + len(rest)),
        out_specs=vmem,
        compiler_params=vmem_limit(32),
        name="score",
    )(pltpu.with_memory_space_constraint(head, pltpu.VMEM), *[pieces[d] for d in order], *rest)


def finish_kernel(stats, place, logprob, entropy, scored, spread, sems):
    tops = stats[:, 0:1, :]
    best = jnp.max(tops, axis=0)
    total = jnp.sum(stats[:, 1:2, :] * jnp.exp(tops - best), axis=0)
    weighted = pltpu.roll(total, CODE - GROUP, 1)
    chosen = pltpu.roll(total, CODE - 2 * GROUP, 1)
    lse = best + jnp.log(total)
    lane = lax.broadcasted_iota(jnp.int32, (LIVE, CODE), 1)
    row = lax.broadcasted_iota(jnp.int32, (LIVE, CODE), 0)

    def to_slots(values):
        column = jnp.sum(jnp.where(lane == row, values, 0.0), axis=1, keepdims=True)
        return jnp.sum(place[...] * column, axis=0, keepdims=True)

    scored[...] = to_slots(chosen - lse)
    first = pltpu.make_async_copy(scored, logprob, sems.at[0])
    first.start()
    spread[...] = to_slots(lse - weighted / total)
    second = pltpu.make_async_copy(spread, entropy, sems.at[1])
    second.start()
    first.wait()
    second.wait()


def finish(stats, place, slot_count):
    vmem = pl.BlockSpec(memory_space=pltpu.VMEM)
    out = jax.ShapeDtypeStruct((1, slot_count), jnp.float32)
    return pl.pallas_call(
        finish_kernel,
        out_shape=(out, out),
        in_specs=[vmem, vmem],
        out_specs=[pl.BlockSpec(memory_space=pltpu.HBM)] * 2,
        scratch_shapes=[
            pltpu.VMEM((1, slot_count), jnp.float32),
            pltpu.VMEM((1, slot_count), jnp.float32),
            pltpu.SemaphoreType.DMA((2,)),
        ],
        compiler_params=vmem_limit(32),
        name="finish",
    )(stats, place)


def swap(x, axis, distance):
    return lax.ppermute(x, axis, [(i, i ^ distance) for i in range(lax.axis_size(axis))])


def per_device(hidden, gain, head, lengths, offsets, targets, mask):
    dp, tensor = lax.axis_size("dp"), lax.axis_size("tensor")
    rows, codes, slots, gain = pick(hidden, gain, lengths, offsets, targets, mask)
    parts = {0: rows} | {s: swap(rows, "tensor", s) for s in reversed(range(1, tensor))}
    rows = join([parts[s] for s in reversed(range(tensor))], codes, gain)

    pieces = {d: swap(rows, "dp", d) for d in reversed(range(2, dp, 2))}
    held, pieces[0] = fetch(head, rows)
    for d in range(0, dp, 2):
        pieces[d + 1] = swap(pieces[d], "dp", 1)
    early = score(range(dp - 2, -1, -2), held, pieces, shape=(dp // 2, 2, CODE))
    stats = score(range(dp - 1, 0, -2), held, pieces, early, shape=(dp, tensor, 2, CODE))
    stats = lax.all_to_all(stats.reshape(dp * tensor, 2, CODE), ("dp", "tensor"), 0, 0, tiled=True)
    return finish(stats, slots, offsets.shape[1])


def solution(mesh):
    return jax.shard_map(
        per_device,
        mesh=mesh,
        in_specs=(
            P("dp", None, "tensor"),
            P(),
            P(None, ("dp", "tensor")),
            P("dp"),
            P("dp", None),
            P("dp", None),
            P("dp", None),
        ),
        out_specs=(P("dp", None), P("dp", None)),
        check_vma=False,
    )
```

```python
import functools

import jax
import jax.numpy as jnp
from jax import lax
from jax.experimental import pallas as pl
from jax.experimental.pallas import tpu as pltpu
from jax.sharding import PartitionSpec as P

LIVE = 16
SPAN = 256
BLOCK = 16
CODE = 128
DIGIT = 64
GROUP = 16
CHUNK = 1024


def vmem_limit(mebibytes):
    return pltpu.CompilerParams(vmem_limit_bytes=mebibytes * 1024 * 1024)


def in_hbm(x):
    return pltpu.with_memory_space_constraint(x, pltpu.HBM)


def pick_kernel(
    lengths, offsets, targets, mask, gain, hidden, rows, codes, place, gain_out, window, offset, target, alive, sems
):
    slot_count = offsets.shape[1]
    depth = window.shape[0]
    first = jnp.minimum((lengths[0] - SPAN) // BLOCK * BLOCK, hidden.shape[1] - depth)
    first = pl.multiple_of(first, BLOCK)
    copies = [
        pltpu.make_async_copy(offsets, offset, sems.at[0]),
        pltpu.make_async_copy(mask, alive, sems.at[1]),
        pltpu.make_async_copy(hidden.at[0, pl.ds(first, depth)], window, sems.at[2]),
        pltpu.make_async_copy(targets, target, sems.at[3]),
        pltpu.make_async_copy(gain, gain_out, sems.at[4]),
    ]
    for copy in copies:
        copy.start()
    for copy in copies[:2]:
        copy.wait()

    def iota(shape, axis):
        return lax.broadcasted_iota(jnp.int32, shape, axis)

    square = (slot_count, slot_count)
    live = jnp.where(alive[...] != 0, 1.0, 0.0)
    column = jnp.sum(jnp.where(iota(square, 0) == iota(square, 1), live, 0.0), axis=1, keepdims=True)
    rank = jnp.sum(jnp.where(iota(square, 0) < iota(square, 1), column, 0.0), axis=0, keepdims=True)
    wide = (LIVE, slot_count)
    chosen = jnp.where(iota(wide, 0).astype(jnp.float32) == rank, jnp.broadcast_to(live, wide), 0.0)
    place[...] = chosen
    offset_in = (lengths[0] - 1 - first) - offset[...]
    wanted = jnp.sum(chosen * (offset_in + 1).astype(jnp.float32), axis=1, keepdims=True) - 1.0
    select = jnp.where(iota((LIVE, depth), 1).astype(jnp.float32) == wanted, 1.0, 0.0).astype(jnp.bfloat16)
    copies[3].wait()
    ids = jnp.sum(chosen * target[...].astype(jnp.float32), axis=1, keepdims=True).astype(jnp.int32)
    lane = iota((LIVE, CODE), 1)
    digits = jnp.where(
        lane == 0, ids % DIGIT, jnp.where(lane == 1, (ids // DIGIT) % DIGIT, jnp.where(lane == 2, ids // (DIGIT * DIGIT), 0))
    )
    codes[...] = digits.astype(jnp.float32).astype(jnp.bfloat16)
    copies[4].wait()
    copies[2].wait()
    rows[...] = jnp.dot(select, window[...], preferred_element_type=jnp.float32).astype(jnp.bfloat16)


def pick(hidden, gain, lengths, offsets, targets, mask):
    features = hidden.shape[2]
    slot_count = offsets.shape[1]
    vmem = pl.BlockSpec(memory_space=pltpu.VMEM)
    return pl.pallas_call(
        pick_kernel,
        out_shape=(
            jax.ShapeDtypeStruct((LIVE, features), jnp.bfloat16),
            jax.ShapeDtypeStruct((LIVE, CODE), jnp.bfloat16),
            jax.ShapeDtypeStruct((LIVE, slot_count), jnp.float32),
            jax.ShapeDtypeStruct((1, gain.shape[0]), jnp.float32),
        ),
        in_specs=[pl.BlockSpec(memory_space=pltpu.SMEM)] + [pl.BlockSpec(memory_space=pltpu.HBM)] * 5,
        out_specs=(vmem, vmem, vmem, vmem),
        scratch_shapes=[
            pltpu.VMEM((SPAN + BLOCK, features), jnp.bfloat16),
            pltpu.VMEM(offsets.shape, jnp.int32),
            pltpu.VMEM(offsets.shape, jnp.int32),
            pltpu.VMEM(offsets.shape, jnp.int32),
            pltpu.SemaphoreType.DMA((5,)),
        ],
        compiler_params=vmem_limit(32),
        name="pick",
    )(lengths, *map(in_hbm, (offsets, targets, mask, gain.reshape(1, -1), hidden)))


def join_kernel(*refs):
    tensor = len(refs) - 3
    parts, (codes, gain, rows) = refs[:tensor], refs[tensor:]
    live, features = parts[0].shape
    square = jnp.zeros((live, 1), jnp.float32)
    for part in parts:
        values = part[...].astype(jnp.float32)
        square += jnp.sum(values * values, axis=-1, keepdims=True)
    scale = lax.rsqrt(square / (tensor * features) + 1e-06)
    shard = lax.axis_index("tensor")
    for s, part in enumerate(parts):
        span = pl.ds(pl.multiple_of((shard ^ s) * features, features), features)
        rows[:, span] = (part[...].astype(jnp.float32) * scale * gain[:, span]).astype(jnp.bfloat16)
    rows[:, tensor * features :] = codes[...]


def join(parts, codes, gain):
    tensor = len(parts)
    live, features = parts[0].shape
    vmem = pl.BlockSpec(memory_space=pltpu.VMEM)
    return pl.pallas_call(
        join_kernel,
        out_shape=jax.ShapeDtypeStruct((live, tensor * features + CODE), jnp.bfloat16),
        in_specs=[vmem] * (tensor + 2),
        out_specs=vmem,
        compiler_params=vmem_limit(32),
        name="join",
    )(*parts, codes, gain)


def fetch_kernel(head, after, held, sems):
    del after
    count = sems.shape[0]
    depth = head.shape[0] // count
    copies = [
        pltpu.make_async_copy(head.at[pl.ds(i * depth, depth)], held.at[pl.ds(i * depth, depth)], sems.at[i])
        for i in range(count)
    ]
    for copy in copies:
        copy.start()
    for copy in copies:
        copy.wait()


def fetch(head, after):
    return pl.pallas_call(
        fetch_kernel,
        out_shape=pltpu.VMEM(head.shape, head.dtype),
        in_specs=[pl.BlockSpec(memory_space=pltpu.HBM), pl.BlockSpec(memory_space=pltpu.VMEM)],
        out_specs=pl.BlockSpec(memory_space=pltpu.VMEM),
        scratch_shapes=[pltpu.SemaphoreType.DMA((4,))],
        compiler_params=vmem_limit(32),
        cost_estimate=pl.CostEstimate(flops=0, bytes_accessed=4 * head.size, transcendentals=0),
        name="fetch",
    )(in_hbm(head), after)


def score_kernel(chips, *refs):
    pieces, (own, other, stats) = refs[:chips], refs[chips:]
    depth, vocab_width = own.shape
    tensor = stats.shape[1]
    live = pieces[0].shape[0]
    row_count = chips * live
    mine, core, shard = lax.axis_index("chip"), lax.axis_index("core"), lax.axis_index("tensor")

    normed = jnp.concatenate([piece[:, :depth] for piece in pieces], axis=0)
    digits = jnp.concatenate([piece[:, depth:] for piece in pieces], axis=0).astype(jnp.float32)
    lane = lax.broadcasted_iota(jnp.int32, (row_count, CODE), 1)
    weight = jnp.where(lane == 0, 1.0, jnp.where(lane == 1, float(DIGIT), jnp.where(lane == 2, float(DIGIT * DIGIT), 0.0)))
    target = jnp.sum(digits * weight, axis=-1, keepdims=True).astype(jnp.int32)
    column = lax.broadcasted_iota(jnp.int32, (row_count, vocab_width), 1)
    logits, hits = [], []
    for head, holder in ((own, core), (other, 1 - core)):
        start = ((mine * 2 + holder) * tensor + shard) * vocab_width
        logits.append(jnp.dot(normed, head[...], preferred_element_type=jnp.float32))
        hits.append(jnp.where(column == target - start, logits[-1], 0.0))
    top = jnp.max(jnp.maximum(*logits), axis=-1, keepdims=True)
    expo = [jnp.exp(part - top) for part in logits]
    total = jnp.sum(expo[0] + expo[1], axis=-1, keepdims=True)
    weighted = jnp.sum(expo[0] * logits[0] + expo[1] * logits[1], axis=-1, keepdims=True)
    chosen = jnp.sum(hits[0] + hits[1], axis=-1, keepdims=True)
    spot = lane - lax.broadcasted_iota(jnp.int32, (row_count, CODE), 0) % live
    tops = jnp.where((spot == 0) | (spot == GROUP), top, 0.0)
    sums = jnp.zeros((row_count, CODE), jnp.float32)
    for group, value in enumerate((total, weighted, chosen)):
        sums = jnp.where(spot == GROUP * group, value, sums)
    for d in range(chips):
        for line, table in enumerate((tops, sums)):
            packed = jnp.sum(table[d * live : (d + 1) * live], axis=0, keepdims=True)
            for t in range(tensor):
                stats[mine ^ d, t, line : line + 1] = packed


def score(pieces, own, other, tensor):
    chips = len(pieces)
    vmem = pl.BlockSpec(memory_space=pltpu.VMEM)
    heads = [pltpu.with_memory_space_constraint(head, pltpu.VMEM) for head in (own, other)]
    return pl.pallas_call(
        functools.partial(score_kernel, chips),
        out_shape=jax.ShapeDtypeStruct((chips, tensor, 2, CODE), jnp.float32),
        in_specs=[vmem] * (chips + 2),
        out_specs=vmem,
        compiler_params=vmem_limit(32),
        name="score",
    )(*pieces, *heads)


def finish_kernel(stats, place, logprob, entropy, scored, spread, sems):
    tops = stats[:, 0:1, :]
    best = jnp.max(tops, axis=0)
    total = jnp.sum(stats[:, 1:2, :] * jnp.exp(tops - best), axis=0)
    weighted = pltpu.roll(total, CODE - GROUP, 1)
    chosen = pltpu.roll(total, CODE - 2 * GROUP, 1)
    lse = best + jnp.log(total)
    lane = lax.broadcasted_iota(jnp.int32, (LIVE, CODE), 1)
    row = lax.broadcasted_iota(jnp.int32, (LIVE, CODE), 0)

    def to_slots(values):
        column = jnp.sum(jnp.where(lane == row, values, 0.0), axis=1, keepdims=True)
        return jnp.sum(place[...] * column, axis=0, keepdims=True)

    scored[...] = to_slots(chosen - lse)
    first = pltpu.make_async_copy(scored, logprob, sems.at[0])
    first.start()
    spread[...] = to_slots(lse - weighted / total)
    second = pltpu.make_async_copy(spread, entropy, sems.at[1])
    second.start()
    first.wait()
    second.wait()


def finish(stats, place, slot_count):
    vmem = pl.BlockSpec(memory_space=pltpu.VMEM)
    out = jax.ShapeDtypeStruct((1, slot_count), jnp.float32)
    return pl.pallas_call(
        finish_kernel,
        out_shape=(out, out),
        in_specs=[vmem, vmem],
        out_specs=[pl.BlockSpec(memory_space=pltpu.HBM)] * 2,
        scratch_shapes=[
            pltpu.VMEM((1, slot_count), jnp.float32),
            pltpu.VMEM((1, slot_count), jnp.float32),
            pltpu.SemaphoreType.DMA((2,)),
        ],
        compiler_params=vmem_limit(32),
        name="finish",
    )(stats, place)


def swap(x, axis, distance):
    return lax.ppermute(x, axis, [(i, i ^ distance) for i in range(lax.axis_size(axis))])


def per_device(hidden, gain, head, lengths, offsets, targets, mask):
    chips, tensor = lax.axis_size("chip"), lax.axis_size("tensor")
    rows, codes, slots, gain = pick(hidden, gain, lengths, offsets, targets, mask)
    parts = {0: rows} | {s: swap(rows, "tensor", s) for s in reversed(range(1, tensor))}
    rows = join([parts[s] for s in range(tensor)], codes, gain)
    pieces = [rows] + [swap(rows, "chip", d) for d in range(1, chips)]
    stats = score(pieces, fetch(head, rows), swap(head, "core", 1), tensor)
    stats = lax.all_to_all(stats.reshape(chips * tensor, 2, CODE), ("chip", "tensor"), 0, 0, tiled=True)
    return finish(stats, slots, offsets.shape[1])


def solution(mesh):
    dp, tensor = mesh.shape["dp"], mesh.shape["tensor"]
    mesh = jax.sharding.Mesh(mesh.devices.reshape(dp // 2, 2, tensor), ("chip", "core", "tensor"))
    dp = ("chip", "core")
    return jax.shard_map(
        per_device,
        mesh=mesh,
        in_specs=(
            P(dp, None, "tensor"),
            P(),
            P(None, (*dp, "tensor")),
            P(dp),
            P(dp, None),
            P(dp, None),
            P(dp, None),
        ),
        out_specs=(P(dp, None), P(dp, None)),
        check_vma=False,
    )
```

```python
import jax
import jax.numpy as jnp
from jax import lax
from jax.experimental import pallas as pl
from jax.experimental.pallas import tpu as pltpu
from jax.sharding import PartitionSpec as P

LIVE = 16
SPAN = 256
BLOCK = 16
CODE = 128
DIGIT = 64
GROUP = 16


def vmem_limit(mebibytes):
    return pltpu.CompilerParams(vmem_limit_bytes=mebibytes * 1024 * 1024)


def in_hbm(x):
    return pltpu.with_memory_space_constraint(x, pltpu.HBM)


def pick_kernel(
    lengths, offsets, targets, mask, gain, hidden, rows, codes, place, gain_out, window, offset, target, alive, sems
):
    slot_count = offsets.shape[1]
    depth = window.shape[0]
    first = jnp.minimum((lengths[0] - SPAN) // BLOCK * BLOCK, hidden.shape[1] - depth)
    first = pl.multiple_of(first, BLOCK)
    copies = [
        pltpu.make_async_copy(offsets, offset, sems.at[0]),
        pltpu.make_async_copy(mask, alive, sems.at[1]),
        pltpu.make_async_copy(hidden.at[0, pl.ds(first, depth)], window, sems.at[2]),
        pltpu.make_async_copy(targets, target, sems.at[3]),
        pltpu.make_async_copy(gain, gain_out, sems.at[4]),
    ]
    for copy in copies:
        copy.start()
    for copy in copies[:2]:
        copy.wait()

    def iota(shape, axis):
        return lax.broadcasted_iota(jnp.int32, shape, axis)

    square = (slot_count, slot_count)
    live = jnp.where(alive[...] != 0, 1.0, 0.0)
    column = jnp.sum(jnp.where(iota(square, 0) == iota(square, 1), live, 0.0), axis=1, keepdims=True)
    rank = jnp.sum(jnp.where(iota(square, 0) < iota(square, 1), column, 0.0), axis=0, keepdims=True)
    wide = (LIVE, slot_count)
    chosen = jnp.where(iota(wide, 0).astype(jnp.float32) == rank, jnp.broadcast_to(live, wide), 0.0)
    place[...] = chosen
    offset_in = (lengths[0] - 1 - first) - offset[...]
    wanted = jnp.sum(chosen * (offset_in + 1).astype(jnp.float32), axis=1, keepdims=True) - 1.0
    select = jnp.where(iota((LIVE, depth), 1).astype(jnp.float32) == wanted, 1.0, 0.0).astype(jnp.bfloat16)
    copies[3].wait()
    ids = jnp.sum(chosen * target[...].astype(jnp.float32), axis=1, keepdims=True).astype(jnp.int32)
    lane = iota((LIVE, CODE), 1)
    digits = jnp.where(
        lane == 0, ids % DIGIT, jnp.where(lane == 1, (ids // DIGIT) % DIGIT, jnp.where(lane == 2, ids // (DIGIT * DIGIT), 0))
    )
    codes[...] = digits.astype(jnp.float32).astype(jnp.bfloat16)
    copies[4].wait()
    copies[2].wait()
    rows[...] = jnp.dot(select, window[...], preferred_element_type=jnp.float32).astype(jnp.bfloat16)


def pick(hidden, gain, lengths, offsets, targets, mask):
    features = hidden.shape[2]
    slot_count = offsets.shape[1]
    vmem = pl.BlockSpec(memory_space=pltpu.VMEM)
    return pl.pallas_call(
        pick_kernel,
        out_shape=(
            jax.ShapeDtypeStruct((LIVE, features), jnp.bfloat16),
            jax.ShapeDtypeStruct((LIVE, CODE), jnp.bfloat16),
            jax.ShapeDtypeStruct((LIVE, slot_count), jnp.float32),
            jax.ShapeDtypeStruct((1, gain.shape[0]), jnp.float32),
        ),
        in_specs=[pl.BlockSpec(memory_space=pltpu.SMEM)] + [pl.BlockSpec(memory_space=pltpu.HBM)] * 5,
        out_specs=(vmem, vmem, vmem, vmem),
        scratch_shapes=[
            pltpu.VMEM((SPAN + BLOCK, features), jnp.bfloat16),
            pltpu.VMEM(offsets.shape, jnp.int32),
            pltpu.VMEM(offsets.shape, jnp.int32),
            pltpu.VMEM(offsets.shape, jnp.int32),
            pltpu.SemaphoreType.DMA((5,)),
        ],
        compiler_params=vmem_limit(32),
        name="pick",
    )(lengths, *map(in_hbm, (offsets, targets, mask, gain.reshape(1, -1), hidden)))


def join_kernel(*refs):
    tensor = len(refs) - 3
    parts, (codes, gain, rows) = refs[:tensor], refs[tensor:]
    live, features = parts[0].shape
    square = jnp.zeros((live, 1), jnp.float32)
    for part in parts:
        values = part[...].astype(jnp.float32)
        square += jnp.sum(values * values, axis=-1, keepdims=True)
    scale = lax.rsqrt(square / (tensor * features) + 1e-06)
    shard = lax.axis_index("tensor")
    for s, part in enumerate(parts):
        span = pl.ds(pl.multiple_of((shard ^ s) * features, features), features)
        rows[:, span] = (part[...].astype(jnp.float32) * scale * gain[:, span]).astype(jnp.bfloat16)
    rows[:, tensor * features :] = codes[...]


def join(parts, codes, gain):
    tensor = len(parts)
    live, features = parts[0].shape
    vmem = pl.BlockSpec(memory_space=pltpu.VMEM)
    return pl.pallas_call(
        join_kernel,
        out_shape=jax.ShapeDtypeStruct((live, tensor * features + CODE), jnp.bfloat16),
        in_specs=[vmem] * (tensor + 2),
        out_specs=vmem,
        compiler_params=vmem_limit(32),
        name="join",
    )(*parts, codes, gain)


def fetch_kernel(head, rows, held, rows_out, sems):
    count = sems.shape[0]
    depth = head.shape[0] // count
    copies = [
        pltpu.make_async_copy(head.at[pl.ds(i * depth, depth)], held.at[pl.ds(i * depth, depth)], sems.at[i])
        for i in range(count)
    ]
    for copy in copies:
        copy.start()
    rows_out[...] = rows[...]
    for copy in copies:
        copy.wait()


def fetch(head, rows):
    vmem = pl.BlockSpec(memory_space=pltpu.VMEM)
    return pl.pallas_call(
        fetch_kernel,
        out_shape=(pltpu.VMEM(head.shape, head.dtype), jax.ShapeDtypeStruct(rows.shape, rows.dtype)),
        in_specs=[pl.BlockSpec(memory_space=pltpu.HBM), vmem],
        out_specs=(vmem, vmem),
        scratch_shapes=[pltpu.SemaphoreType.DMA((4,))],
        compiler_params=vmem_limit(32),
        cost_estimate=pl.CostEstimate(flops=0, bytes_accessed=2 * head.size * 2, transcendentals=0),
        name="fetch",
    )(in_hbm(head), rows)


def score_kernel(*refs):
    dp = len(refs) - 2
    pieces, (head, stats) = refs[:dp], refs[dp:]
    depth, vocab_width = head.shape
    live = pieces[0].shape[0]
    row_count = dp * live
    mine = lax.axis_index("dp")
    start = (mine * stats.shape[1] + lax.axis_index("tensor")) * vocab_width

    normed = jnp.concatenate([piece[:, :depth] for piece in pieces], axis=0)
    logits = jnp.dot(normed, head[...], preferred_element_type=jnp.float32)
    digits = jnp.concatenate([piece[:, depth:] for piece in pieces], axis=0).astype(jnp.float32)
    lane = lax.broadcasted_iota(jnp.int32, (row_count, CODE), 1)
    weight = jnp.where(lane == 0, 1.0, jnp.where(lane == 1, float(DIGIT), jnp.where(lane == 2, float(DIGIT * DIGIT), 0.0)))
    target = jnp.sum(digits * weight, axis=-1, keepdims=True).astype(jnp.int32) - start
    column = lax.broadcasted_iota(jnp.int32, (row_count, vocab_width), 1)
    top = jnp.max(logits, axis=-1, keepdims=True)
    expo = jnp.exp(logits - top)
    total = jnp.sum(expo, axis=-1, keepdims=True)
    weighted = jnp.sum(expo * logits, axis=-1, keepdims=True)
    chosen = jnp.sum(jnp.where(column == target, logits, 0.0), axis=-1, keepdims=True)
    spot = lane - lax.broadcasted_iota(jnp.int32, (row_count, CODE), 0) % live
    tops = jnp.where((spot == 0) | (spot == GROUP), top, 0.0)
    sums = jnp.zeros((row_count, CODE), jnp.float32)
    for group, value in enumerate((total, weighted, chosen)):
        sums = jnp.where(spot == GROUP * group, value, sums)
    for d in range(dp):
        for line, table in enumerate((tops, sums)):
            packed = jnp.sum(table[d * live : (d + 1) * live], axis=0, keepdims=True)
            for t in range(stats.shape[1]):
                stats[mine ^ d, t, line : line + 1] = packed


def score(pieces, head, copies):
    dp = len(pieces)
    vmem = pl.BlockSpec(memory_space=pltpu.VMEM)
    return pl.pallas_call(
        score_kernel,
        out_shape=jax.ShapeDtypeStruct((dp, copies, 2, CODE), jnp.float32),
        in_specs=[vmem] * (dp + 1),
        out_specs=vmem,
        compiler_params=vmem_limit(32),
        name="score",
    )(*pieces, pltpu.with_memory_space_constraint(head, pltpu.VMEM))


def finish_kernel(stats, place, logprob, entropy, scored, spread, sems):
    tops = stats[:, 0:1, :]
    best = jnp.max(tops, axis=0)
    total = jnp.sum(stats[:, 1:2, :] * jnp.exp(tops - best), axis=0)
    weighted = pltpu.roll(total, CODE - GROUP, 1)
    chosen = pltpu.roll(total, CODE - 2 * GROUP, 1)
    lse = best + jnp.log(total)
    lane = lax.broadcasted_iota(jnp.int32, (LIVE, CODE), 1)
    row = lax.broadcasted_iota(jnp.int32, (LIVE, CODE), 0)

    def to_slots(values):
        column = jnp.sum(jnp.where(lane == row, values, 0.0), axis=1, keepdims=True)
        return jnp.sum(place[...] * column, axis=0, keepdims=True)

    scored[...] = to_slots(chosen - lse)
    first = pltpu.make_async_copy(scored, logprob, sems.at[0])
    first.start()
    spread[...] = to_slots(lse - weighted / total)
    second = pltpu.make_async_copy(spread, entropy, sems.at[1])
    second.start()
    first.wait()
    second.wait()


def finish(stats, place, slot_count):
    vmem = pl.BlockSpec(memory_space=pltpu.VMEM)
    out = jax.ShapeDtypeStruct((1, slot_count), jnp.float32)
    return pl.pallas_call(
        finish_kernel,
        out_shape=(out, out),
        in_specs=[vmem, vmem],
        out_specs=[pl.BlockSpec(memory_space=pltpu.HBM)] * 2,
        scratch_shapes=[
            pltpu.VMEM((1, slot_count), jnp.float32),
            pltpu.VMEM((1, slot_count), jnp.float32),
            pltpu.SemaphoreType.DMA((2,)),
        ],
        compiler_params=vmem_limit(32),
        name="finish",
    )(stats, place)


def swap(x, axis, distance):
    return lax.ppermute(x, axis, [(i, i ^ distance) for i in range(lax.axis_size(axis))])


def per_device(hidden, gain, head, lengths, offsets, targets, mask):
    dp, tensor = lax.axis_size("dp"), lax.axis_size("tensor")
    rows, codes, slots, gain = pick(hidden, gain, lengths, offsets, targets, mask)
    parts = {0: rows} | {s: swap(rows, "tensor", s) for s in reversed(range(1, tensor))}
    rows = join([parts[s] for s in range(tensor)], codes, gain)

    pieces = {d: swap(rows, "dp", d) for d in reversed(range(2, dp, 2))}
    held, pieces[0] = fetch(head, rows)
    for d in range(0, dp, 2):
        pieces[d + 1] = swap(pieces[d], "dp", 1)
    stats = score([pieces[d] for d in range(dp)], held, tensor)
    stats = lax.all_to_all(stats.reshape(dp * tensor, 2, CODE), ("dp", "tensor"), 0, 0, tiled=True)
    return finish(stats, slots, offsets.shape[1])


def solution(mesh):
    return jax.shard_map(
        per_device,
        mesh=mesh,
        in_specs=(
            P("dp", None, "tensor"),
            P(),
            P(None, ("dp", "tensor")),
            P("dp"),
            P("dp", None),
            P("dp", None),
            P("dp", None),
        ),
        out_specs=(P("dp", None), P("dp", None)),
        check_vma=False,
    )
```

```python
import jax
import jax.numpy as jnp
from jax import lax
from jax.experimental import pallas as pl
from jax.experimental.pallas import tpu as pltpu
from jax.sharding import PartitionSpec as P

LIVE = 16
SPAN = 256
BLOCK = 16
CODE = 128
DIGIT = 64
GROUP = 16


def vmem_limit(mebibytes):
    return pltpu.CompilerParams(vmem_limit_bytes=mebibytes * 1024 * 1024)


def in_hbm(x):
    return pltpu.with_memory_space_constraint(x, pltpu.HBM)


def pick_kernel(
    lengths, offsets, targets, mask, gain, hidden, rows, codes, place, gain_out, window, offset, target, alive, sems
):
    slot_count = offsets.shape[1]
    depth = window.shape[0]
    first = jnp.minimum((lengths[0] - SPAN) // BLOCK * BLOCK, hidden.shape[1] - depth)
    first = pl.multiple_of(first, BLOCK)
    copies = [
        pltpu.make_async_copy(offsets, offset, sems.at[0]),
        pltpu.make_async_copy(mask, alive, sems.at[1]),
        pltpu.make_async_copy(hidden.at[0, pl.ds(first, depth)], window, sems.at[2]),
        pltpu.make_async_copy(targets, target, sems.at[3]),
        pltpu.make_async_copy(gain, gain_out, sems.at[4]),
    ]
    for copy in copies:
        copy.start()
    for copy in copies[:2]:
        copy.wait()

    def iota(shape, axis):
        return lax.broadcasted_iota(jnp.int32, shape, axis)

    square = (slot_count, slot_count)
    live = jnp.where(alive[...] != 0, 1.0, 0.0)
    column = jnp.sum(jnp.where(iota(square, 0) == iota(square, 1), live, 0.0), axis=1, keepdims=True)
    rank = jnp.sum(jnp.where(iota(square, 0) < iota(square, 1), column, 0.0), axis=0, keepdims=True)
    wide = (LIVE, slot_count)
    chosen = jnp.where(iota(wide, 0).astype(jnp.float32) == rank, jnp.broadcast_to(live, wide), 0.0)
    place[...] = chosen
    offset_in = (lengths[0] - 1 - first) - offset[...]
    wanted = jnp.sum(chosen * (offset_in + 1).astype(jnp.float32), axis=1, keepdims=True) - 1.0
    select = jnp.where(iota((LIVE, depth), 1).astype(jnp.float32) == wanted, 1.0, 0.0).astype(jnp.bfloat16)
    copies[3].wait()
    ids = jnp.sum(chosen * target[...].astype(jnp.float32), axis=1, keepdims=True).astype(jnp.int32)
    lane = iota((LIVE, CODE), 1)
    digits = jnp.where(
        lane == 0, ids % DIGIT, jnp.where(lane == 1, (ids // DIGIT) % DIGIT, jnp.where(lane == 2, ids // (DIGIT * DIGIT), 0))
    )
    codes[...] = digits.astype(jnp.float32).astype(jnp.bfloat16)
    copies[4].wait()
    copies[2].wait()
    rows[...] = jnp.dot(select, window[...], preferred_element_type=jnp.float32).astype(jnp.bfloat16)


def pick(hidden, gain, lengths, offsets, targets, mask):
    features = hidden.shape[2]
    slot_count = offsets.shape[1]
    vmem = pl.BlockSpec(memory_space=pltpu.VMEM)
    return pl.pallas_call(
        pick_kernel,
        out_shape=(
            jax.ShapeDtypeStruct((LIVE, features), jnp.bfloat16),
            jax.ShapeDtypeStruct((LIVE, CODE), jnp.bfloat16),
            jax.ShapeDtypeStruct((LIVE, slot_count), jnp.float32),
            jax.ShapeDtypeStruct((1, gain.shape[0]), jnp.float32),
        ),
        in_specs=[pl.BlockSpec(memory_space=pltpu.SMEM)] + [pl.BlockSpec(memory_space=pltpu.HBM)] * 5,
        out_specs=(vmem, vmem, vmem, vmem),
        scratch_shapes=[
            pltpu.VMEM((SPAN + BLOCK, features), jnp.bfloat16),
            pltpu.VMEM(offsets.shape, jnp.int32),
            pltpu.VMEM(offsets.shape, jnp.int32),
            pltpu.VMEM(offsets.shape, jnp.int32),
            pltpu.SemaphoreType.DMA((5,)),
        ],
        compiler_params=vmem_limit(32),
        name="pick",
    )(lengths, *map(in_hbm, (offsets, targets, mask, gain.reshape(1, -1), hidden)))


def join_kernel(*refs):
    tensor = len(refs) - 3
    parts, (codes, gain, rows) = refs[:tensor], refs[tensor:]
    live, features = parts[0].shape
    square = jnp.zeros((live, 1), jnp.float32)
    for part in parts:
        values = part[...].astype(jnp.float32)
        square += jnp.sum(values * values, axis=-1, keepdims=True)
    scale = lax.rsqrt(square / (tensor * features) + 1e-06)
    shard = lax.axis_index("tensor")
    for s, part in enumerate(parts):
        span = pl.ds(pl.multiple_of((shard ^ s) * features, features), features)
        rows[:, span] = (part[...].astype(jnp.float32) * scale * gain[:, span]).astype(jnp.bfloat16)
    rows[:, tensor * features :] = codes[...]


def join(parts, codes, gain):
    tensor = len(parts)
    live, features = parts[0].shape
    vmem = pl.BlockSpec(memory_space=pltpu.VMEM)
    return pl.pallas_call(
        join_kernel,
        out_shape=jax.ShapeDtypeStruct((live, tensor * features + CODE), jnp.bfloat16),
        in_specs=[vmem] * (tensor + 2),
        out_specs=vmem,
        compiler_params=vmem_limit(32),
        name="join",
    )(*parts, codes, gain)


def fetch_kernel(head, rows, held, rows_out, sems):
    count = sems.shape[0]
    depth = head.shape[0] // count
    copies = [
        pltpu.make_async_copy(head.at[pl.ds(i * depth, depth)], held.at[pl.ds(i * depth, depth)], sems.at[i])
        for i in range(count)
    ]
    for copy in copies:
        copy.start()
    rows_out[...] = rows[...]
    for copy in copies:
        copy.wait()


def fetch(head, rows):
    vmem = pl.BlockSpec(memory_space=pltpu.VMEM)
    return pl.pallas_call(
        fetch_kernel,
        out_shape=(pltpu.VMEM(head.shape, head.dtype), jax.ShapeDtypeStruct(rows.shape, rows.dtype)),
        in_specs=[pl.BlockSpec(memory_space=pltpu.HBM), vmem],
        out_specs=(vmem, vmem),
        scratch_shapes=[pltpu.SemaphoreType.DMA((4,))],
        compiler_params=vmem_limit(32),
        cost_estimate=pl.CostEstimate(flops=0, bytes_accessed=2 * head.size * 2, transcendentals=0),
        name="fetch",
    )(in_hbm(head), rows)


def score_kernel(*refs):
    dp = len(refs) - 2
    pieces, (head, stats) = refs[:dp], refs[dp:]
    depth, vocab_width = head.shape
    live = pieces[0].shape[0]
    row_count = dp * live
    mine = lax.axis_index("dp")
    start = (mine * stats.shape[0] + lax.axis_index("tensor")) * vocab_width

    normed = jnp.concatenate([piece[:, :depth] for piece in pieces], axis=0)
    logits = jnp.dot(normed, head[...], preferred_element_type=jnp.float32)
    digits = jnp.concatenate([piece[:, depth:] for piece in pieces], axis=0).astype(jnp.float32)
    lane = lax.broadcasted_iota(jnp.int32, (row_count, CODE), 1)
    weight = jnp.where(lane == 0, 1.0, jnp.where(lane == 1, float(DIGIT), jnp.where(lane == 2, float(DIGIT * DIGIT), 0.0)))
    target = jnp.sum(digits * weight, axis=-1, keepdims=True).astype(jnp.int32) - start
    column = lax.broadcasted_iota(jnp.int32, (row_count, vocab_width), 1)
    top = jnp.max(logits, axis=-1, keepdims=True)
    expo = jnp.exp(logits - top)
    total = jnp.sum(expo, axis=-1, keepdims=True)
    weighted = jnp.sum(expo * logits, axis=-1, keepdims=True)
    chosen = jnp.sum(jnp.where(column == target, logits, 0.0), axis=-1, keepdims=True)
    spot = lane - lax.broadcasted_iota(jnp.int32, (row_count, CODE), 0) % live
    tops = jnp.where((spot == 0) | (spot == GROUP), top, 0.0)
    sums = jnp.zeros((row_count, CODE), jnp.float32)
    for group, value in enumerate((total, weighted, chosen)):
        sums = jnp.where(spot == GROUP * group, value, sums)
    for d in range(dp):
        for line, table in enumerate((tops, sums)):
            packed = jnp.sum(table[d * live : (d + 1) * live], axis=0, keepdims=True)
            for t in range(stats.shape[0]):
                stats[t, mine ^ d, line : line + 1] = packed


def score(pieces, head, copies):
    dp = len(pieces)
    vmem = pl.BlockSpec(memory_space=pltpu.VMEM)
    return pl.pallas_call(
        score_kernel,
        out_shape=jax.ShapeDtypeStruct((copies, dp, 2, CODE), jnp.float32),
        in_specs=[vmem] * (dp + 1),
        out_specs=vmem,
        compiler_params=vmem_limit(32),
        name="score",
    )(*pieces, pltpu.with_memory_space_constraint(head, pltpu.VMEM))


def finish_kernel(stats, place, logprob, entropy, scored, spread, sems):
    tops = stats[:, 0:1, :]
    best = jnp.max(tops, axis=0)
    total = jnp.sum(stats[:, 1:2, :] * jnp.exp(tops - best), axis=0)
    weighted = pltpu.roll(total, CODE - GROUP, 1)
    chosen = pltpu.roll(total, CODE - 2 * GROUP, 1)
    lse = best + jnp.log(total)
    lane = lax.broadcasted_iota(jnp.int32, (LIVE, CODE), 1)
    row = lax.broadcasted_iota(jnp.int32, (LIVE, CODE), 0)

    def to_slots(values):
        column = jnp.sum(jnp.where(lane == row, values, 0.0), axis=1, keepdims=True)
        return jnp.sum(place[...] * column, axis=0, keepdims=True)

    scored[...] = to_slots(chosen - lse)
    first = pltpu.make_async_copy(scored, logprob, sems.at[0])
    first.start()
    spread[...] = to_slots(lse - weighted / total)
    second = pltpu.make_async_copy(spread, entropy, sems.at[1])
    second.start()
    first.wait()
    second.wait()


def finish(stats, place, slot_count):
    vmem = pl.BlockSpec(memory_space=pltpu.VMEM)
    out = jax.ShapeDtypeStruct((1, slot_count), jnp.float32)
    return pl.pallas_call(
        finish_kernel,
        out_shape=(out, out),
        in_specs=[vmem, vmem],
        out_specs=[pl.BlockSpec(memory_space=pltpu.HBM)] * 2,
        scratch_shapes=[
            pltpu.VMEM((1, slot_count), jnp.float32),
            pltpu.VMEM((1, slot_count), jnp.float32),
            pltpu.SemaphoreType.DMA((2,)),
        ],
        compiler_params=vmem_limit(32),
        name="finish",
    )(stats, place)


def swap(x, axis, distance):
    return lax.ppermute(x, axis, [(i, i ^ distance) for i in range(lax.axis_size(axis))])


def per_device(hidden, gain, head, lengths, offsets, targets, mask):
    dp, tensor = lax.axis_size("dp"), lax.axis_size("tensor")
    rows, codes, slots, gain = pick(hidden, gain, lengths, offsets, targets, mask)
    parts = {0: rows} | {s: swap(rows, "tensor", s) for s in reversed(range(1, tensor))}
    rows = join([parts[s] for s in range(tensor)], codes, gain)

    pieces = {d: swap(rows, "dp", d) for d in reversed(range(2, dp, 2))}
    held, pieces[0] = fetch(head, rows)
    for d in range(0, dp, 2):
        pieces[d + 1] = swap(pieces[d], "dp", 1)
    stats = score([pieces[d] for d in range(dp)], held, tensor)
    stats = lax.all_to_all(stats.reshape(tensor * dp, 2, CODE), ("tensor", "dp"), 0, 0, tiled=True)
    return finish(stats, slots, offsets.shape[1])


def solution(mesh):
    return jax.shard_map(
        per_device,
        mesh=mesh,
        in_specs=(
            P("dp", None, "tensor"),
            P(),
            P(None, ("dp", "tensor")),
            P("dp"),
            P("dp", None),
            P("dp", None),
            P("dp", None),
        ),
        out_specs=(P("dp", None), P("dp", None)),
        check_vma=False,
    )
```

```python
import functools

import jax
import jax.numpy as jnp
from jax import lax
from jax.experimental import pallas as pl
from jax.experimental.pallas import tpu as pltpu
from jax.sharding import PartitionSpec as P

LIVE = 16
SPAN = 256
BLOCK = 16
CODE = 128
DIGIT = 64
GROUP = 16


def vmem_limit(mebibytes):
    return pltpu.CompilerParams(vmem_limit_bytes=mebibytes * 1024 * 1024)


def in_hbm(x):
    return pltpu.with_memory_space_constraint(x, pltpu.HBM)


def pick_kernel(
    lengths, offsets, targets, mask, gain, hidden, rows, codes, place, gain_out, window, offset, target, alive, sems
):
    slot_count = offsets.shape[1]
    depth = window.shape[0]
    first = jnp.minimum((lengths[0] - SPAN) // BLOCK * BLOCK, hidden.shape[1] - depth)
    first = pl.multiple_of(first, BLOCK)
    copies = [
        pltpu.make_async_copy(offsets, offset, sems.at[0]),
        pltpu.make_async_copy(mask, alive, sems.at[1]),
        pltpu.make_async_copy(hidden.at[0, pl.ds(first, depth)], window, sems.at[2]),
        pltpu.make_async_copy(targets, target, sems.at[3]),
        pltpu.make_async_copy(gain, gain_out, sems.at[4]),
    ]
    for copy in copies:
        copy.start()
    for copy in copies[:2]:
        copy.wait()

    def iota(shape, axis):
        return lax.broadcasted_iota(jnp.int32, shape, axis)

    square = (slot_count, slot_count)
    live = jnp.where(alive[...] != 0, 1.0, 0.0)
    column = jnp.sum(jnp.where(iota(square, 0) == iota(square, 1), live, 0.0), axis=1, keepdims=True)
    rank = jnp.sum(jnp.where(iota(square, 0) < iota(square, 1), column, 0.0), axis=0, keepdims=True)
    wide = (LIVE, slot_count)
    chosen = jnp.where(iota(wide, 0).astype(jnp.float32) == rank, jnp.broadcast_to(live, wide), 0.0)
    place[...] = chosen
    offset_in = (lengths[0] - 1 - first) - offset[...]
    wanted = jnp.sum(chosen * (offset_in + 1).astype(jnp.float32), axis=1, keepdims=True) - 1.0
    select = jnp.where(iota((LIVE, depth), 1).astype(jnp.float32) == wanted, 1.0, 0.0).astype(jnp.bfloat16)
    copies[3].wait()
    ids = jnp.sum(chosen * target[...].astype(jnp.float32), axis=1, keepdims=True).astype(jnp.int32)
    lane = iota((LIVE, CODE), 1)
    digits = jnp.where(
        lane == 0, ids % DIGIT, jnp.where(lane == 1, (ids // DIGIT) % DIGIT, jnp.where(lane == 2, ids // (DIGIT * DIGIT), 0))
    )
    codes[...] = digits.astype(jnp.float32).astype(jnp.bfloat16)
    copies[4].wait()
    copies[2].wait()
    rows[...] = jnp.dot(select, window[...], preferred_element_type=jnp.float32).astype(jnp.bfloat16)


def pick(hidden, gain, lengths, offsets, targets, mask):
    features = hidden.shape[2]
    slot_count = offsets.shape[1]
    vmem = pl.BlockSpec(memory_space=pltpu.VMEM)
    return pl.pallas_call(
        pick_kernel,
        out_shape=(
            jax.ShapeDtypeStruct((LIVE, features), jnp.bfloat16),
            jax.ShapeDtypeStruct((LIVE, CODE), jnp.bfloat16),
            jax.ShapeDtypeStruct((LIVE, slot_count), jnp.float32),
            jax.ShapeDtypeStruct((1, gain.shape[0]), jnp.float32),
        ),
        in_specs=[pl.BlockSpec(memory_space=pltpu.SMEM)] + [pl.BlockSpec(memory_space=pltpu.HBM)] * 5,
        out_specs=(vmem, vmem, vmem, vmem),
        scratch_shapes=[
            pltpu.VMEM((SPAN + BLOCK, features), jnp.bfloat16),
            pltpu.VMEM(offsets.shape, jnp.int32),
            pltpu.VMEM(offsets.shape, jnp.int32),
            pltpu.VMEM(offsets.shape, jnp.int32),
            pltpu.SemaphoreType.DMA((5,)),
        ],
        compiler_params=vmem_limit(32),
        name="pick",
    )(lengths, *map(in_hbm, (offsets, targets, mask, gain.reshape(1, -1), hidden)))


def join_kernel(*refs):
    tensor = len(refs) - 3
    parts, (codes, gain, rows) = refs[:tensor], refs[tensor:]
    live, features = parts[0].shape
    square = jnp.zeros((live, 1), jnp.float32)
    for part in parts:
        values = part[...].astype(jnp.float32)
        square += jnp.sum(values * values, axis=-1, keepdims=True)
    scale = lax.rsqrt(square / (tensor * features) + 1e-06)
    shard = lax.axis_index("tensor")
    for s, part in enumerate(parts):
        span = pl.ds(pl.multiple_of((shard ^ s) * features, features), features)
        rows[:, span] = (part[...].astype(jnp.float32) * scale * gain[:, span]).astype(jnp.bfloat16)
    rows[:, tensor * features :] = codes[...]


def join(parts, codes, gain):
    tensor = len(parts)
    live, features = parts[0].shape
    vmem = pl.BlockSpec(memory_space=pltpu.VMEM)
    return pl.pallas_call(
        join_kernel,
        out_shape=jax.ShapeDtypeStruct((live, tensor * features + CODE), jnp.bfloat16),
        in_specs=[vmem] * (tensor + 2),
        out_specs=vmem,
        compiler_params=vmem_limit(32),
        name="join",
    )(*parts, codes, gain)


def fetch_kernel(head, rows, held, rows_out, sems):
    count = sems.shape[0]
    depth = head.shape[0] // count
    copies = [
        pltpu.make_async_copy(head.at[pl.ds(i * depth, depth)], held.at[pl.ds(i * depth, depth)], sems.at[i])
        for i in range(count)
    ]
    for copy in copies:
        copy.start()
    rows_out[...] = rows[...]
    for copy in copies:
        copy.wait()


def fetch(head, rows):
    vmem = pl.BlockSpec(memory_space=pltpu.VMEM)
    return pl.pallas_call(
        fetch_kernel,
        out_shape=(pltpu.VMEM(head.shape, head.dtype), jax.ShapeDtypeStruct(rows.shape, rows.dtype)),
        in_specs=[pl.BlockSpec(memory_space=pltpu.HBM), vmem],
        out_specs=(vmem, vmem),
        scratch_shapes=[pltpu.SemaphoreType.DMA((4,))],
        compiler_params=vmem_limit(32),
        cost_estimate=pl.CostEstimate(flops=0, bytes_accessed=2 * head.size * 2, transcendentals=0),
        name="fetch",
    )(in_hbm(head), rows)


def score_kernel(order, *refs):
    dp = len(order)
    pieces, (head, stats) = refs[:dp], refs[dp:]
    depth, vocab_width = head.shape
    live = pieces[0].shape[0]
    row_count = dp * live
    mine = lax.axis_index("dp")
    start = (mine * stats.shape[1] + lax.axis_index("tensor")) * vocab_width

    normed = jnp.concatenate([piece[:, :depth] for piece in pieces], axis=0)
    logits = jnp.dot(normed, head[...], preferred_element_type=jnp.float32)
    digits = jnp.concatenate([piece[:, depth:] for piece in pieces], axis=0).astype(jnp.float32)
    lane = lax.broadcasted_iota(jnp.int32, (row_count, CODE), 1)
    weight = jnp.where(lane == 0, 1.0, jnp.where(lane == 1, float(DIGIT), jnp.where(lane == 2, float(DIGIT * DIGIT), 0.0)))
    target = jnp.sum(digits * weight, axis=-1, keepdims=True).astype(jnp.int32) - start
    column = lax.broadcasted_iota(jnp.int32, (row_count, vocab_width), 1)
    top = jnp.max(logits, axis=-1, keepdims=True)
    expo = jnp.exp(logits - top)
    total = jnp.sum(expo, axis=-1, keepdims=True)
    weighted = jnp.sum(expo * logits, axis=-1, keepdims=True)
    chosen = jnp.sum(jnp.where(column == target, logits, 0.0), axis=-1, keepdims=True)
    spot = lane - lax.broadcasted_iota(jnp.int32, (row_count, CODE), 0) % live
    tops = jnp.where((spot == 0) | (spot == GROUP), top, 0.0)
    sums = jnp.zeros((row_count, CODE), jnp.float32)
    for group, value in enumerate((total, weighted, chosen)):
        sums = jnp.where(spot == GROUP * group, value, sums)
    for i, d in enumerate(order):
        for line, table in enumerate((tops, sums)):
            packed = jnp.sum(table[i * live : (i + 1) * live], axis=0, keepdims=True)
            for t in range(stats.shape[1]):
                stats[mine ^ d, t, line : line + 1] = packed


def score(pieces, order, head, copies):
    dp = len(order)
    vmem = pl.BlockSpec(memory_space=pltpu.VMEM)
    return pl.pallas_call(
        functools.partial(score_kernel, order),
        out_shape=jax.ShapeDtypeStruct((dp, copies, 2, CODE), jnp.float32),
        in_specs=[vmem] * (dp + 1),
        out_specs=vmem,
        compiler_params=vmem_limit(32),
        name="score",
    )(*pieces, pltpu.with_memory_space_constraint(head, pltpu.VMEM))


def finish_kernel(stats, place, logprob, entropy, scored, spread, sems):
    tops = stats[:, 0:1, :]
    best = jnp.max(tops, axis=0)
    total = jnp.sum(stats[:, 1:2, :] * jnp.exp(tops - best), axis=0)
    weighted = pltpu.roll(total, CODE - GROUP, 1)
    chosen = pltpu.roll(total, CODE - 2 * GROUP, 1)
    lse = best + jnp.log(total)
    lane = lax.broadcasted_iota(jnp.int32, (LIVE, CODE), 1)
    row = lax.broadcasted_iota(jnp.int32, (LIVE, CODE), 0)

    def to_slots(values):
        column = jnp.sum(jnp.where(lane == row, values, 0.0), axis=1, keepdims=True)
        return jnp.sum(place[...] * column, axis=0, keepdims=True)

    scored[...] = to_slots(chosen - lse)
    first = pltpu.make_async_copy(scored, logprob, sems.at[0])
    first.start()
    spread[...] = to_slots(lse - weighted / total)
    second = pltpu.make_async_copy(spread, entropy, sems.at[1])
    second.start()
    first.wait()
    second.wait()


def finish(stats, place, slot_count):
    vmem = pl.BlockSpec(memory_space=pltpu.VMEM)
    out = jax.ShapeDtypeStruct((1, slot_count), jnp.float32)
    return pl.pallas_call(
        finish_kernel,
        out_shape=(out, out),
        in_specs=[vmem, vmem],
        out_specs=[pl.BlockSpec(memory_space=pltpu.HBM)] * 2,
        scratch_shapes=[
            pltpu.VMEM((1, slot_count), jnp.float32),
            pltpu.VMEM((1, slot_count), jnp.float32),
            pltpu.SemaphoreType.DMA((2,)),
        ],
        compiler_params=vmem_limit(32),
        name="finish",
    )(stats, place)


def swap(x, axis, distance):
    return lax.ppermute(x, axis, [(i, i ^ distance) for i in range(lax.axis_size(axis))])


def per_device(hidden, gain, head, lengths, offsets, targets, mask):
    dp, tensor = lax.axis_size("dp"), lax.axis_size("tensor")
    rows, codes, slots, gain = pick(hidden, gain, lengths, offsets, targets, mask)
    parts = {0: rows} | {s: swap(rows, "tensor", s) for s in reversed(range(1, tensor))}
    rows = join([parts[s] for s in range(tensor)], codes, gain)

    pieces = {d: swap(rows, "dp", d) for d in reversed(range(2, dp, 2))}
    held, pieces[0] = fetch(head, rows)
    for d in range(0, dp, 2):
        pieces[d + 1] = swap(pieces[d], "dp", 1)
    order = [0, 1, *range(4, dp - 2), 2, 3, dp - 2, dp - 1]
    stats = score([pieces[d] for d in order], order, held, tensor)
    stats = lax.all_to_all(stats.reshape(dp * tensor, 2, CODE), ("dp", "tensor"), 0, 0, tiled=True)
    return finish(stats, slots, offsets.shape[1])


def solution(mesh):
    return jax.shard_map(
        per_device,
        mesh=mesh,
        in_specs=(
            P("dp", None, "tensor"),
            P(),
            P(None, ("dp", "tensor")),
            P("dp"),
            P("dp", None),
            P("dp", None),
            P("dp", None),
        ),
        out_specs=(P("dp", None), P("dp", None)),
        check_vma=False,
    )
```

```python
import functools

import jax
import jax.numpy as jnp
from jax import lax
from jax.experimental import pallas as pl
from jax.experimental.pallas import tpu as pltpu
from jax.sharding import PartitionSpec as P

LIVE = 16
SPAN = 256
BLOCK = 16
CODE = 128
DIGIT = 64
GROUP = 16


def vmem_limit(mebibytes):
    return pltpu.CompilerParams(vmem_limit_bytes=mebibytes * 1024 * 1024)


def in_hbm(x):
    return pltpu.with_memory_space_constraint(x, pltpu.HBM)


def pick_kernel(
    lengths, offsets, targets, mask, gain, hidden, rows, codes, place, gain_out, window, offset, target, alive, sems
):
    slot_count = offsets.shape[1]
    depth = window.shape[0]
    first = jnp.minimum((lengths[0] - SPAN) // BLOCK * BLOCK, hidden.shape[1] - depth)
    first = pl.multiple_of(first, BLOCK)
    copies = [
        pltpu.make_async_copy(offsets, offset, sems.at[0]),
        pltpu.make_async_copy(mask, alive, sems.at[1]),
        pltpu.make_async_copy(hidden.at[0, pl.ds(first, depth)], window, sems.at[2]),
        pltpu.make_async_copy(targets, target, sems.at[3]),
        pltpu.make_async_copy(gain, gain_out, sems.at[4]),
    ]
    for copy in copies:
        copy.start()
    for copy in copies[:2]:
        copy.wait()

    def iota(shape, axis):
        return lax.broadcasted_iota(jnp.int32, shape, axis)

    square = (slot_count, slot_count)
    live = jnp.where(alive[...] != 0, 1.0, 0.0)
    column = jnp.sum(jnp.where(iota(square, 0) == iota(square, 1), live, 0.0), axis=1, keepdims=True)
    rank = jnp.sum(jnp.where(iota(square, 0) < iota(square, 1), column, 0.0), axis=0, keepdims=True)
    wide = (LIVE, slot_count)
    chosen = jnp.where(iota(wide, 0).astype(jnp.float32) == rank, jnp.broadcast_to(live, wide), 0.0)
    place[...] = chosen
    offset_in = (lengths[0] - 1 - first) - offset[...]
    wanted = jnp.sum(chosen * (offset_in + 1).astype(jnp.float32), axis=1, keepdims=True) - 1.0
    select = jnp.where(iota((LIVE, depth), 1).astype(jnp.float32) == wanted, 1.0, 0.0).astype(jnp.bfloat16)
    copies[3].wait()
    ids = jnp.sum(chosen * target[...].astype(jnp.float32), axis=1, keepdims=True).astype(jnp.int32)
    lane = iota((LIVE, CODE), 1)
    digits = jnp.where(
        lane == 0, ids % DIGIT, jnp.where(lane == 1, (ids // DIGIT) % DIGIT, jnp.where(lane == 2, ids // (DIGIT * DIGIT), 0))
    )
    codes[...] = digits.astype(jnp.float32).astype(jnp.bfloat16)
    copies[4].wait()
    copies[2].wait()
    rows[...] = jnp.dot(select, window[...], preferred_element_type=jnp.float32).astype(jnp.bfloat16)


def pick(hidden, gain, lengths, offsets, targets, mask):
    features = hidden.shape[2]
    slot_count = offsets.shape[1]
    vmem = pl.BlockSpec(memory_space=pltpu.VMEM)
    return pl.pallas_call(
        pick_kernel,
        out_shape=(
            jax.ShapeDtypeStruct((LIVE, features), jnp.bfloat16),
            jax.ShapeDtypeStruct((LIVE, CODE), jnp.bfloat16),
            jax.ShapeDtypeStruct((LIVE, slot_count), jnp.float32),
            jax.ShapeDtypeStruct((1, gain.shape[0]), jnp.float32),
        ),
        in_specs=[pl.BlockSpec(memory_space=pltpu.SMEM)] + [pl.BlockSpec(memory_space=pltpu.HBM)] * 5,
        out_specs=(vmem, vmem, vmem, vmem),
        scratch_shapes=[
            pltpu.VMEM((SPAN + BLOCK, features), jnp.bfloat16),
            pltpu.VMEM(offsets.shape, jnp.int32),
            pltpu.VMEM(offsets.shape, jnp.int32),
            pltpu.VMEM(offsets.shape, jnp.int32),
            pltpu.SemaphoreType.DMA((5,)),
        ],
        compiler_params=vmem_limit(32),
        name="pick",
    )(lengths, *map(in_hbm, (offsets, targets, mask, gain.reshape(1, -1), hidden)))


def join_kernel(*refs):
    tensor = len(refs) - 3
    parts, (codes, gain, rows) = refs[:tensor], refs[tensor:]
    live, features = parts[0].shape
    square = jnp.zeros((live, 1), jnp.float32)
    for part in parts:
        values = part[...].astype(jnp.float32)
        square += jnp.sum(values * values, axis=-1, keepdims=True)
    scale = lax.rsqrt(square / (tensor * features) + 1e-06)
    shard = lax.axis_index("tensor")
    for s, part in enumerate(parts):
        span = pl.ds(pl.multiple_of((shard ^ s) * features, features), features)
        rows[:, span] = (part[...].astype(jnp.float32) * scale * gain[:, span]).astype(jnp.bfloat16)
    rows[:, tensor * features :] = codes[...]


def join(parts, codes, gain):
    tensor = len(parts)
    live, features = parts[0].shape
    vmem = pl.BlockSpec(memory_space=pltpu.VMEM)
    return pl.pallas_call(
        join_kernel,
        out_shape=jax.ShapeDtypeStruct((live, tensor * features + CODE), jnp.bfloat16),
        in_specs=[vmem] * (tensor + 2),
        out_specs=vmem,
        compiler_params=vmem_limit(32),
        name="join",
    )(*parts, codes, gain)


def fetch_kernel(head, rows, held, rows_out, sems):
    count = sems.shape[0]
    depth = head.shape[0] // count
    copies = [
        pltpu.make_async_copy(head.at[pl.ds(i * depth, depth)], held.at[pl.ds(i * depth, depth)], sems.at[i])
        for i in range(count)
    ]
    for copy in copies:
        copy.start()
    rows_out[...] = rows[...]
    for copy in copies:
        copy.wait()


def fetch(head, rows):
    vmem = pl.BlockSpec(memory_space=pltpu.VMEM)
    return pl.pallas_call(
        fetch_kernel,
        out_shape=(pltpu.VMEM(head.shape, head.dtype), jax.ShapeDtypeStruct(rows.shape, rows.dtype)),
        in_specs=[pl.BlockSpec(memory_space=pltpu.HBM), vmem],
        out_specs=(vmem, vmem),
        scratch_shapes=[pltpu.SemaphoreType.DMA((4,))],
        compiler_params=vmem_limit(32),
        cost_estimate=pl.CostEstimate(flops=0, bytes_accessed=2 * head.size * 2, transcendentals=0),
        name="fetch",
    )(in_hbm(head), rows)


def stack_kernel(*refs):
    *pieces, _, out = refs
    live = pieces[0].shape[0]
    for i, piece in enumerate(pieces):
        out[i * live : (i + 1) * live] = piece[...]


def stack(pieces, after):
    live, width = pieces[0].shape
    vmem = pl.BlockSpec(memory_space=pltpu.VMEM)
    return pl.pallas_call(
        stack_kernel,
        out_shape=jax.ShapeDtypeStruct((len(pieces) * live, width), pieces[0].dtype),
        in_specs=[vmem] * (len(pieces) + 1),
        out_specs=vmem,
        compiler_params=vmem_limit(32),
        name="stack",
    )(*pieces, after)


def score_kernel(order, *refs):
    dp = len(order)
    pieces, (head, stats) = refs[:-2], refs[-2:]
    depth, vocab_width = head.shape
    live = pieces[0].shape[0]
    row_count = dp * live
    mine = lax.axis_index("dp")
    start = (mine * stats.shape[1] + lax.axis_index("tensor")) * vocab_width

    normed = jnp.concatenate([piece[:, :depth] for piece in pieces], axis=0)
    logits = jnp.dot(normed, head[...], preferred_element_type=jnp.float32)
    digits = jnp.concatenate([piece[:, depth:] for piece in pieces], axis=0).astype(jnp.float32)
    lane = lax.broadcasted_iota(jnp.int32, (row_count, CODE), 1)
    weight = jnp.where(lane == 0, 1.0, jnp.where(lane == 1, float(DIGIT), jnp.where(lane == 2, float(DIGIT * DIGIT), 0.0)))
    target = jnp.sum(digits * weight, axis=-1, keepdims=True).astype(jnp.int32) - start
    column = lax.broadcasted_iota(jnp.int32, (row_count, vocab_width), 1)
    top = jnp.max(logits, axis=-1, keepdims=True)
    expo = jnp.exp(logits - top)
    total = jnp.sum(expo, axis=-1, keepdims=True)
    weighted = jnp.sum(expo * logits, axis=-1, keepdims=True)
    chosen = jnp.sum(jnp.where(column == target, logits, 0.0), axis=-1, keepdims=True)
    spot = lane - lax.broadcasted_iota(jnp.int32, (row_count, CODE), 0) % live
    tops = jnp.where((spot == 0) | (spot == GROUP), top, 0.0)
    sums = jnp.zeros((row_count, CODE), jnp.float32)
    for group, value in enumerate((total, weighted, chosen)):
        sums = jnp.where(spot == GROUP * group, value, sums)
    for i, d in enumerate(order):
        for line, table in enumerate((tops, sums)):
            packed = jnp.sum(table[i * live : (i + 1) * live], axis=0, keepdims=True)
            for t in range(stats.shape[1]):
                stats[mine ^ d, t, line : line + 1] = packed


def score(pieces, order, head, copies):
    dp = len(order)
    vmem = pl.BlockSpec(memory_space=pltpu.VMEM)
    return pl.pallas_call(
        functools.partial(score_kernel, order),
        out_shape=jax.ShapeDtypeStruct((dp, copies, 2, CODE), jnp.float32),
        in_specs=[vmem] * (len(pieces) + 1),
        out_specs=vmem,
        compiler_params=vmem_limit(32),
        name="score",
    )(*pieces, pltpu.with_memory_space_constraint(head, pltpu.VMEM))


def finish_kernel(stats, place, logprob, entropy, scored, spread, sems):
    tops = stats[:, 0:1, :]
    best = jnp.max(tops, axis=0)
    total = jnp.sum(stats[:, 1:2, :] * jnp.exp(tops - best), axis=0)
    weighted = pltpu.roll(total, CODE - GROUP, 1)
    chosen = pltpu.roll(total, CODE - 2 * GROUP, 1)
    lse = best + jnp.log(total)
    lane = lax.broadcasted_iota(jnp.int32, (LIVE, CODE), 1)
    row = lax.broadcasted_iota(jnp.int32, (LIVE, CODE), 0)

    def to_slots(values):
        column = jnp.sum(jnp.where(lane == row, values, 0.0), axis=1, keepdims=True)
        return jnp.sum(place[...] * column, axis=0, keepdims=True)

    scored[...] = to_slots(chosen - lse)
    first = pltpu.make_async_copy(scored, logprob, sems.at[0])
    first.start()
    spread[...] = to_slots(lse - weighted / total)
    second = pltpu.make_async_copy(spread, entropy, sems.at[1])
    second.start()
    first.wait()
    second.wait()


def finish(stats, place, slot_count):
    vmem = pl.BlockSpec(memory_space=pltpu.VMEM)
    out = jax.ShapeDtypeStruct((1, slot_count), jnp.float32)
    return pl.pallas_call(
        finish_kernel,
        out_shape=(out, out),
        in_specs=[vmem, vmem],
        out_specs=[pl.BlockSpec(memory_space=pltpu.HBM)] * 2,
        scratch_shapes=[
            pltpu.VMEM((1, slot_count), jnp.float32),
            pltpu.VMEM((1, slot_count), jnp.float32),
            pltpu.SemaphoreType.DMA((2,)),
        ],
        compiler_params=vmem_limit(32),
        name="finish",
    )(stats, place)


def swap(x, axis, distance):
    return lax.ppermute(x, axis, [(i, i ^ distance) for i in range(lax.axis_size(axis))])


def per_device(hidden, gain, head, lengths, offsets, targets, mask):
    dp, tensor = lax.axis_size("dp"), lax.axis_size("tensor")
    rows, codes, slots, gain = pick(hidden, gain, lengths, offsets, targets, mask)
    parts = {0: rows} | {s: swap(rows, "tensor", s) for s in reversed(range(1, tensor))}
    rows = join([parts[s] for s in range(tensor)], codes, gain)

    pieces = {d: swap(rows, "dp", d) for d in reversed(range(2, dp, 2))}
    held, pieces[0] = fetch(head, rows)
    far, near = 2, range(4, dp, 2)
    for d in (0, far):
        pieces[d + 1] = swap(pieces[d], "dp", 1)
    partner = swap(stack([pieces[d] for d in near], pieces[0]), "dp", 1)
    order = [0, 1, far, far + 1, *near, *(d + 1 for d in near)]
    stats = score([pieces[d] for d in order[: -len(near)]] + [partner], order, held, tensor)
    stats = lax.all_to_all(stats.reshape(dp * tensor, 2, CODE), ("dp", "tensor"), 0, 0, tiled=True)
    return finish(stats, slots, offsets.shape[1])


def solution(mesh):
    return jax.shard_map(
        per_device,
        mesh=mesh,
        in_specs=(
            P("dp", None, "tensor"),
            P(),
            P(None, ("dp", "tensor")),
            P("dp"),
            P("dp", None),
            P("dp", None),
            P("dp", None),
        ),
        out_specs=(P("dp", None), P("dp", None)),
        check_vma=False,
    )
```

```python
import jax
import jax.numpy as jnp
from jax import lax
from jax.experimental import pallas as pl
from jax.experimental.pallas import tpu as pltpu
from jax.sharding import PartitionSpec as P

LIVE = 16
SPAN = 256
BLOCK = 16
CODE = 128
DIGIT = 64
GROUP = 16


def vmem_limit(mebibytes):
    return pltpu.CompilerParams(vmem_limit_bytes=mebibytes * 1024 * 1024)


def in_hbm(x):
    return pltpu.with_memory_space_constraint(x, pltpu.HBM)


def pick_kernel(
    lengths, offsets, targets, mask, gain, hidden, rows, codes, place, gain_out, window, offset, target, alive, sems
):
    slot_count = offsets.shape[1]
    depth = window.shape[0]
    first = jnp.minimum((lengths[0] - SPAN) // BLOCK * BLOCK, hidden.shape[1] - depth)
    first = pl.multiple_of(first, BLOCK)
    copies = [
        pltpu.make_async_copy(offsets, offset, sems.at[0]),
        pltpu.make_async_copy(mask, alive, sems.at[1]),
        pltpu.make_async_copy(hidden.at[0, pl.ds(first, depth)], window, sems.at[2]),
        pltpu.make_async_copy(targets, target, sems.at[3]),
        pltpu.make_async_copy(gain, gain_out, sems.at[4]),
    ]
    for copy in copies:
        copy.start()
    for copy in copies[:2]:
        copy.wait()

    def iota(shape, axis):
        return lax.broadcasted_iota(jnp.int32, shape, axis)

    square = (slot_count, slot_count)
    live = jnp.where(alive[...] != 0, 1.0, 0.0)
    column = jnp.sum(jnp.where(iota(square, 0) == iota(square, 1), live, 0.0), axis=1, keepdims=True)
    rank = jnp.sum(jnp.where(iota(square, 0) < iota(square, 1), column, 0.0), axis=0, keepdims=True)
    wide = (LIVE, slot_count)
    chosen = jnp.where(iota(wide, 0).astype(jnp.float32) == rank, jnp.broadcast_to(live, wide), 0.0)
    place[...] = chosen
    offset_in = (lengths[0] - 1 - first) - offset[...]
    wanted = jnp.sum(chosen * (offset_in + 1).astype(jnp.float32), axis=1, keepdims=True) - 1.0
    select = jnp.where(iota((LIVE, depth), 1).astype(jnp.float32) == wanted, 1.0, 0.0).astype(jnp.bfloat16)
    copies[3].wait()
    ids = jnp.sum(chosen * target[...].astype(jnp.float32), axis=1, keepdims=True).astype(jnp.int32)
    lane = iota((LIVE, CODE), 1)
    digits = jnp.where(
        lane == 0, ids % DIGIT, jnp.where(lane == 1, (ids // DIGIT) % DIGIT, jnp.where(lane == 2, ids // (DIGIT * DIGIT), 0))
    )
    codes[...] = digits.astype(jnp.float32).astype(jnp.bfloat16)
    copies[4].wait()
    copies[2].wait()
    rows[...] = jnp.dot(select, window[...], preferred_element_type=jnp.float32).astype(jnp.bfloat16)


def pick(hidden, gain, lengths, offsets, targets, mask):
    features = hidden.shape[2]
    slot_count = offsets.shape[1]
    vmem = pl.BlockSpec(memory_space=pltpu.VMEM)
    return pl.pallas_call(
        pick_kernel,
        out_shape=(
            jax.ShapeDtypeStruct((LIVE, features), jnp.bfloat16),
            jax.ShapeDtypeStruct((LIVE, CODE), jnp.bfloat16),
            jax.ShapeDtypeStruct((LIVE, slot_count), jnp.float32),
            jax.ShapeDtypeStruct((1, gain.shape[0]), jnp.float32),
        ),
        in_specs=[pl.BlockSpec(memory_space=pltpu.SMEM)] + [pl.BlockSpec(memory_space=pltpu.HBM)] * 5,
        out_specs=(vmem, vmem, vmem, vmem),
        scratch_shapes=[
            pltpu.VMEM((SPAN + BLOCK, features), jnp.bfloat16),
            pltpu.VMEM(offsets.shape, jnp.int32),
            pltpu.VMEM(offsets.shape, jnp.int32),
            pltpu.VMEM(offsets.shape, jnp.int32),
            pltpu.SemaphoreType.DMA((5,)),
        ],
        compiler_params=vmem_limit(32),
        name="pick",
    )(lengths, *map(in_hbm, (offsets, targets, mask, gain.reshape(1, -1), hidden)))


def join_kernel(*refs):
    tensor = len(refs) - 3
    parts, (codes, gain, rows) = refs[:tensor], refs[tensor:]
    live, features = parts[0].shape
    square = jnp.zeros((live, 1), jnp.float32)
    for part in parts:
        values = part[...].astype(jnp.float32)
        square += jnp.sum(values * values, axis=-1, keepdims=True)
    scale = lax.rsqrt(square / (tensor * features) + 1e-06)
    shard = lax.axis_index("tensor")
    for s, part in enumerate(parts):
        span = pl.ds(pl.multiple_of((shard ^ s) * features, features), features)
        rows[:, span] = (part[...].astype(jnp.float32) * scale * gain[:, span]).astype(jnp.bfloat16)
    rows[:, tensor * features :] = codes[...]


def join(parts, codes, gain):
    tensor = len(parts)
    live, features = parts[0].shape
    vmem = pl.BlockSpec(memory_space=pltpu.VMEM)
    return pl.pallas_call(
        join_kernel,
        out_shape=jax.ShapeDtypeStruct((live, tensor * features + CODE), jnp.bfloat16),
        in_specs=[vmem] * (tensor + 2),
        out_specs=vmem,
        compiler_params=vmem_limit(32),
        name="join",
    )(*parts, codes, gain)


def fetch_kernel(head, rows, held, rows_out, sems):
    count = sems.shape[0]
    depth = head.shape[0] // count
    copies = [
        pltpu.make_async_copy(head.at[pl.ds(i * depth, depth)], held.at[pl.ds(i * depth, depth)], sems.at[i])
        for i in range(count)
    ]
    for copy in copies:
        copy.start()
    rows_out[...] = rows[...]
    for copy in copies:
        copy.wait()


def fetch(head, rows):
    vmem = pl.BlockSpec(memory_space=pltpu.VMEM)
    return pl.pallas_call(
        fetch_kernel,
        out_shape=(pltpu.VMEM(head.shape, head.dtype), jax.ShapeDtypeStruct(rows.shape, rows.dtype)),
        in_specs=[pl.BlockSpec(memory_space=pltpu.HBM), vmem],
        out_specs=(vmem, vmem),
        scratch_shapes=[pltpu.SemaphoreType.DMA((4,))],
        compiler_params=vmem_limit(32),
        cost_estimate=pl.CostEstimate(flops=0, bytes_accessed=2 * head.size * 2, transcendentals=0),
        name="fetch",
    )(in_hbm(head), rows)


def score_kernel(*refs):
    dp = len(refs) - 2
    pieces, (head, stats) = refs[:dp], refs[dp:]
    depth, vocab_width = head.shape
    live = pieces[0].shape[0]
    row_count = dp * live
    mine = lax.axis_index("dp")
    start = (mine * stats.shape[1] + lax.axis_index("tensor")) * vocab_width

    normed = jnp.concatenate([piece[:, :depth] for piece in pieces], axis=0)
    logits = jnp.dot(normed, head[...], preferred_element_type=jnp.float32)
    digits = jnp.concatenate([piece[:, depth:] for piece in pieces], axis=0).astype(jnp.float32)
    lane = lax.broadcasted_iota(jnp.int32, (row_count, CODE), 1)
    weight = jnp.where(lane == 0, 1.0, jnp.where(lane == 1, float(DIGIT), jnp.where(lane == 2, float(DIGIT * DIGIT), 0.0)))
    target = jnp.sum(digits * weight, axis=-1, keepdims=True).astype(jnp.int32) - start
    column = lax.broadcasted_iota(jnp.int32, (row_count, vocab_width), 1)
    top = jnp.max(logits, axis=-1, keepdims=True)
    expo = jnp.exp(logits - top)
    total = jnp.sum(expo, axis=-1, keepdims=True)
    weighted = jnp.sum(expo * logits, axis=-1, keepdims=True)
    chosen = jnp.sum(jnp.where(column == target, logits, 0.0), axis=-1, keepdims=True)
    spot = lane - lax.broadcasted_iota(jnp.int32, (row_count, CODE), 0) % live
    tops = jnp.where((spot == 0) | (spot == GROUP), top, 0.0)
    sums = jnp.zeros((row_count, CODE), jnp.float32)
    for group, value in enumerate((total, weighted, chosen)):
        sums = jnp.where(spot == GROUP * group, value, sums)
    for d in range(dp):
        for line, table in enumerate((tops, sums)):
            packed = jnp.sum(table[d * live : (d + 1) * live], axis=0, keepdims=True)
            for t in range(stats.shape[1]):
                stats[mine ^ d, t, line : line + 1] = packed


def score(pieces, head, copies):
    dp = len(pieces)
    vmem = pl.BlockSpec(memory_space=pltpu.VMEM)
    return pl.pallas_call(
        score_kernel,
        out_shape=jax.ShapeDtypeStruct((dp, copies, 2, CODE), jnp.float32),
        in_specs=[vmem] * (dp + 1),
        out_specs=vmem,
        compiler_params=vmem_limit(32),
        name="score",
    )(*pieces, pltpu.with_memory_space_constraint(head, pltpu.VMEM))


def finish_kernel(stats, place, logprob, entropy, scored, spread, sems):
    tops = stats[:, 0:1, :]
    best = jnp.max(tops, axis=0)
    total = jnp.sum(stats[:, 1:2, :] * jnp.exp(tops - best), axis=0)
    weighted = pltpu.roll(total, CODE - GROUP, 1)
    chosen = pltpu.roll(total, CODE - 2 * GROUP, 1)
    lse = best + jnp.log(total)
    lane = lax.broadcasted_iota(jnp.int32, (LIVE, CODE), 1)
    row = lax.broadcasted_iota(jnp.int32, (LIVE, CODE), 0)

    def to_slots(values):
        column = jnp.sum(jnp.where(lane == row, values, 0.0), axis=1, keepdims=True)
        return jnp.sum(place[...] * column, axis=0, keepdims=True)

    scored[...] = to_slots(chosen - lse)
    first = pltpu.make_async_copy(scored, logprob, sems.at[0])
    first.start()
    spread[...] = to_slots(lse - weighted / total)
    second = pltpu.make_async_copy(spread, entropy, sems.at[1])
    second.start()
    first.wait()
    second.wait()


def finish(stats, place, slot_count):
    vmem = pl.BlockSpec(memory_space=pltpu.VMEM)
    out = jax.ShapeDtypeStruct((1, slot_count), jnp.float32)
    return pl.pallas_call(
        finish_kernel,
        out_shape=(out, out),
        in_specs=[vmem, vmem],
        out_specs=[pl.BlockSpec(memory_space=pltpu.HBM)] * 2,
        scratch_shapes=[
            pltpu.VMEM((1, slot_count), jnp.float32),
            pltpu.VMEM((1, slot_count), jnp.float32),
            pltpu.SemaphoreType.DMA((2,)),
        ],
        compiler_params=vmem_limit(32),
        name="finish",
    )(stats, place)


def swap(x, axis, distance):
    return lax.ppermute(x, axis, [(i, i ^ distance) for i in range(lax.axis_size(axis))])


def per_device(hidden, gain, head, lengths, offsets, targets, mask):
    dp, tensor = lax.axis_size("dp"), lax.axis_size("tensor")
    rows, codes, slots, gain = pick(hidden, gain, lengths, offsets, targets, mask)
    parts = {0: rows} | {s: swap(rows, "tensor", s) for s in reversed(range(1, tensor))}
    held, codes = fetch(head, codes)
    rows = join([parts[s] for s in range(tensor)], codes, gain)

    pieces = {d: swap(rows, "dp", d) for d in reversed(range(2, dp, 2))}
    pieces[0] = rows
    for d in range(0, dp, 2):
        pieces[d + 1] = swap(pieces[d], "dp", 1)
    stats = score([pieces[d] for d in range(dp)], held, tensor)
    stats = lax.all_to_all(stats.reshape(dp * tensor, 2, CODE), ("dp", "tensor"), 0, 0, tiled=True)
    return finish(stats, slots, offsets.shape[1])


def solution(mesh):
    return jax.shard_map(
        per_device,
        mesh=mesh,
        in_specs=(
            P("dp", None, "tensor"),
            P(),
            P(None, ("dp", "tensor")),
            P("dp"),
            P("dp", None),
            P("dp", None),
            P("dp", None),
        ),
        out_specs=(P("dp", None), P("dp", None)),
        check_vma=False,
    )
```

```python
import jax
import jax.numpy as jnp
from jax import lax
from jax.experimental import pallas as pl
from jax.experimental.pallas import tpu as pltpu
from jax.sharding import PartitionSpec as P

LIVE = 16
SPAN = 256
BLOCK = 16
CODE = 128
DIGIT = 64
GROUP = 16


def vmem_limit(mebibytes):
    return pltpu.CompilerParams(vmem_limit_bytes=mebibytes * 1024 * 1024)


def in_hbm(x):
    return pltpu.with_memory_space_constraint(x, pltpu.HBM)


def pick_kernel(
    lengths, offsets, targets, mask, gain, hidden, rows, codes, place, gain_out, window, offset, target, alive, sems
):
    slot_count = offsets.shape[1]
    depth = window.shape[0]
    first = jnp.minimum((lengths[0] - SPAN) // BLOCK * BLOCK, hidden.shape[1] - depth)
    first = pl.multiple_of(first, BLOCK)
    copies = [
        pltpu.make_async_copy(offsets, offset, sems.at[0]),
        pltpu.make_async_copy(mask, alive, sems.at[1]),
        pltpu.make_async_copy(hidden.at[0, pl.ds(first, depth)], window, sems.at[2]),
        pltpu.make_async_copy(targets, target, sems.at[3]),
        pltpu.make_async_copy(gain, gain_out, sems.at[4]),
    ]
    for copy in copies:
        copy.start()
    for copy in copies[:2]:
        copy.wait()

    def iota(shape, axis):
        return lax.broadcasted_iota(jnp.int32, shape, axis)

    square = (slot_count, slot_count)
    live = jnp.where(alive[...] != 0, 1.0, 0.0)
    column = jnp.sum(jnp.where(iota(square, 0) == iota(square, 1), live, 0.0), axis=1, keepdims=True)
    rank = jnp.sum(jnp.where(iota(square, 0) < iota(square, 1), column, 0.0), axis=0, keepdims=True)
    wide = (LIVE, slot_count)
    chosen = jnp.where(iota(wide, 0).astype(jnp.float32) == rank, jnp.broadcast_to(live, wide), 0.0)
    place[...] = chosen
    offset_in = (lengths[0] - 1 - first) - offset[...]
    wanted = jnp.sum(chosen * (offset_in + 1).astype(jnp.float32), axis=1, keepdims=True) - 1.0
    select = jnp.where(iota((LIVE, depth), 1).astype(jnp.float32) == wanted, 1.0, 0.0).astype(jnp.bfloat16)
    copies[3].wait()
    ids = jnp.sum(chosen * target[...].astype(jnp.float32), axis=1, keepdims=True).astype(jnp.int32)
    lane = iota((LIVE, CODE), 1)
    digits = jnp.where(
        lane == 0, ids % DIGIT, jnp.where(lane == 1, (ids // DIGIT) % DIGIT, jnp.where(lane == 2, ids // (DIGIT * DIGIT), 0))
    )
    codes[...] = digits.astype(jnp.float32).astype(jnp.bfloat16)
    copies[4].wait()
    copies[2].wait()
    rows[...] = jnp.dot(select, window[...], preferred_element_type=jnp.float32).astype(jnp.bfloat16)


def pick(hidden, gain, lengths, offsets, targets, mask):
    features = hidden.shape[2]
    slot_count = offsets.shape[1]
    vmem = pl.BlockSpec(memory_space=pltpu.VMEM)
    return pl.pallas_call(
        pick_kernel,
        out_shape=(
            jax.ShapeDtypeStruct((LIVE, features), jnp.bfloat16),
            jax.ShapeDtypeStruct((LIVE, CODE), jnp.bfloat16),
            jax.ShapeDtypeStruct((LIVE, slot_count), jnp.float32),
            jax.ShapeDtypeStruct((1, gain.shape[0]), jnp.float32),
        ),
        in_specs=[pl.BlockSpec(memory_space=pltpu.SMEM)] + [pl.BlockSpec(memory_space=pltpu.HBM)] * 5,
        out_specs=(vmem, vmem, vmem, vmem),
        scratch_shapes=[
            pltpu.VMEM((SPAN + BLOCK, features), jnp.bfloat16),
            pltpu.VMEM(offsets.shape, jnp.int32),
            pltpu.VMEM(offsets.shape, jnp.int32),
            pltpu.VMEM(offsets.shape, jnp.int32),
            pltpu.SemaphoreType.DMA((5,)),
        ],
        compiler_params=vmem_limit(32),
        name="pick",
    )(lengths, *map(in_hbm, (offsets, targets, mask, gain.reshape(1, -1), hidden)))


def join_kernel(*refs):
    tensor = len(refs) - 3
    parts, (codes, gain, rows) = refs[:tensor], refs[tensor:]
    live, features = parts[0].shape
    square = jnp.zeros((live, 1), jnp.float32)
    for part in parts:
        values = part[...].astype(jnp.float32)
        square += jnp.sum(values * values, axis=-1, keepdims=True)
    scale = lax.rsqrt(square / (tensor * features) + 1e-06)
    shard = lax.axis_index("tensor")
    for s, part in enumerate(parts):
        span = pl.ds(pl.multiple_of((shard ^ s) * features, features), features)
        rows[:, span] = (part[...].astype(jnp.float32) * scale * gain[:, span]).astype(jnp.bfloat16)
    rows[:, tensor * features :] = codes[...]


def join(parts, codes, gain):
    tensor = len(parts)
    live, features = parts[0].shape
    vmem = pl.BlockSpec(memory_space=pltpu.VMEM)
    return pl.pallas_call(
        join_kernel,
        out_shape=jax.ShapeDtypeStruct((live, tensor * features + CODE), jnp.bfloat16),
        in_specs=[vmem] * (tensor + 2),
        out_specs=vmem,
        compiler_params=vmem_limit(32),
        name="join",
    )(*parts, codes, gain)


def fetch_kernel(head, rows, held, rows_out, sems):
    count = sems.shape[0]
    depth = head.shape[0] // count
    copies = [
        pltpu.make_async_copy(head.at[pl.ds(i * depth, depth)], held.at[pl.ds(i * depth, depth)], sems.at[i])
        for i in range(count)
    ]
    for copy in copies:
        copy.start()
    rows_out[...] = rows[...]
    for copy in copies:
        copy.wait()


def fetch(head, rows):
    vmem = pl.BlockSpec(memory_space=pltpu.VMEM)
    return pl.pallas_call(
        fetch_kernel,
        out_shape=(pltpu.VMEM(head.shape, head.dtype), jax.ShapeDtypeStruct(rows.shape, rows.dtype)),
        in_specs=[pl.BlockSpec(memory_space=pltpu.HBM), vmem],
        out_specs=(vmem, vmem),
        scratch_shapes=[pltpu.SemaphoreType.DMA((8,))],
        compiler_params=vmem_limit(32),
        cost_estimate=pl.CostEstimate(flops=0, bytes_accessed=2 * head.size * 2, transcendentals=0),
        name="fetch",
    )(in_hbm(head), rows)


def score_kernel(*refs):
    dp = len(refs) - 2
    pieces, (head, stats) = refs[:dp], refs[dp:]
    depth, vocab_width = head.shape
    live = pieces[0].shape[0]
    row_count = dp * live
    mine = lax.axis_index("dp")
    start = (mine * stats.shape[1] + lax.axis_index("tensor")) * vocab_width

    normed = jnp.concatenate([piece[:, :depth] for piece in pieces], axis=0)
    logits = jnp.dot(normed, head[...], preferred_element_type=jnp.float32)
    digits = jnp.concatenate([piece[:, depth:] for piece in pieces], axis=0).astype(jnp.float32)
    lane = lax.broadcasted_iota(jnp.int32, (row_count, CODE), 1)
    weight = jnp.where(lane == 0, 1.0, jnp.where(lane == 1, float(DIGIT), jnp.where(lane == 2, float(DIGIT * DIGIT), 0.0)))
    target = jnp.sum(digits * weight, axis=-1, keepdims=True).astype(jnp.int32) - start
    column = lax.broadcasted_iota(jnp.int32, (row_count, vocab_width), 1)
    top = jnp.max(logits, axis=-1, keepdims=True)
    expo = jnp.exp(logits - top)
    total = jnp.sum(expo, axis=-1, keepdims=True)
    weighted = jnp.sum(expo * logits, axis=-1, keepdims=True)
    chosen = jnp.sum(jnp.where(column == target, logits, 0.0), axis=-1, keepdims=True)
    spot = lane - lax.broadcasted_iota(jnp.int32, (row_count, CODE), 0) % live
    tops = jnp.where((spot == 0) | (spot == GROUP), top, 0.0)
    sums = jnp.zeros((row_count, CODE), jnp.float32)
    for group, value in enumerate((total, weighted, chosen)):
        sums = jnp.where(spot == GROUP * group, value, sums)
    for d in range(dp):
        for line, table in enumerate((tops, sums)):
            packed = jnp.sum(table[d * live : (d + 1) * live], axis=0, keepdims=True)
            for t in range(stats.shape[1]):
                stats[mine ^ d, t, line : line + 1] = packed


def score(pieces, head, copies):
    dp = len(pieces)
    vmem = pl.BlockSpec(memory_space=pltpu.VMEM)
    return pl.pallas_call(
        score_kernel,
        out_shape=jax.ShapeDtypeStruct((dp, copies, 2, CODE), jnp.float32),
        in_specs=[vmem] * (dp + 1),
        out_specs=vmem,
        compiler_params=vmem_limit(32),
        name="score",
    )(*pieces, pltpu.with_memory_space_constraint(head, pltpu.VMEM))


def finish_kernel(stats, place, logprob, entropy, scored, spread, sems):
    tops = stats[:, 0:1, :]
    best = jnp.max(tops, axis=0)
    total = jnp.sum(stats[:, 1:2, :] * jnp.exp(tops - best), axis=0)
    weighted = pltpu.roll(total, CODE - GROUP, 1)
    chosen = pltpu.roll(total, CODE - 2 * GROUP, 1)
    lse = best + jnp.log(total)
    lane = lax.broadcasted_iota(jnp.int32, (LIVE, CODE), 1)
    row = lax.broadcasted_iota(jnp.int32, (LIVE, CODE), 0)

    def to_slots(values):
        column = jnp.sum(jnp.where(lane == row, values, 0.0), axis=1, keepdims=True)
        return jnp.sum(place[...] * column, axis=0, keepdims=True)

    scored[...] = to_slots(chosen - lse)
    first = pltpu.make_async_copy(scored, logprob, sems.at[0])
    first.start()
    spread[...] = to_slots(lse - weighted / total)
    second = pltpu.make_async_copy(spread, entropy, sems.at[1])
    second.start()
    first.wait()
    second.wait()


def finish(stats, place, slot_count):
    vmem = pl.BlockSpec(memory_space=pltpu.VMEM)
    out = jax.ShapeDtypeStruct((1, slot_count), jnp.float32)
    return pl.pallas_call(
        finish_kernel,
        out_shape=(out, out),
        in_specs=[vmem, vmem],
        out_specs=[pl.BlockSpec(memory_space=pltpu.HBM)] * 2,
        scratch_shapes=[
            pltpu.VMEM((1, slot_count), jnp.float32),
            pltpu.VMEM((1, slot_count), jnp.float32),
            pltpu.SemaphoreType.DMA((2,)),
        ],
        compiler_params=vmem_limit(32),
        name="finish",
    )(stats, place)


def swap(x, axis, distance):
    return lax.ppermute(x, axis, [(i, i ^ distance) for i in range(lax.axis_size(axis))])


def per_device(hidden, gain, head, lengths, offsets, targets, mask):
    dp, tensor = lax.axis_size("dp"), lax.axis_size("tensor")
    rows, codes, slots, gain = pick(hidden, gain, lengths, offsets, targets, mask)
    parts = {0: rows} | {s: swap(rows, "tensor", s) for s in reversed(range(1, tensor))}
    rows = join([parts[s] for s in range(tensor)], codes, gain)

    pieces = {d: swap(rows, "dp", d) for d in reversed(range(2, dp, 2))}
    held, pieces[0] = fetch(head, rows)
    for d in range(0, dp, 2):
        pieces[d + 1] = swap(pieces[d], "dp", 1)
    stats = score([pieces[d] for d in range(dp)], held, tensor)
    stats = lax.all_to_all(stats.reshape(dp * tensor, 2, CODE), ("dp", "tensor"), 0, 0, tiled=True)
    return finish(stats, slots, offsets.shape[1])


def solution(mesh):
    return jax.shard_map(
        per_device,
        mesh=mesh,
        in_specs=(
            P("dp", None, "tensor"),
            P(),
            P(None, ("dp", "tensor")),
            P("dp"),
            P("dp", None),
            P("dp", None),
            P("dp", None),
        ),
        out_specs=(P("dp", None), P("dp", None)),
        check_vma=False,
    )
```
